32 devices in a mesh: freq: 16 (over z, y, x), tp: 2 (over core).
Axes of the slice: x: 2, y: 2, z: 4, core: 2. Of those that a mesh axis runs over, the one named last changes fastest.
Arguments:
- tokens: bfloat16 [16384, 768], P('freq'), may hold values from -6 to 6
- lengths: int32 [16], P('freq'), may hold values from 1 to 1024, 8192 in all
- mixgain: float32 [768], replicated, may hold values from 0.5 to 1.5
- mixbias: float32 [768], replicated, may hold values from -1 to 1
- query_weight: bfloat16 [768, 768], P(None, 'tp'), may hold values from -0.21875 to 0.21875
- key_weight: bfloat16 [768, 768], P(None, 'tp'), may hold values from -0.21875 to 0.21875
- value_weight: bfloat16 [768, 768], P(None, 'tp'), may hold values from -0.21875 to 0.21875
- shift_taps: float32 [4, 768], P(None, 'tp'), may hold values from -3 to 3
- state_coef: float32 [768, 64], P('tp'), may hold values from -0.0625 to 0.0625
- state_rate: float32 [768, 64], P('tp'), may hold values from 0.0005 to 0.05
- state_skip: float32 [768], P('tp'), may hold values from -4 to 4
- out_weight: bfloat16 [768, 768], P('tp'), may hold values from -0.21875 to 0.21875
- feedgain: float32 [768], replicated, may hold values from 0.5 to 1.5
- feedbias: float32 [768], replicated, may hold values from -1 to 1
- up_weight: bfloat16 [768, 3072], P(None, 'tp'), may hold values from -0.21875 to 0.21875
- up_bias: float32 [3072], P('tp'), may hold values from -2.5 to 2.5
- down_weight: bfloat16 [3072, 768], P('tp'), may hold values from -0.109375 to 0.109375
- down_bias: float32 [768], replicated, may hold values from -1.5 to 1.5
- cotangent: bfloat16 [16384, 768], P('freq'), may hold values from -6 to 6
Outputs:
- layer_out: bfloat16 [16384, 768], P('freq')
- tokens_grad: float32 [16384, 768], P('freq')
- mixgain_grad: float32 [768], replicated
- mixbias_grad: float32 [768], replicated
- query_grad: float32 [768, 768], P('freq', 'tp')
- key_grad: float32 [768, 768], P('freq', 'tp')
- value_grad: float32 [768, 768], P('freq', 'tp')
- taps_grad: float32 [4, 768], P(None, 'tp')
- coef_grad: float32 [768, 64], P('tp')
- rate_grad: float32 [768, 64], P('tp')
- skip_grad: float32 [768], P('tp')
- outweight_grad: float32 [768, 768], P('tp', 'freq')
- feedgain_grad: float32 [768], replicated
- feedbias_grad: float32 [768], replicated
- upweight_grad: float32 [768, 3072], P('freq', 'tp')
- upbias_grad: float32 [3072], P('tp')
- downweight_grad: float32 [3072, 768], P('tp', 'freq')
- downbias_grad: float32 [768], replicated
The draws below stay inside these ranges and needn't reach their ends.
Inputs may be any that keep to these rules, and one draw needn't show every extreme that they name: Sequence s fills the first lengths[s] rows of its slot of 1024 rows; the rest of the slot is padding. The lengths sum to 8192, and one of them is 1024.
All inputs are finite; a program needn't handle non-finite values. No bound on the sum of `lengths` on one device may be relied on, other than what follows from the above.
Results may differ from the reference program's by a relative error of at most 0.0075.
Values sent between devices are 32-bit elements; how exact they have to be, the bound alone decides.
No kernel may reach another device: no remote copies, remote signals or barrier semaphores. Data moves between devices by JAX's collectives and lax.ppermute only.
A program may use at most 192 MiB of HBM per device.

```python
import math
import jax
import jax.numpy as jnp
import numpy as np
from jax import lax

D = 768
FF = 3072
NS = 64
SHIFT = 4
LEN = 1024
SEQS = 16
TOKENS = 16384


def spiked(drawn, stream_key, source, target, shards_of, factor):
    owner, partner = [(jnp.arange(drawn.shape[axis_at]) // (drawn.shape[axis_at] // shards_of)).reshape([-1 if axis == axis_at else 1 for axis in range(drawn.ndim)]) for axis_at in (source, target)]
    chosen = jax.random.permutation(stream_key, shards_of)[partner]
    strong = (owner == chosen) | (owner == (partner + shards_of // 2) % shards_of)
    return jnp.where(strong, factor * drawn, drawn)


def levels(own_key, dims, cuts, least, top_value):
    level = 1.0
    for dim, parts in cuts:
        draws = jax.random.uniform(jax.random.fold_in(jax.random.fold_in(own_key, 6), dim), (parts,), jnp.float32, least / len(cuts), top_value / len(cuts))
        level = level * jnp.repeat(jnp.exp(draws), dims[dim] // parts).reshape((-1,) + (1,) * (len(dims) - 1 - dim))
    return level


def length_profile(count, total, limit, slope):
    loads = [(1 << 20) // math.isqrt(grade ** slope) + 1 for grade in range(2, count + 1)]
    rest, counts = total - limit - (count - 1), [1] * (count - 1)
    while rest > 0:
        candidates = [i for i in range(count - 1) if counts[i] < limit]
        pool, budget = sum([loads[i] for i in candidates]), rest
        for i in candidates:
            extra = min(limit - counts[i], max(1, budget * loads[i] // pool), rest)
            counts[i] = counts[i] + extra
            rest = rest - extra
    return np.array([limit] + counts)


def uneven(own_key, amount, total, reach, skew):
    if amount == 2:
        one = jax.random.randint(own_key, (), max(1, total - reach), min(reach, total - 1) + 1)
        return jnp.stack([one, total - one])
    tallies = jnp.asarray(length_profile(amount, total, reach, skew), jnp.int32)
    pairs = (amount - 1) // 2
    giver, receiver = tallies[1:1 + 2 * pairs:2], tallies[2:2 + 2 * pairs:2]
    room = jnp.minimum(giver - 1, reach - receiver)
    passed = jax.random.randint(jax.random.fold_in(own_key, 1), (pairs,), 0, 1 << 20) % (room + 1)
    tallies = tallies.at[1:1 + 2 * pairs:2].set(giver - passed).at[2:2 + 2 * pairs:2].set(receiver + passed)
    return tallies[jax.random.permutation(jax.random.fold_in(own_key, 2), amount)]


def normal_values(stream_key, dims, deviation, limit, split=(), dtype=jnp.bfloat16):
    level = levels(stream_key, dims, split, -0.22, 0.18) if split else 1.0
    values = jax.random.normal(stream_key, dims, jnp.float32) * deviation * level
    return jnp.minimum(jnp.maximum(values, -limit), limit).astype(dtype)


def noise_with(rng, extent, width, most, pieces, heavy, held_as=jnp.bfloat16):
    array = width * jax.random.normal(rng, extent, jnp.float32)
    if pieces:
        array = array * levels(rng, extent, pieces, -0.22, 0.18)
    return jnp.clip(spiked(array, jax.random.fold_in(rng, 3), *heavy), -most, most).astype(held_as)


def setup_inputs(seed: int = 0) -> dict:
    key_list = jax.random.split(jax.random.key(seed), 20)
    return {
        "tokens": noise_with(key_list[0], (TOKENS, D), 1.0, 6.0, ((0, 16),), (0, 1, 16, 2.0)),
        "lengths": uneven(key_list[1], SEQS, SEQS * LEN // 2, LEN, 2).astype(jnp.int32),
        "mixgain": jnp.clip(1.0 + 0.1 * jax.random.normal(key_list[2], (D,), jnp.float32), 0.5, 1.5),
        "mixbias": normal_values(key_list[3], (D,), 0.2, 1.0, (), jnp.float32),
        "query_weight": normal_values(key_list[4], (D, D), D ** -0.5, 0.21875, ((1, 2),)),
        "key_weight": normal_values(key_list[5], (D, D), D ** -0.5, 0.21875, ((1, 2),)),
        "value_weight": normal_values(key_list[6], (D, D), D ** -0.5, 0.21875, ((1, 2),)),
        "shift_taps": normal_values(key_list[7], (SHIFT, D), 0.5, 3.0, ((1, 2),), jnp.float32),
        "state_coef": normal_values(key_list[8], (D, NS), (NS * 128) ** -0.5, 0.0625, ((0, 2),), jnp.float32),
        "state_rate": jnp.clip(jnp.exp(math.log(0.05) - 4.6051702 * jax.random.uniform(key_list[9], (D, NS), jnp.float32) ** levels(key_list[9], (D, NS), ((0, 2),), -0.2, 0.2)), 0.0005, 0.05),
        "state_skip": normal_values(key_list[10], (D,), 1.0, 4.0, ((0, 2),), jnp.float32),
        "out_weight": normal_values(key_list[11], (D, D), D ** -0.5, 0.21875, ((0, 2),)),
        "feedgain": jnp.clip(1.0 + 0.1 * jax.random.normal(key_list[12], (D,), jnp.float32), 0.5, 1.5),
        "feedbias": normal_values(key_list[13], (D,), 0.2, 1.0, (), jnp.float32),
        "up_weight": normal_values(key_list[14], (D, FF), D ** -0.5, 0.21875, ((1, 2),)),
        "up_bias": normal_values(key_list[15], (FF,), 0.5, 2.5, ((0, 2),), jnp.float32),
        "down_weight": normal_values(key_list[16], (FF, D), FF ** -0.5, 0.109375, ((0, 2),)),
        "down_bias": normal_values(key_list[17], (D,), 0.3, 1.5, (), jnp.float32),
        "cotangent": noise_with(key_list[18], (TOKENS, D), 1.0, 6.0, ((0, 16),), (0, 1, 16, 2.0)),
    }


@jax.custom_vjp
def low(v):
    return lax.optimization_barrier(v.astype(jnp.bfloat16)).astype(jnp.float32)

@jax.custom_vjp
def low_back(v):
    return v

def low_keep(v):
    return (low(v), None)

def low_pass(kept, grad):
    return (grad,)

def back_keep(v):
    return (v, None)

def back_low(kept, grad):
    return (low(grad),)
low.defvjp(low_keep, low_pass)
low_back.defvjp(back_keep, back_low)

def norm_rows(value, gain, bias):
    mean = lax.optimization_barrier(jnp.mean(value, -1, keepdims=True))
    centered = value - mean
    return centered * lax.rsqrt(lax.optimization_barrier(jnp.mean(centered * centered, -1, keepdims=True)) + 1e-05) * gain + bias

def spectrum_table(coef, rate, span):
    bins = jnp.arange(span + 1)
    theta = bins.astype(jnp.float32) * (math.pi / span)
    sign = (1 - 2 * (bins % 2)).astype(jnp.float32)[:, None, None]
    half = jnp.sin(0.5 * theta)[:, None, None]
    wave = jnp.sin(theta)[:, None, None]

    def block(pair):
        part_coef, part_rate = pair
        decay = jnp.exp(-part_rate)[None]
        tail = jnp.exp(-part_rate * span)[None]
        real_den = -jnp.expm1(-part_rate)[None] + decay * 2.0 * half * half
        imag_den = decay * wave
        scale = part_coef[None] * (1.0 - tail * sign) / (real_den * real_den + imag_den * imag_den)
        return (lax.optimization_barrier(jnp.sum(scale * real_den, -1)), -lax.optimization_barrier(jnp.sum(scale * imag_den, -1)))
    count = coef.shape[0] // 64
    real, imag = lax.map(jax.checkpoint(block), (coef.reshape(count, 64, -1), rate.reshape(count, 64, -1)))
    real = jnp.transpose(real, (1, 0, 2)).reshape(span + 1, coef.shape[0])
    imag = jnp.transpose(imag, (1, 0, 2)).reshape(span + 1, coef.shape[0])
    return (real, imag)

def reference(tokens, lengths, mixgain, mixbias, query_weight, key_weight, value_weight, shift_taps, state_coef, state_rate, state_skip, out_weight, feedgain, feedbias, up_weight, up_bias, down_weight, down_bias, cotangent):
    group = math.gcd(SEQS, max(1, 4096 // LEN))
    exact = lax.Precision.HIGHEST

    def forward(tokens32, mixgain, mixbias, query_weight, key_weight, value_weight, shift_taps, state_coef, state_rate, state_skip, out_weight, feedgain, feedbias, up_weight, up_bias, down_weight, down_bias):
        ker_real, ker_imag = spectrum_table(state_coef, state_rate, LEN)
        kernel = ker_real + 1j * ker_imag

        def one_group(pair):
            block_tokens, block_lengths = pair
            rows = group * LEN
            positions = jnp.arange(LEN)
            mask = (positions[None, :] < block_lengths[:, None]).astype(jnp.float32).reshape(rows, 1)
            normed = low(norm_rows(block_tokens, mixgain, mixbias))
            query = low_back(jnp.dot(normed, query_weight, precision=exact))
            key = low_back(jnp.dot(normed, key_weight, precision=exact))
            value = low_back(jnp.dot(normed, value_weight, precision=exact))
            key3 = key.reshape(group, LEN, -1)
            shifted = sum((shift_taps[lag] * jnp.pad(key3, ((0, 0), (lag, 0), (0, 0)))[:, :LEN] for lag in range(SHIFT)))
            signal = mask.reshape(group, LEN, 1) * shifted * value.reshape(group, LEN, -1)
            spec = jnp.fft.rfft(signal, n=2 * LEN, axis=1)
            conv = jnp.fft.irfft(spec * kernel[None], n=2 * LEN, axis=1)[:, :LEN]
            mixed = conv + state_skip * signal
            gated = low(mask * query * mixed.reshape(rows, -1))
            resid = block_tokens + low_back(jnp.dot(gated, out_weight, precision=exact))
            second = low(norm_rows(resid, feedgain, feedbias))
            hidden = low_back(jnp.dot(second, up_weight, precision=exact) + up_bias)
            activated = low(jax.nn.gelu(hidden, approximate=False))
            down_sum = low_back(jnp.dot(activated, down_weight, precision=exact) + down_bias)
            return mask * (resid + down_sum)
        result = lax.map(jax.checkpoint(one_group), (tokens32.reshape(SEQS // group, group * LEN, D), lengths.reshape(SEQS // group, group)))
        return result.reshape(TOKENS, D)
    floats = (tokens, mixgain, mixbias, query_weight, key_weight, value_weight, shift_taps, state_coef, state_rate, state_skip, out_weight, feedgain, feedbias, up_weight, up_bias, down_weight, down_bias)
    floats = tuple((item.astype(jnp.float32) for item in floats))
    primal, pull = jax.vjp(forward, *floats)
    grads = pull(cotangent.astype(jnp.float32))
    return (primal.astype(jnp.bfloat16), grads[0], grads[1], grads[2], grads[3], grads[4], grads[5], grads[6], grads[7], grads[8], grads[9], grads[10], grads[11], grads[12], grads[13], grads[14], grads[15], grads[16])
```

```python
import math

import jax
import jax.numpy as jnp
import numpy as np
from jax import lax
from jax.experimental import pallas as pl
from jax.experimental.pallas import tpu as pltpu
from jax.sharding import PartitionSpec as P

f32 = jnp.float32
bf16 = jnp.bfloat16


def layer_norm(value, gain, bias):
    mean = jnp.mean(value, -1, keepdims=True)
    centered = value - mean
    inverse = lax.rsqrt(jnp.mean(centered * centered, -1, keepdims=True) + 1e-05)
    scaled = centered * inverse
    return (scaled * gain + bias, scaled, inverse)


def norm_back(grad_out, scaled, inverse, gain):
    weighted = grad_out * gain
    return inverse * (
        weighted
        - jnp.mean(weighted, -1, keepdims=True)
        - scaled * jnp.mean(weighted * scaled, -1, keepdims=True)
    )


def inner(left, right):
    return lax.dot_general(left, right, (((0,), (0,)), ((), ())), preferred_element_type=f32)


def times_transposed(grad, weight):
    return lax.dot_general(grad, weight, (((1,), (1,)), ((), ())), preferred_element_type=f32)


def matmul(left, right):
    return jnp.dot(left, right, preferred_element_type=f32)


def dft_table(span):
    bins = np.arange(span)[:, None].astype(np.int64)
    times = np.arange(span)[None, :].astype(np.int64)
    angle = (bins * times % (2 * span)) * (math.pi / span)
    table = np.concatenate([np.cos(angle), np.sin(angle)], 0)
    table[span] = 1 - 2 * (np.arange(span) % 2)
    return table


def packed_product(left, right, first, sign):
    half = left.shape[0] // 2
    a, b, c, d = left[:half], left[half:], right[:half], right[half:]
    bd = b * d
    real = a * c - sign * jnp.where(first, 0.0, bd)
    imag = jnp.where(first, bd, b * c + sign * (a * d))
    return jnp.concatenate([real, imag], 0)


def swap(value, axis, bit):
    size = lax.axis_size(axis)
    return lax.ppermute(value, axis, [(i, i ^ (1 << bit)) for i in range(size)])


def pair_sum(value):
    if lax.axis_size("tp") == 1:
        return value
    return value + swap(value, "tp", 0)


def scatter_sum(value, order, after=()):
    places = lax.axis_size("freq")
    count = places.bit_length() - 1
    place = lax.axis_index("freq")
    value = value.reshape((2,) * count + (value.shape[0] // places, value.shape[1]))
    dims = list(range(count - 1, -1, -1))
    for step, bit in enumerate(order):
        dim = dims.index(bit)
        mine = (place >> bit) & 1
        give = lax.dynamic_index_in_dim(value, 1 - mine, dim, keepdims=False)
        keep = lax.dynamic_index_in_dim(value, mine, dim, keepdims=False)
        got = swap(give, "freq", bit)
        if step < len(after):
            got, _ = lax.optimization_barrier((got, after[step]))
        value = keep + got
        dims.pop(dim)
    return value


def lane_parts(chans):
    return 128 if chans % 128 == 0 else chans


def state_kernel(coef_t, rate_t, span):
    states, chans = coef_t.shape
    step = 32
    blocks = span // step
    lanes = lane_parts(chans)
    group = 8

    def run(coef_ref, rate_ref, out_ref, fine, coarse):
        rate = rate_ref[...][:, None, :]
        within = lax.broadcasted_iota(jnp.int32, (1, step, 1), 1).astype(f32)
        across = lax.broadcasted_iota(jnp.int32, (1, blocks, 1), 1).astype(f32)
        fine[...] = jnp.exp(-rate * within)
        coarse[...] = coef_ref[...][:, None, :] * jnp.exp(-rate * (step * across))
        for base in range(0, blocks, group):

            def add(n, sums):
                near = fine[n]
                return tuple(
                    sums[j] + coarse[n, pl.ds(base + j, 1), :] * near for j in range(group)
                )

            zero = jnp.zeros((step, lanes), f32)
            sums = lax.fori_loop(0, states, add, (zero,) * group, unroll=8)
            for j in range(group):
                out_ref[pl.ds((base + j) * step, step), :] = sums[j].astype(bf16)

    return pl.pallas_call(
        run,
        grid=(chans // lanes,),
        in_specs=[pl.BlockSpec((states, lanes), lambda i: (0, i))] * 2,
        out_specs=pl.BlockSpec((span, lanes), lambda i: (0, i)),
        out_shape=jax.ShapeDtypeStruct((span, chans), bf16),
        scratch_shapes=[
            pltpu.VMEM((states, step, lanes), f32),
            pltpu.VMEM((states, blocks, lanes), f32),
        ],
        compiler_params=pltpu.CompilerParams(vmem_limit_bytes=32 << 20),
        cost_estimate=pl.CostEstimate(
            flops=2 * span * chans * states, bytes_accessed=2 * span * chans, transcendentals=0
        ),
        name="state_kernel",
    )(coef_t, rate_t)


def state_grads(coef_t, rate_t, lag_grad):
    states, chans = coef_t.shape
    span = lag_grad.shape[0]
    step = 32
    blocks = span // step
    lanes = lane_parts(chans)
    group = 8
    tiles = step // 8

    def run(coef_ref, rate_ref, lag_ref, coef_out, rate_out, fine, coarse, plain, place, ramp):
        rate = rate_ref[...][:, None, :]
        within = lax.broadcasted_iota(jnp.int32, (1, step, 1), 1).astype(f32)
        across = lax.broadcasted_iota(jnp.int32, (1, blocks, 1), 1).astype(f32)
        fine[...] = jnp.exp(-rate * within)
        coarse[...] = jnp.exp(-rate * (step * across))
        plain[...] = jnp.zeros_like(plain)
        place[...] = jnp.zeros_like(place)
        ramp[...] = jnp.zeros_like(ramp)
        for base in range(0, blocks, group):
            lag = [
                [
                    lag_ref[pl.ds((base + j) * step + 8 * a, 8), :]
                    for a in range(tiles)
                ]
                for j in range(group)
            ]

            def add(n, _):
                near = [fine[n, pl.ds(8 * a, 8), :] for a in range(tiles)]
                suffix = None
                later = None
                tilted = None
                for j in reversed(range(group)):
                    far = coarse[n, pl.ds(base + j, 1), :]
                    total = None
                    slope = None
                    for a in reversed(range(tiles)):
                        term = lag[j][a] * near[a]
                        if total is None:
                            total = term
                        else:
                            slope = total if slope is None else slope + total
                            total = total + term
                    weighted = far * total
                    bent = far * slope
                    tilted = bent if tilted is None else tilted + bent
                    if suffix is None:
                        suffix = weighted
                    else:
                        later = suffix if later is None else later + suffix
                        suffix = suffix + weighted
                plain[n] = plain[n] + suffix
                place[n] = place[n] + (later + float(base) * suffix)
                ramp[n] = ramp[n] + tilted
                return 0

            lax.fori_loop(0, states, add, 0, unroll=4)
        rows = lax.broadcasted_iota(jnp.int32, (1, 8, 1), 1).astype(f32)
        whole = plain[...]
        coef_out[...] = jnp.sum(whole, 1)
        times = float(step) * place[...] + 8.0 * ramp[...] + rows * whole
        rate_out[...] = -coef_ref[...] * jnp.sum(times, 1)

    shape = jax.ShapeDtypeStruct((states, chans), f32)
    block = pl.BlockSpec((states, lanes), lambda i: (0, i))
    return pl.pallas_call(
        run,
        grid=(chans // lanes,),
        in_specs=[block, block, pl.BlockSpec((span, lanes), lambda i: (0, i))],
        out_specs=[block, block],
        out_shape=[shape, shape],
        scratch_shapes=[
            pltpu.VMEM((states, step, lanes), f32),
            pltpu.VMEM((states, blocks, lanes), f32),
        ]
        + [pltpu.VMEM((states, 8, lanes), f32)] * 3,
        compiler_params=pltpu.CompilerParams(vmem_limit_bytes=32 << 20),
        cost_estimate=pl.CostEstimate(
            flops=4 * span * chans * states, bytes_accessed=4 * span * chans, transcendentals=0
        ),
        name="state_grads",
    )(coef_t, rate_t, lag_grad)


def body(
    tokens,
    lengths,
    mixgain,
    mixbias,
    query_weight,
    key_weight,
    value_weight,
    shift_taps,
    state_coef,
    state_rate,
    state_skip,
    out_weight,
    feedgain,
    feedbias,
    up_weight,
    up_bias,
    down_weight,
    down_bias,
    cotangent,
):
    seqs = lengths.shape[0]
    rows = tokens.shape[0]
    span = rows // seqs
    assert seqs == 1
    chans = query_weight.shape[1]
    lags = shift_taps.shape[0]
    places = lax.axis_size("freq")
    count = places.bit_length() - 1
    assert places == 1 << count
    bits = list(range(count))
    orders = [bits, [1, 0] + bits[2:], [2, 0, 1] + bits[3:]]
    positions = jnp.arange(span)
    mask = (positions < lengths[0]).astype(f32)[:, None]
    table_np = dft_table(span)
    table = jnp.asarray(table_np.astype(jnp.bfloat16))
    fold = jnp.full((2 * span, 1), 1.0 / span, f32).at[0].set(0.5 / span).at[span].set(0.5 / span)
    first = (jnp.arange(span) == 0)[:, None]

    def to_bins(series):
        return matmul(table, series.astype(bf16))

    def from_bins(bins):
        return inner(table, (bins * fold).astype(bf16))

    coef_t, rate_t = state_coef.T, state_rate.T
    ker_bins = to_bins(state_kernel(coef_t, rate_t, span))

    first_full, first_hat, first_inv = layer_norm(tokens.astype(f32), mixgain, mixbias)
    normed = first_full.astype(bf16)
    query = matmul(normed, query_weight)
    key = matmul(normed, key_weight)
    value = matmul(normed, value_weight)
    lagged = [jnp.pad(key, ((lag, 0), (0, 0)))[:span] for lag in range(lags)]
    shifted = sum((shift_taps[lag] * lagged[lag] for lag in range(lags)))
    signal = mask * shifted * value
    sig_bins = to_bins(signal)
    conv = from_bins(packed_product(sig_bins, ker_bins, first, 1.0))
    mixed = conv + state_skip * signal
    gated = (mask * query * mixed).astype(bf16)
    mixout = pair_sum(matmul(gated, out_weight))
    resid = tokens.astype(f32) + mixout
    second_full, second_hat, second_inv = layer_norm(resid, feedgain, feedbias)
    second = second_full.astype(bf16)
    hidden = matmul(second, up_weight) + up_bias
    cdf = 0.5 * (1.0 + lax.erf(hidden * (1.0 / math.sqrt(2.0))))
    slope = cdf + hidden * jnp.exp(-0.5 * hidden * hidden) * (1.0 / math.sqrt(2.0 * math.pi))
    activated = (hidden * cdf).astype(bf16)
    grad_out = mask * cotangent.astype(f32)
    grad_down = grad_out.astype(bf16)
    down_grad = inner(grad_down, activated)
    third = down_grad.shape[1] // 3
    downbias_part = jnp.sum(grad_down.astype(f32), 0)
    grad_hidden = (times_transposed(grad_down, down_weight) * slope).astype(bf16)
    up_grad = inner(second, grad_hidden)
    upbias_part = jnp.sum(grad_hidden.astype(f32), 0)
    second_part = times_transposed(grad_hidden, up_weight)
    feedgain_part = jnp.sum(second_part * second_hat, 0)
    feedbias_part = jnp.sum(second_part, 0)
    grad_second = pair_sum(second_part)
    grad_resid = grad_out + norm_back(grad_second, second_hat, second_inv, feedgain)
    grad_mix = grad_resid.astype(bf16)
    out_grad = inner(grad_mix, gated)
    grad_gated = times_transposed(grad_mix, out_weight)
    grad_query = (mask * grad_gated * mixed).astype(bf16)
    query_grad = inner(normed, grad_query)
    grad_mixed = mask * grad_gated * query
    skip_part = jnp.sum(grad_mixed * signal, 0)
    grad_bins = to_bins(grad_mixed)
    grad_signal = state_skip * grad_mixed + from_bins(
        packed_product(grad_bins, ker_bins, first, -1.0)
    )
    lag_grad = from_bins(packed_product(grad_bins, sig_bins, first, -1.0))
    grad_shifted = grad_signal * mask * value
    grad_value = (grad_signal * mask * shifted).astype(bf16)
    grad_key = sum(
        (
            shift_taps[lag] * jnp.pad(grad_shifted, ((0, lag), (0, 0)))[lag:]
            for lag in range(lags)
        )
    ).astype(bf16)
    key_grad = inner(normed, grad_key)
    value_grad = inner(normed, grad_value)
    taps_part = jnp.stack([jnp.sum(grad_shifted * lagged[lag], 0) for lag in range(lags)])
    normed_part = (
        times_transposed(grad_query, query_weight)
        + times_transposed(grad_key, key_weight)
        + times_transposed(grad_value, value_weight)
    )
    mixgain_part = jnp.sum(normed_part * first_hat, 0)
    mixbias_part = jnp.sum(normed_part, 0)
    grad_normed = pair_sum(normed_part)
    tokens_grad = grad_resid + norm_back(grad_normed, first_hat, first_inv, mixgain)

    coef_part, rate_part = state_grads(coef_t, rate_t, lag_grad)

    down_sums = [
        scatter_sum(down_grad[:, i * third : (i + 1) * third], orders[i], (grad_gated, lag_grad, grad_key, normed_part)) for i in range(3)
    ]
    up_sums = [scatter_sum(up_grad[:, i * third : (i + 1) * third], orders[i], (lag_grad, grad_key, normed_part)) for i in range(3)]
    out_sum = scatter_sum(out_grad, orders[0], (grad_key,))
    query_sum = scatter_sum(query_grad, orders[1], (normed_part,))
    key_sum = scatter_sum(key_grad, orders[2])
    part = chans // 3
    value_sums = [
        scatter_sum(value_grad[:, i * part : (i + 1) * part], orders[i]) for i in range(3)
    ]

    both = jnp.stack([mixgain_part, mixbias_part, feedgain_part, feedbias_part])
    both = pair_sum(both)
    small = jnp.concatenate(
        [
            jnp.concatenate([coef_part, rate_part], 0).reshape(-1),
            taps_part.reshape(-1),
            skip_part,
            upbias_part,
            downbias_part,
            both.reshape(-1),
        ]
    ).reshape(-1, 128)
    for bit in bits:
        small = small + swap(small, "freq", bit)
    small = small.reshape(-1)
    cuts = np.cumsum(
        [
            coef_part.size,
            rate_part.size,
            taps_part.size,
            chans,
            upbias_part.size,
            downbias_part.size,
        ]
    )
    coef_sum, rate_sum, taps_sum, skip_sum, upbias_sum, downbias_sum, norms = jnp.split(small, cuts)
    norms = norms.reshape(4, -1)

    down_sum = pair_sum(matmul(activated, down_weight)) + down_bias
    layer_out = (mask * (resid + down_sum)).astype(bf16)
    return (
        layer_out,
        tokens_grad,
        norms[0],
        norms[1],
        query_sum,
        key_sum,
        jnp.concatenate(value_sums, 1),
        taps_sum.reshape(lags, chans),
        coef_sum.reshape(-1, chans).T,
        rate_sum.reshape(-1, chans).T,
        skip_sum,
        out_sum.T,
        norms[2],
        norms[3],
        jnp.concatenate(up_sums, 1),
        upbias_sum,
        jnp.concatenate(down_sums, 1).T,
        downbias_sum,
    )


def solution(mesh):
    in_specs = (
        P("freq", None),
        P("freq"),
        P(),
        P(),
        P(None, "tp"),
        P(None, "tp"),
        P(None, "tp"),
        P(None, "tp"),
        P("tp", None),
        P("tp", None),
        P("tp"),
        P("tp", None),
        P(),
        P(),
        P(None, "tp"),
        P("tp"),
        P("tp", None),
        P(),
        P("freq", None),
    )
    out_specs = (
        P("freq", None),
        P("freq", None),
        P(),
        P(),
        P("freq", "tp"),
        P("freq", "tp"),
        P("freq", "tp"),
        P(None, "tp"),
        P("tp", None),
        P("tp", None),
        P("tp"),
        P("tp", "freq"),
        P(),
        P(),
        P("freq", "tp"),
        P("tp"),
        P("tp", "freq"),
        P(),
    )
    return jax.shard_map(body, mesh=mesh, in_specs=in_specs, out_specs=out_specs, check_vma=False)
```

```python
import math

import jax
import jax.numpy as jnp
import numpy as np
from jax import lax
from jax.experimental import pallas as pl
from jax.experimental.pallas import tpu as pltpu
from jax.sharding import PartitionSpec as P

f32 = jnp.float32
bf16 = jnp.bfloat16
in_vmem = pl.BlockSpec(memory_space=pltpu.VMEM)
in_smem = pl.BlockSpec(memory_space=pltpu.SMEM)
anywhere = pl.BlockSpec(memory_space=pl.ANY)
pad = 8
small_cost = pl.CostEstimate(flops=1, bytes_accessed=1, transcendentals=0)


def shaped(shape, dtype):
    return jax.ShapeDtypeStruct(shape, dtype)


def size_of(item):
    return math.prod(item.shape) * jnp.dtype(item.dtype).itemsize


def call(run, ins, outs, name, scratch=(), flops=0, moved=0, specs=None):
    held = sum(size_of(item) for item in (*ins, *outs, *scratch))
    return pl.pallas_call(
        run,
        in_specs=specs or [in_vmem] * len(ins),
        out_specs=[in_vmem] * len(outs),
        out_shape=outs,
        scratch_shapes=list(scratch),
        compiler_params=pltpu.CompilerParams(vmem_limit_bytes=held + (6 << 20)),
        cost_estimate=small_cost,
        name=name,
    )(*ins)


def matmul(left, right):
    return jnp.dot(left, right, preferred_element_type=f32)


def times_transposed(left, right):
    return lax.dot_general(left, right, (((1,), (1,)), ((), ())), preferred_element_type=f32)


def swap(value, axis, bit):
    size = lax.axis_size(axis)
    return lax.ppermute(value, axis, [(i, i ^ (1 << bit)) for i in range(size)])


def dft_table(block):
    bins = np.arange(block)[:, None].astype(np.int64)
    times = np.arange(block)[None, :].astype(np.int64)
    angle = (bins * times % (2 * block)) * (math.pi / block)
    table = np.concatenate([np.cos(angle), np.sin(angle)], 0)
    table[block] = 1 - 2 * (np.arange(block) % 2)
    return table.astype(jnp.bfloat16)


def iota(shape, dim):
    return lax.broadcasted_iota(jnp.int32, shape, dim)


def row_mask(first, count, length):
    return (iota((count, 1), 0) + first < length).astype(f32)


def insert_bit(index, pos, bit):
    low = index & ((1 << pos) - 1)
    return ((index >> pos) << (pos + 1)) | (bit << pos) | low


def norm_rows(value):
    mean = jnp.mean(value, -1, keepdims=True)
    centered = value - mean
    inverse = lax.rsqrt(jnp.mean(centered * centered, -1, keepdims=True) + 1e-05)
    return centered * inverse, inverse


def norm_back(grad_out, scaled, inverse, gain):
    weighted = grad_out * gain
    return inverse * (
        weighted
        - jnp.mean(weighted, -1, keepdims=True)
        - scaled * jnp.mean(weighted * scaled, -1, keepdims=True)
    )


def column_sum(value):
    rows, width = value.shape
    return jnp.sum(value.reshape(rows // 8, 8, width), 0)


def shift_conv(taps, keypad, start, count):
    lags = taps.shape[0]
    return sum(
        taps[lag : lag + 1, :] * keypad[pl.ds(start + pad - lag, count), :] for lag in range(lags)
    )


def edge(first, real, imag):
    return jnp.where(first, imag, real), jnp.where(first, 0.0, imag)


class Coming:
    def __init__(self, source, held, sems, cuts=1):
        self.held, self.started, self.here = held, False, 0
        if source.shape[-2:] != held.shape[-2:] and len(source.shape) > 1:
            last = pl.ds(source.shape[0] - held.shape[0], held.shape[0])
            self.copies = [pltpu.make_async_copy(source.at[last], held, sems.at[0])]
            return
        if len(source.shape) == 1:
            self.copies = [pltpu.make_async_copy(source, held.at[0], sems.at[0])]
            return
        rows = held.shape[0] // cuts
        self.copies = []
        for i in range(cuts):
            part = pl.ds(i * rows, rows) if cuts > 1 else pl.ds(0, held.shape[0])
            self.copies.append(pltpu.make_async_copy(source.at[part], held.at[part], sems.at[i]))

    def start(self, cuts=None):
        if not self.started:
            for copy in self.copies:
                copy.start()
            self.started = True

    def get(self, cut=None):
        self.start()
        until = len(self.copies) if cut is None else cut + 1
        while self.here < until:
            self.copies[self.here].wait()
            self.here += 1
        return self.held


class Going:
    def __init__(self, target, held, sems):
        self.target, self.ref, self.sems, self.copies = target, held, sems, []

    def put(self, start=0, count=None, source=None):
        rows = pl.ds(start, self.ref.shape[0] if count is None else count)
        sem = self.sems.at[len(self.copies)]
        if len(self.target.shape) == 1:
            copy = pltpu.make_async_copy(self.ref.at[0], self.target, sem)
        else:
            source = self.ref.at[rows] if source is None else source
            copy = pltpu.make_async_copy(source, self.target.at[rows], sem)
        copy.start()
        self.copies.append(copy)


most_puts = 16
most_cuts = 4
in_hbm = pl.BlockSpec(memory_space=pl.ANY)


def staged(run, ins, outs, name, scratch=(), aliases=None):
    spec = {"s": in_smem}
    plain = ("s", "a")
    shared = lambda kind: isinstance(kind, str) and kind[0] == "="
    tail = lambda x, kind: shaped((32, x.shape[1]), x.dtype) if kind == "t" else x
    held = [tail(x, kind) for x, kind in (*ins, *outs) if kind not in plain and not shared(kind)]
    held = [shaped(x.shape if len(x.shape) > 1 else (1, *x.shape), x.dtype) for x in held]
    n_in = sum(kind not in plain for _, kind in ins)
    n_out = sum(kind not in plain for _, kind in outs)

    def whole(*refs):
        refs = list(refs)
        given, made = refs[: len(ins)], refs[len(ins) : len(ins) + len(outs)]
        rest = refs[len(ins) + len(outs) :]
        own, bufs = rest[: len(scratch)], rest[len(scratch) :]
        in_sems, out_sems = bufs[-2:]
        bufs = list(bufs[:-2])
        views, at = [], 0
        for ref, (_, kind) in zip(given, ins):
            if kind not in plain:
                cuts = kind if isinstance(kind, int) else 1
                views.append(Coming(ref, bufs.pop(0), in_sems.at[at], cuts))
                at += 1
                if kind != "l":
                    views[-1].start()
            else:
                views.append(ref)
        going, at = [], 0
        for ref, (_, kind) in zip(made, outs):
            if kind not in plain:
                held_at = views[int(kind[1:])].held if shared(kind) else bufs.pop(0)
                going.append(Going(ref, held_at, out_sems.at[at]))
                at += 1
            else:
                going.append(ref)
        for view, (_, kind) in zip(views, ins):
            if kind in ("v", "t"):
                view.get()
        views = [view.held if kind in ("v", "t") else view for view, (_, kind) in zip(views, ins)]
        small = [item for item, (_, kind) in zip(going, outs) if kind == "v"]
        run(*views, *[item.ref if item in small else item for item in going], *own)
        for item in small:
            item.put()
        for view in views:
            if isinstance(view, Coming):
                view.get()
        for item in going:
            if isinstance(item, Going):
                for copy in item.copies:
                    copy.wait()

    return pl.pallas_call(
        whole,
        in_specs=[spec.get(kind, in_hbm) for _, kind in ins],
        out_specs=[spec.get(kind, in_hbm) for _, kind in outs],
        out_shape=[item for item, _ in outs],
        scratch_shapes=list(scratch)
        + [pltpu.VMEM(x.shape, x.dtype) for x in held]
        + [
            pltpu.SemaphoreType.DMA((max(n_in, 1), most_cuts)),
            pltpu.SemaphoreType.DMA((max(n_out, 1), most_puts)),
        ],
        input_output_aliases=aliases or {},
        compiler_params=pltpu.CompilerParams(vmem_limit_bytes=60 << 20),
        cost_estimate=small_cost,
        name=name,
    )(*[x for x, _ in ins])


def split_products(place_ref, bit, source, chosen, pairs, give, keep):
    groups, rows, _ = source.shape
    mine = (place_ref[0] >> bit) & 1
    for k, (out, side) in enumerate(((give, 1 - mine), (keep, mine))):
        for j in range(groups // 2):
            chosen[k, pl.ds(j * rows, rows), :] = source[insert_bit(j, bit, side)]
    for k, out in enumerate((give, keep)):
        for right, start, count, to in pairs:
            out[:, pl.ds(to, count)] = matmul(chosen[k], right[:, pl.ds(start, count)])


def mixer_forward(length, tokens, gain, bias, weights, taps, coef_t, rate_t, skip, out_weight, table, table_t):
    span, width = tokens.shape
    chans = out_weight.shape[0]
    states = coef_t.shape[0]
    block = table.shape[1]
    count = span // block
    step = 32
    far_steps = span // step
    group = 8
    lanes = 128

    def run(
        len_ref, tok, gain_ref, bias_ref, wq, wk, wv, taps_ref, coef_ref, rate_ref, skip_ref, wo, tab, tab_t,
        normed_o, query_o, keypad_o, value_o, mixed_o, gated_o, sig_o, ker_o, part_o,
        fine, coarse, signal, sig_bins, ker_bins, prod,
    ):
        size = len_ref[0]
        normed, query, keypad, value = normed_o.ref, query_o.ref, keypad_o.ref, value_o.ref
        sig16, ker16 = sig_o.ref, ker_o.ref

        within = iota((1, step, 1), 1).astype(f32)
        across = iota((1, group, 1), 1).astype(f32) * float(step)
        rate = rate_ref[...][:, None, :]
        fine[...] = jnp.exp(-rate * within)
        for k in range(far_steps // group):
            coarse[:, k] = coef_ref[...][:, None, :] * jnp.exp(-rate * (across + float(step * group * k)))
        keypad[pl.ds(0, pad), :] = jnp.zeros((pad, chans), f32)
        tok_ref, wq_ref, wk_ref, wv_ref = tok.get(), wq.get(), wk.get(), wv.get()
        for item in (wo, tab, tab_t):
            item.start()

        def first_part(i, _):
            start = pl.multiple_of(i * block, block)
            rows = pl.ds(start, block)
            scaled, _ = norm_rows(tok_ref[rows, :].astype(f32))
            norm = (scaled * gain_ref[...] + bias_ref[...]).astype(bf16)
            normed[rows, :] = norm
            key_rows = pl.ds(pl.multiple_of(start + pad, 8), block)
            products = [(query, rows, wq_ref), (keypad, key_rows, wk_ref), (value, rows, wv_ref)]
            for lane in range(0, chans, lanes):
                if products:
                    out, place, weight = products.pop(0)
                    out[place, :] = matmul(norm, weight[...])
                cols = pl.ds(lane, lanes)
                sums = [None] * group
                for n in range(states):
                    near = fine[n, :, cols]
                    for j in range(group):
                        term = coarse[n, i, pl.ds(j, 1), cols] * near
                        sums[j] = term if n == 0 else sums[j] + term
                for j in range(group):
                    place = pl.ds(pl.multiple_of(start + j * step, step), step)
                    ker16[place, cols] = sums[j].astype(bf16)
            return 0

        lax.fori_loop(0, count, first_part, 0)
        normed_o.put()
        for i in range(count):
            rows = pl.ds(i * block, block)
            shifted = shift_conv(taps_ref, keypad, i * block, block)
            sig = row_mask(i * block, block, size) * shifted * value[rows, :]
            signal[rows, :] = sig
            sig16[rows, :] = sig.astype(bf16)
        sig_o.put()
        ker_o.put()
        query_o.put()
        keypad_o.put()
        value_o.put()

        sign = 1.0 - 2.0 * (iota((2 * block, 1), 0) % 2).astype(f32)
        before = None
        for i in range(count):
            bins = pl.ds(i * 2 * block, 2 * block)
            rows = pl.ds(i * block, block)
            sig_bins[bins, :] = matmul(tab.get()[...], sig16[rows, :])
            ker = matmul(tab.get()[...], ker16[rows, :])
            ker_bins[bins, :] = ker if before is None else ker + sign * before
            before = ker

        def product(i, _):
            start = pl.multiple_of(i * 16, 16)
            first = (iota((16, 1), 0) + start) == 0
            scale = jnp.where(first, 0.5 / block, 1.0 / block)
            for lane in range(0, chans, lanes):
                cols = pl.ds(lane, lanes)

                def pair(ref, j):
                    return (
                        ref[pl.ds(j * 2 * block + start, 16), cols],
                        ref[pl.ds(j * 2 * block + block + start, 16), cols],
                    )

                sigs = [pair(sig_bins, j) for j in range(count)]
                kers = []
                for j in range(count):
                    c, d = pair(ker_bins, j)
                    other, d = edge(first, c, d)
                    kers.append((c, other, d))
                for j in range(count):
                    real = imag = None
                    for m in range(j + 1):
                        a, b = sigs[m]
                        c, other, d = kers[j - m]
                        r = a * c - b * d
                        s = a * d + b * other
                        real = r if real is None else real + r
                        imag = s if imag is None else imag + s
                    prod[pl.ds(j * 2 * block + start, 16), cols] = (real * scale).astype(bf16)
                    prod[pl.ds(j * 2 * block + block + start, 16), cols] = (imag * scale).astype(bf16)
            return 0

        lax.fori_loop(0, block // 16, product, 0)
        for i in range(count):
            rows = pl.ds(i * block, block)
            conv = matmul(tab_t.get()[...], prod[pl.ds(i * 2 * block, 2 * block), :])
            mixed = conv + skip_ref[...] * signal[rows, :]
            mixed_o.ref[rows, :] = mixed
            gated = (row_mask(i * block, block, size) * query[rows, :] * mixed).astype(bf16)
            gated_o.ref[rows, :] = gated
            part_o.ref[rows, :] = matmul(gated, wo.get()[...])
            part_o.put(i * block, block)
        mixed_o.put()
        gated_o.put()

    outs = [
        (shaped((span, width), bf16), "h"),
        (shaped((span, chans), f32), "h"),
        (shaped((span + pad, chans), f32), "h"),
        (shaped((span, chans), f32), "h"),
        (shaped((span, chans), f32), "h"),
        (shaped((span, chans), bf16), "h"),
        (shaped((span, chans), bf16), "h"),
        (shaped((span, chans), bf16), "h"),
        (shaped((span, width), f32), "h"),
    ]
    scratch = [
        pltpu.VMEM((states, step, chans), f32),
        pltpu.VMEM((states, far_steps // group, group, chans), f32),
        pltpu.VMEM((span, chans), f32),
        pltpu.VMEM((2 * span, chans), f32),
        pltpu.VMEM((2 * span, chans), f32),
        pltpu.VMEM((2 * span, chans), bf16),
    ]
    ins = [(length, "s"), (tokens, "h"), (gain, "v"), (bias, "v")]
    ins += [(weight, "h") for weight in weights]
    ins += [(taps, "v"), (coef_t, "v"), (rate_t, "v"), (skip, "v")]
    ins += [(out_weight, "l"), (table, "l"), (table_t, "l")]
    return staged(run, ins, outs, "mixer_forward", scratch)


def norm_sums(grad, value, start, gain_sum, bias_sum):
    rows = pl.ds(start, 128)
    scaled, _ = norm_rows(value[rows, :].astype(f32))
    part = grad[rows, :]
    return gain_sum + column_sum(part * scaled), bias_sum + column_sum(part)


def feed_prepare(length, cotangent, normed):
    span, width = cotangent.shape

    def run(len_ref, cot, normed_ref, down_o, down_t, normed_t, sums):
        size = len_ref[0]
        total = jnp.zeros((8, width), f32)
        for start in range(0, span, 256):
            rows = pl.ds(start, 256)
            grad = row_mask(start, 256, size) * cot.get()[rows, :].astype(f32)
            total = total + column_sum(grad)
            down_o.ref[rows, :] = grad.astype(bf16)
            down_o.put(start, 256)
            down_t.ref[:, rows] = grad.astype(bf16).T
        down_t.put()
        for start in range(0, span, 256):
            rows = pl.ds(start, 256)
            normed_t.ref[:, rows] = normed_ref.get()[rows, :].T
        normed_t.put()
        sums[...] = total

    outs = [
        (shaped((span, width), bf16), "h"),
        (shaped((width, span), bf16), "h"),
        (shaped((width, span), bf16), "h"),
        (shaped((8, width), f32), "v"),
    ]
    return staged(run, [(length, "s"), (cotangent, "h"), (normed, "h")], outs, "feed_prepare")


def feed_forward_back(place, tokens, mine, other, gain, bias, down, down_t, up_weight, up_bias, down_weight, cuts):
    span, width = tokens.shape
    hidden = up_weight.shape[1]
    groups, rows_each, _ = down_t.shape
    half = width // 2
    bits, widths, thirds = cuts
    size = hidden // 3
    parts = len(bits)
    step = 256

    def run(*refs):
        place_ref, tok, mine_ref, other_ref, gain_ref, bias_ref, dn, dn_t, up, upb, dw = refs[:11]
        resid_o, acts_o, part_o, sums, upb_sums = refs[11:16]
        gives, keeps = refs[16 : 16 + parts], refs[16 + parts : 16 + 2 * parts]
        second, second_t, grad_hid, hid_a, hid_b, pre_a, pre_b, chosen_a, chosen_b = refs[16 + 2 * parts :]
        resid, acts = resid_o.ref, acts_o.ref
        later = (up, dw, dn, dn_t)
        cuts = span // step
        for k in range(cuts):
            rows = pl.ds(k * step, step)
            value = tok.get(k)[rows, :].astype(f32) + (mine_ref.get(k)[rows, :] + other_ref.get(k)[rows, :])
            if k == 0:
                for item in later:
                    item.start()
            resid[rows, :] = value
            resid_o.put(k * step, step)
            scaled, _ = norm_rows(value)
            norm = (scaled * gain_ref[...] + bias_ref[...]).astype(bf16)
            second[rows, :] = norm
            turned = norm.T
            for j in range(groups):
                second_t[j, :, rows] = turned[j * rows_each : (j + 1) * rows_each, :]
        up_ref, dw_ref, dn_ref = up.get(), dw.get(), dn.get()
        slots = [(hid_a, pre_a), (hid_b, pre_b)]

        def rise(i, k):
            rows, cols = pl.ds(k * step, step), pl.ds(i * size, size)
            hid, pre = slots[k % 2]
            hid[...] = matmul(second[rows, :], up_ref[:, cols])
            pre[...] = times_transposed(dn_ref[rows, :], dw_ref[cols, :])

        def gelu(i, k):
            rows, cols = pl.ds(k * step, step), pl.ds(i * size, size)
            hid, pre = slots[k % 2]
            h = hid[...] + upb[:, cols]
            cdf = 0.5 + 0.5 * lax.erf(h * (1.0 / math.sqrt(2.0)))
            slope = cdf + h * jnp.exp(-0.5 * h * h) * (1.0 / math.sqrt(2.0 * math.pi))
            acts[rows, cols] = (h * cdf).astype(bf16)
            grad = (pre[...] * slope).astype(bf16)
            grad_hid[rows, cols] = grad
            return column_sum(grad.astype(f32))

        for i in range(3):
            total = jnp.zeros((8, size), f32)
            rise(i, 0)
            for k in range(cuts):
                if k + 1 < cuts:
                    rise(i, k + 1)
                total = total + gelu(i, k)
            upb_sums[:, pl.ds(i * size, size)] = total
            (down_part, down_at), (up_part, up_at) = thirds[i]
            for source, chosen, right, (which, at) in (
                (dn_t.get(), chosen_a, acts, (down_part, down_at)),
                (second_t, chosen_b, grad_hid, (up_part, up_at)),
            ):
                split_products(
                    place_ref, bits[which], source, chosen, [(right, i * size, size, at)], gives[which].ref, keeps[which].ref
                )
            for which in {down_part, up_part}:
                gives[which].put()
                keeps[which].put()
        acts_o.put()
        gain_sum = jnp.zeros((8, width), f32)
        bias_sum = jnp.zeros((8, width), f32)
        for start in range(0, span, 128):
            rows = pl.ds(start, 128)
            part_o.ref[rows, :] = times_transposed(grad_hid[rows, :], up_ref[...])
            part_o.put(start, 128)
            if start:
                gain_sum, bias_sum = norm_sums(part_o.ref, resid, start - 128, gain_sum, bias_sum)
        gain_sum, bias_sum = norm_sums(part_o.ref, resid, span - 128, gain_sum, bias_sum)
        sums[pl.ds(0, 8), :] = gain_sum
        sums[pl.ds(8, 8), :] = bias_sum

    outs = [
        (shaped((span, width), f32), "h"),
        (shaped((span, hidden), bf16), "h"),
        (shaped((span, width), f32), "h"),
        (shaped((16, width), f32), "v"),
        (shaped((8, hidden), f32), "v"),
    ]
    outs += [(shaped((half, w), f32), "h") for w in widths] * 2
    scratch = [
        pltpu.VMEM((span, width), bf16),
        pltpu.VMEM((groups, rows_each, span), bf16),
        pltpu.VMEM((span, hidden), bf16),
        pltpu.VMEM((step, size), f32),
        pltpu.VMEM((step, size), f32),
        pltpu.VMEM((step, size), f32),
        pltpu.VMEM((step, size), f32),
        pltpu.VMEM((2, half, span), bf16),
        pltpu.VMEM((2, half, span), bf16),
    ]
    cut = span // step
    ins = [(place, "s"), (tokens, cut), (mine, cut), (other, cut), (gain, "v"), (bias, "v")]
    ins += [(down, "l"), (down_t, "l"), (up_weight, "l"), (up_bias, "v"), (down_weight, "l")]
    res = staged(run, ins, outs, "feed_forward_back", scratch)
    return res[:5], res[5 : 5 + parts], res[5 + parts :]


def mixer_back(
    length, place, down, mine, other, resid, feedgain, out_weight, mixed, query, sig16, ker16, table, table_t, skip,
    keypad, value, taps, normed_t, gated, weights, tokens, feed_sums, cuts,
):
    span, width = resid.shape
    chans = query.shape[1]
    groups, rows_each, _ = normed_t.shape
    half = width // 2
    block = table.shape[1]
    count = span // block
    lags = taps.shape[0]
    lanes = 128
    bits, pieces = cuts
    widths = [sum(n for _, _, n in part) for part in pieces]
    parts = len(bits)

    def run(*refs):
        len_ref, place_ref, dn, mine_ref, other_ref, resid_ref, gain_ref, wo, mixed_ref, query_ref = refs[:10]
        sig_ref, ker_ref, tab, tab_t, skip_ref, key, value_ref, taps_ref, norm_t, gated_ref = refs[10:20]
        wq, wk, wv, tok, feed_ref = refs[20:25]
        grad_resid_o, lag_o, part_o, skip_sums, taps_sums = refs[25:30]
        gives, keeps = refs[30 : 30 + parts], refs[30 + parts : 30 + 2 * parts]
        grad_mix, mix_t, mix_grad, bins, sigs, kers, back_prod, lag_prod, shifted_grad, grads, chosen, mix_sums = refs[30 + 2 * parts :]
        size = len_ref[0]
        grad_resid = grad_resid_o.ref
        grad_query, grad_key, grad_value = [pl.ds(k * chans, chans) for k in range(3)]

        for i in range(count):
            rows = pl.ds(i * block, block)
            scaled, inverse = norm_rows(resid_ref.get(i)[rows, :])
            grad = norm_back(mine_ref.get(i)[rows, :] + other_ref.get(i)[rows, :], scaled, inverse, gain_ref[...])
            grad = dn.get(i)[rows, :].astype(f32) + grad
            if i == 0:
                for item in (wo, query_ref, mixed_ref, tab, sig_ref, ker_ref, key, value_ref):
                    item.start()
            grad_resid[rows, :] = grad
            grad_resid_o.put(i * block, block)
            grad = grad.astype(bf16)
            grad_mix[rows, :] = grad
            turned = grad.T
            for j in range(groups):
                mix_t[j, :, rows] = turned[j * rows_each : (j + 1) * rows_each, :]
        before = None
        turn = 1.0 - 2.0 * (iota((2 * block, 1), 0) % 2).astype(f32)
        keypad, val = key.get(), value_ref.get()
        for item in (tab_t, norm_t, gated_ref, wq, wk, wv, tok):
            item.start()
        total = jnp.zeros((8, chans), f32)
        for i in range(count):
            rows, bin_rows = pl.ds(i * block, block), pl.ds(i * 2 * block, 2 * block)
            mask = row_mask(i * block, block, size)
            grad_gated = mask * times_transposed(grad_mix[rows, :], wo.get()[...])
            grads[rows, grad_query] = (grad_gated * mixed_ref.get()[rows, :]).astype(bf16)
            grad = grad_gated * query_ref.get()[rows, :]
            mix_grad[rows, :] = grad
            signal = mask * shift_conv(taps_ref, keypad, i * block, block) * val[rows, :]
            total = total + column_sum(grad * signal)
            sigs[bin_rows, :] = matmul(tab.get()[...], sig_ref.get()[rows, :])
            ker = matmul(tab.get()[...], ker_ref.get()[rows, :])
            kers[bin_rows, :] = ker if before is None else ker + turn * before
            before = ker
            bins[bin_rows, :] = matmul(tab.get()[...], grad.astype(bf16))
        skip_sums[...] = total

        def product(i, _):
            start = pl.multiple_of(i * 16, 16)
            row = iota((16, 1), 0) + start
            first = row == 0
            scale = jnp.where(first, 0.5 / block, 1.0 / block)
            sign = 1.0 - 2.0 * (row % 2).astype(f32)
            for lane in range(0, chans, lanes):
                cols = pl.ds(lane, lanes)

                def pair(ref, j):
                    return (
                        ref[pl.ds(j * 2 * block + start, 16), cols],
                        ref[pl.ds(j * 2 * block + block + start, 16), cols],
                    )

                def put(ref, j, real, imag):
                    ref[pl.ds(j * 2 * block + start, 16), cols] = (real * scale).astype(bf16)
                    ref[pl.ds(j * 2 * block + block + start, 16), cols] = (imag * scale).astype(bf16)

                grad_pairs = [pair(bins, j) for j in range(count)]

                def correlate(ref, pairs):
                    real = imag = None
                    for g, j in pairs:
                        a, b = grad_pairs[g]
                        c, d = pair(ref, j)
                        other, d = edge(first, c, d)
                        r = a * c + b * d
                        s = b * other - a * d
                        real = r if real is None else real + r
                        imag = s if imag is None else imag + s
                    return real, imag

                for j in range(count):
                    real, imag = correlate(kers, [(m, m - j) for m in range(j, count)])
                    put(back_prod, j, real, imag)
                later = None
                for j in reversed(range(count)):
                    real, imag = correlate(sigs, [(m + j, m) for m in range(count - j)])
                    if later is None:
                        put(lag_prod, j, real, imag)
                    else:
                        put(lag_prod, j, real + sign * later[0], imag + sign * later[1])
                    later = (real, imag)
            return 0

        lax.fori_loop(0, block // 16, product, 0)
        shifted_grad[pl.ds(span, pad), :] = jnp.zeros((pad, chans), f32)
        totals = [jnp.zeros((8, chans), f32)] * lags
        for i in range(count):
            rows = pl.ds(i * block, block)
            bin_rows = pl.ds(i * 2 * block, 2 * block)
            mask = row_mask(i * block, block, size)
            signal_grad = matmul(tab_t.get()[...], back_prod[bin_rows, :])
            lag_o.ref[rows, :] = matmul(tab_t.get()[...], lag_prod[bin_rows, :])
            signal_grad = mask * (signal_grad + skip_ref[...] * mix_grad[rows, :])
            shifted = shift_conv(taps_ref, keypad, i * block, block)
            grads[rows, grad_value] = (signal_grad * shifted).astype(bf16)
            moved = signal_grad * val[rows, :]
            shifted_grad[rows, :] = moved
            for lag in range(lags):
                lagged = keypad[pl.ds(i * block + pad - lag, block), :]
                totals[lag] = totals[lag] + column_sum(moved * lagged)
        lag_o.put()
        for lag in range(lags):
            taps_sums[pl.ds(lag * 8, 8), :] = totals[lag]
        for i in range(count):
            rows = pl.ds(i * block, block)
            grads[rows, grad_key] = sum(
                taps_ref[lag : lag + 1, :] * shifted_grad[pl.ds(i * block + lag, block), :]
                for lag in range(lags)
            ).astype(bf16)

        for i in range(parts):
            at, pairs = 0, ([], [])
            for which, start, n in pieces[i]:
                if which == 0:
                    pairs[0].append((gated_ref.get(), start, n, at))
                else:
                    pairs[1].append((grads, (which - 1) * chans + start, n, at))
                at += n
            for source, some in ((mix_t, pairs[0]), (norm_t.get(), pairs[1])):
                if some:
                    split_products(place_ref, bits[i], source, chosen, some, gives[i].ref, keeps[i].ref)
            gives[i].put()
            keeps[i].put()

        gain_sum = jnp.zeros((8, width), f32)
        bias_sum = jnp.zeros((8, width), f32)
        for start in range(0, span, 128):
            rows = pl.ds(start, 128)
            part_o.ref[rows, :] = sum(
                times_transposed(grads[rows, pl.ds(k * chans, chans)], w.get()[...]) for k, w in enumerate((wq, wk, wv))
            )
            part_o.put(start, 128)
            if start:
                gain_sum, bias_sum = norm_sums(part_o.ref, tok.get(), start - 128, gain_sum, bias_sum)
        gain_sum, bias_sum = norm_sums(part_o.ref, tok.get(), span - 128, gain_sum, bias_sum)
        mix_sums[pl.ds(0, 8), :] = gain_sum
        mix_sums[pl.ds(8, 8), :] = bias_sum
        mix_sums[pl.ds(16, 16), :] = feed_ref[...]
        part_o.put(span, 32, mix_sums)

    outs = [
        (shaped((span, width), f32), "=5"),
        (shaped((span, chans), f32), "h"),
        (shaped((span + 32, width), f32), "=3"),
        (shaped((8, chans), f32), "v"),
        (shaped((8 * lags, chans), f32), "v"),
    ]
    outs += [(shaped((half, w), f32), "h") for w in widths] * 2
    scratch = [
        pltpu.VMEM((span, width), bf16),
        pltpu.VMEM((groups, rows_each, span), bf16),
        pltpu.VMEM((span, chans), f32),
        pltpu.VMEM((2 * span, chans), f32),
        pltpu.VMEM((2 * span, chans), f32),
        pltpu.VMEM((2 * span, chans), f32),
        pltpu.VMEM((2 * span, chans), bf16),
        pltpu.VMEM((2 * span, chans), bf16),
        pltpu.VMEM((span + pad, chans), f32),
        pltpu.VMEM((span, 3 * chans), bf16),
        pltpu.VMEM((2, half, span), bf16),
        pltpu.VMEM((32, width), f32),
    ]
    ins = [(length, "s"), (place, "s"), (down, count), (mine, count), (other, count), (resid, count), (feedgain, "v")]
    ins += [(x, "l") for x in (out_weight, mixed, query, sig16, ker16, table, table_t)] + [(skip, "v")]
    ins += [(keypad, "l"), (value, "l"), (taps, "v"), (normed_t, "l"), (gated, "l")]
    ins += [(weight, "l") for weight in weights] + [(tokens, "l"), (feed_sums, "v")]
    res = staged(run, ins, outs, "mixer_back", scratch)
    return res[:5], res[5 : 5 + parts], res[5 + parts :]


def feed_down(acts, down_weight):
    span = acts.shape[0]
    width = down_weight.shape[1]

    def run(act, down, out):
        for start in range(0, span, 128):
            out.ref[pl.ds(start, 128), :] = matmul(act.get()[pl.ds(start, 128), :], down.get()[...])
            out.put(start, 128)

    outs = [(shaped((span, width), f32), "h")]
    return staged(run, [(acts, "h"), (down_weight, "h")], outs, "feed_down")[0]


def finish_rows(length, tokens, grad_resid, mine, other, gain, resid, down_mine, down_other, down_bias):
    span, width = tokens.shape
    rows = 128

    def run(len_ref, tok, grad_ref, mine_ref, other_ref, gain_ref, resid_ref, a, b, bias_ref, grad_o, out):
        scaled, inverse = norm_rows(tok[...].astype(f32))
        grad = mine_ref[...] + other_ref[...]
        grad_o[...] = grad_ref[...] + norm_back(grad, scaled, inverse, gain_ref[...].reshape(1, width))
        mask = row_mask(pl.program_id(0) * rows, rows, len_ref[0])
        value = resid_ref[...] + ((a[...] + b[...]) + bias_ref[...].reshape(1, width))
        out[...] = (mask * value).astype(bf16)

    block = pl.BlockSpec((rows, width), lambda i: (i, 0))
    return pl.pallas_call(
        run,
        grid=(span // rows,),
        in_specs=[in_smem] + [block] * 4 + [in_vmem] + [block] * 3 + [in_vmem],
        out_specs=[block, block],
        out_shape=[shaped((span, width), f32), shaped((span, width), bf16)],
        compiler_params=pltpu.CompilerParams(vmem_limit_bytes=60 << 20),
        cost_estimate=small_cost,
        name="finish_rows",
    )(length, tokens, grad_resid, mine, other, gain, resid, down_mine, down_other, down_bias)


def halve(place, parts, rows, widths, theirs, before=None):
    n, n_out = len(parts), len(widths)
    halves = [keep.shape[0] // 2 for keep, *_ in parts]
    runs = [1 << pos for _, _, pos, *_ in parts]
    copies_each = [half // rows // size for half, size in zip(halves, runs)]

    def run(place_ref, *refs):
        keeps, gots = refs[:n], refs[n : 2 * n]
        refs = refs[2 * n + (0 if before is None else n_out) :]
        outs, refs = refs[:n_out], refs[n_out:]
        sums, adds, sems = refs[:n], refs[n : 2 * n], refs[2 * n]
        waits, at = [], 0
        for i, (_, _, pos, bit, _, _) in enumerate(parts):
            mine = (place_ref[0] >> bit) & 1
            side = 1 - mine if theirs else mine
            waits.append([])
            for j in range(copies_each[i]):
                first = insert_bit(j * runs[i], pos, side) * rows
                source = pl.ds(pl.multiple_of(first, rows), runs[i] * rows)
                target = pl.ds(j * runs[i] * rows, runs[i] * rows)
                for array, held in ((keeps[i], sums[i]), (gots[i], adds[i])):
                    copy = pltpu.make_async_copy(array.at[source], held.at[target], sems.at[at])
                    copy.start()
                    waits[i].append(copy)
                    at += 1
        copies = []
        for i, (_, _, _, _, out, start) in enumerate(parts):
            for copy in waits[i]:
                copy.wait()
            sums[i][...] = sums[i][...] + adds[i][...]
            target = outs[out].at[:, pl.ds(start, sums[i].shape[1])]
            copies.append(pltpu.make_async_copy(sums[i], target, sems.at[at]))
            copies[-1].start()
            at += 1
        for copy in copies:
            copy.wait()

    ins = [(place, "s")] + [(part[0], "a") for part in parts] + [(part[1], "a") for part in parts]
    aliases = None
    if before is not None:
        aliases = {len(ins) + k: k for k in range(n_out)}
        ins += [(item, "a") for item in before]
    outs = [(shaped((halves[0], w), f32), "a") for w in widths]
    scratch = [pltpu.VMEM((halves[i], parts[i][0].shape[1]), f32) for i in range(n)] * 2
    scratch.append(pltpu.SemaphoreType.DMA((2 * sum(copies_each) + n,)))
    return staged(run, ins, outs, "halve", scratch, aliases)


def pack_small(coef, rate, taps, skip, upbias, downbias, norms, norms_other):
    states, chans = coef.shape
    lags = taps.shape[0] // 8
    wide = [(upbias, None), (downbias, None)]
    counts = [states, states, lags, 1, upbias.shape[1] // chans, downbias.shape[1] // chans]
    counts.append(4 * (norms.shape[1] // chans))
    total = -(-sum(counts) // 8) * 8

    def run(coef_ref, rate_ref, taps_ref, skip_ref, up_ref, down_ref, norm_a, norm_b, out):
        out[...] = jnp.zeros_like(out)
        out[pl.ds(0, states), :] = coef_ref[...]
        out[pl.ds(states, states), :] = rate_ref[...]
        at = 2 * states

        def lay(value, at):
            row = jnp.sum(value, 0, keepdims=True)
            for start in range(0, row.shape[1], chans):
                out[pl.ds(at, 1), :] = row[:, start : start + chans]
                at += 1
            return at

        for lag in range(lags):
            at = lay(taps_ref[pl.ds(8 * lag, 8), :], at)
        at = lay(skip_ref[...], at)
        at = lay(up_ref[...], at)
        at = lay(down_ref[...], at)
        for start in range(0, 32, 8):
            rows = pl.ds(start, 8)
            at = lay(norm_a[rows, :] + norm_b[rows, :], at)

    ins = [coef, rate, taps, skip, upbias, downbias, norms, norms_other]
    ins = [(x, "v") for x in ins[:6]] + [(x, "t") for x in ins[6:]]
    out = staged(run, ins, [(shaped((total, chans), f32), "v")], "pack_small")[0]
    return out, counts


def unpack_small(mine, other, counts, lags, hidden, width):
    chans = mine.shape[1]

    def run(a, b, coef, rate, taps, skip, up, down, *norms):
        at = 0
        for out in (coef, rate, taps):
            rows = pl.ds(at, out.shape[0])
            out[...] = a[rows, :] + b[rows, :]
            at += out.shape[0]
        for out in (skip, up, down, *norms):
            for start in range(0, out.shape[1], chans):
                row = pl.ds(at, 1)
                out[:, pl.ds(start, chans)] = a[row, :] + b[row, :]
                at += 1

    states = counts[0]
    outs = [(shaped((n, chans), f32), "v") for n in (states, states, lags)]
    outs += [(shaped((n,), f32), "v") for n in (chans, hidden, width, width, width, width, width)]
    return staged(run, [(mine, "v"), (other, "v")], outs, "unpack_small")


def collect(keeps, gots, layout, sizes):
    n = len(keeps)
    rows = keeps[0].shape[0]
    names = list(sizes)

    def run(*refs):
        outs = dict(zip(names, refs[2 * n :]))
        for i in range(n):
            total = refs[i][...] + refs[n + i][...]
            at = 0
            for name, start, count in layout[i]:
                piece = total[:, at : at + count]
                if sizes[name][1]:
                    outs[name][pl.ds(start, count), :] = piece.T
                else:
                    outs[name][:, pl.ds(start, count)] = piece
                at += count

    outs = []
    for columns, turned in sizes.values():
        outs.append((shaped((columns, rows) if turned else (rows, columns), f32), "v"))
    res = staged(run, [(x, "v") for x in (*keeps, *gots)], outs, "collect")
    return dict(zip(names, res))


def state_grads(coef_t, rate_t, lag_grad):
    states, chans = coef_t.shape
    span = lag_grad.shape[0]
    step = 32
    blocks = span // step
    lanes = 128
    group = 8
    tiles = step // 8

    def run(coef_ref, rate_ref, lag_ref, coef_out, rate_out, fine, coarse, plain, place, ramp):
        rate = rate_ref[...][:, None, :]
        within = lax.broadcasted_iota(jnp.int32, (1, step, 1), 1).astype(f32)
        across = lax.broadcasted_iota(jnp.int32, (1, blocks, 1), 1).astype(f32)
        fine[...] = jnp.exp(-rate * within)
        coarse[...] = jnp.exp(-rate * (step * across))
        plain[...] = jnp.zeros_like(plain)
        place[...] = jnp.zeros_like(place)
        ramp[...] = jnp.zeros_like(ramp)
        for base in range(0, blocks, group):
            lag = [
                [
                    lag_ref[pl.ds((base + j) * step + 8 * a, 8), :]
                    for a in range(tiles)
                ]
                for j in range(group)
            ]

            def add(n, _):
                near = [fine[n, pl.ds(8 * a, 8), :] for a in range(tiles)]
                suffix = None
                later = None
                tilted = None
                for j in reversed(range(group)):
                    far = coarse[n, pl.ds(base + j, 1), :]
                    total = None
                    slope = None
                    for a in reversed(range(tiles)):
                        term = lag[j][a] * near[a]
                        if total is None:
                            total = term
                        else:
                            slope = total if slope is None else slope + total
                            total = total + term
                    weighted = far * total
                    bent = far * slope
                    tilted = bent if tilted is None else tilted + bent
                    if suffix is None:
                        suffix = weighted
                    else:
                        later = suffix if later is None else later + suffix
                        suffix = suffix + weighted
                plain[n] = plain[n] + suffix
                place[n] = place[n] + (later + float(base) * suffix)
                ramp[n] = ramp[n] + tilted
                return 0

            lax.fori_loop(0, states, add, 0, unroll=4)
        rows = lax.broadcasted_iota(jnp.int32, (1, 8, 1), 1).astype(f32)
        whole = plain[...]
        coef_out[...] = jnp.sum(whole, 1)
        times = float(step) * place[...] + 8.0 * ramp[...] + rows * whole
        rate_out[...] = -coef_ref[...] * jnp.sum(times, 1)

    shape = jax.ShapeDtypeStruct((states, chans), f32)
    block = pl.BlockSpec((states, lanes), lambda i: (0, i))
    return pl.pallas_call(
        run,
        grid=(chans // lanes,),
        in_specs=[block, block, pl.BlockSpec((span, lanes), lambda i: (0, i))],
        out_specs=[block, block],
        out_shape=[shape, shape],
        scratch_shapes=[
            pltpu.VMEM((states, step, lanes), f32),
            pltpu.VMEM((states, blocks, lanes), f32),
        ]
        + [pltpu.VMEM((states, 8, lanes), f32)] * 3,
        compiler_params=pltpu.CompilerParams(vmem_limit_bytes=60 << 20),
        cost_estimate=small_cost,
        name="state_grads",
    )(coef_t, rate_t, lag_grad)


def follow(values, *before):
    held = lax.optimization_barrier((list(values), before))[0]
    return held


def body(
    tokens,
    lengths,
    mixgain,
    mixbias,
    query_weight,
    key_weight,
    value_weight,
    shift_taps,
    state_coef,
    state_rate,
    state_skip,
    out_weight,
    feedgain,
    feedbias,
    up_weight,
    up_bias,
    down_weight,
    down_bias,
    cotangent,
):
    assert lengths.shape[0] == 1
    span, width = tokens.shape
    chans = query_weight.shape[1]
    hidden = up_weight.shape[1]
    lags = shift_taps.shape[0]
    places = lax.axis_size("freq")
    halving = places == 16 and width % (16 * places) == 0
    groups = places if halving else 2
    rows = width // groups
    place = lax.axis_index("freq").astype(jnp.int32).reshape(1)
    if halving:
        orders = [[0, 1, 2, 3], [1, 0, 3, 2], [2, 3, 0, 1], [3, 2, 0, 1]]
        small_bits = [1, 0, 2, 3]
    else:
        place = jnp.zeros_like(place)
        orders = [[0]] * 4
    bits = [order[0] for order in orders]

    third, part = hidden // 3, chans // 3
    layout = [
        [("down", 0, third), ("up", 0, third), ("out", 0, 3 * part), ("query", 0, part)],
        [("down", third, third), ("up", third, third), ("query", part, 2 * part), ("key", 0, 2 * part)],
        [("down", 2 * third, third), ("key", 2 * part, part), ("value", 0, part)],
        [("up", 2 * third, third), ("value", part, 2 * part)],
    ]
    first_widths = [2 * third, 2 * third, third, third]
    thirds = [((0, 0), (0, third)), ((1, 0), (1, third)), ((2, 0), (3, 0))]
    order_of = {"out": 0, "query": 1, "key": 2, "value": 3}
    pieces = [[(order_of[n], s, c) for n, s, c in cols if n in order_of] for cols in layout]
    widths = [sum(c for _, _, c in cols) for cols in layout]

    block = 256
    table_np = dft_table(block)
    table, table_t = jnp.asarray(table_np), jnp.asarray(np.ascontiguousarray(table_np.T))
    coef_t, rate_t = state_coef.T, state_rate.T

    normed, query, keypad, value, mixed, gated, sig16, ker16, out_part = mixer_forward(
        lengths,
        tokens,
        mixgain,
        mixbias,
        (query_weight, key_weight, value_weight),
        shift_taps,
        coef_t,
        rate_t,
        state_skip,
        out_weight,
        table,
        table_t,
    )
    out_other = swap(out_part, "tp", 0)
    down, down_t, normed_t, downbias_part = feed_prepare(lengths, cotangent, normed)
    down_t = down_t.reshape(groups, rows, span)
    normed_t = normed_t.reshape(groups, rows, span)
    (resid, acts, second_part, feed_sums, upbias_part), gives, keeps = feed_forward_back(
        place, tokens, out_part, out_other, feedgain, feedbias, down, down_t, up_weight, up_bias, down_weight, (bits, first_widths, thirds)
    )
    second_other = swap(second_part, "tp", 0)
    if halving:
        gots = [swap(give, "freq", bit) for give, bit in zip(gives, bits)]
    (grad_resid, lag_grad, normed_part, skip_part, taps_part), more_gives, more_keeps = mixer_back(
        lengths, place, down, second_part, second_other, resid, feedgain, out_weight, mixed, query, sig16, ker16, table, table_t, state_skip,
        keypad, value, shift_taps, normed_t, gated, (query_weight, key_weight, value_weight), tokens, feed_sums, (bits, pieces)
    )
    if halving:

        def parts(keeps, gots, step, places):
            return [
                (keep, got, sorted(order[step:]).index(order[step]), order[step], *to)
                for keep, got, order, to in zip(keeps, gots, orders, places)
            ]

        def exchange(gives, step):
            return [swap(give, "freq", order[step]) for give, order in zip(gives, orders)]

        def add_swapped(value, bit):
            return value + swap(value, "freq", bit)

        gots = follow(gots, *more_gives)
        more_gives, lag_grad, normed_part = follow([more_gives, lag_grad, normed_part], *gots)
        more_gots = exchange(more_gives, 0)
        at_first = [(i, 0) for i in range(4)]
        pieces = parts(keeps, gots, 1, at_first)
        held_gives = halve(place, pieces, rows, widths, True)
        held_keeps = halve(place, pieces, rows, widths, False)
        (acts,) = follow([acts], held_keeps[0], held_gives[0])
    normed_other = swap(normed_part, "tp", 0)
    down_part = feed_down(acts, down_weight)
    if halving:
        more_gots = follow(more_gots, down_part, normed_other)
        pieces = parts(more_keeps, more_gots, 1, list(enumerate(first_widths)))
        gives = halve(place, pieces, rows, widths, True, held_gives)
        gots = exchange(gives, 1)
        down_part, lag_grad, more_gots[0] = follow([down_part, lag_grad, more_gots[0]], *gives)
        pieces = parts(more_keeps, more_gots, 1, list(enumerate(first_widths)))
        keeps = halve(place, pieces, rows, widths, False, held_keeps)
        (lag_grad,) = follow([lag_grad], *keeps)
    down_other = swap(down_part, "tp", 0)
    coef_part, rate_part = state_grads(coef_t, rate_t, lag_grad)
    small, counts = pack_small(
        coef_part, rate_part, taps_part, skip_part, upbias_part, downbias_part, normed_part, normed_other
    )
    if halving:
        gots = follow(gots, down_other, small)
        at_last = [(0, 0), (1, 0), (2, 0), (2, widths[2])]
        last_widths = [widths[0], widths[1], widths[2] + widths[3]]
        pieces = parts(keeps, gots, 2, at_last)
        gives = halve(place, pieces, rows, last_widths, True)
        small, normed_part = follow([small, normed_part], *gives)
        old = gots
        gots = exchange(gives, 2)
        (old[0],) = follow([old[0]], *gives)
        keeps = halve(place, parts(keeps, old, 2, at_last), rows, last_widths, False)
        small = add_swapped(small, small_bits[0])
        small = add_swapped(small, small_bits[1])
        (normed_part,) = follow([normed_part], *keeps)
    tokens_grad, layer_out = finish_rows(
        lengths, tokens, grad_resid, normed_part, normed_other, mixgain, resid, down_part, down_other, down_bias
    )
    if halving:
        gots = follow(gots, tokens_grad, small)
        pieces = parts(keeps, gots, 3, at_first)
        gives = halve(place, pieces, rows, last_widths, True)
        (small,) = follow([small], *gives)
        old = gots
        gots = exchange(gives, 3)
        (old[0],) = follow([old[0]], *gives)
        keeps = halve(place, parts(keeps, old, 3, at_first), rows, last_widths, False)
        small = add_swapped(small, small_bits[2])
        coef_sum, rate_sum, taps_sum, skip_sum, upbias_sum, downbias_sum, *norms = unpack_small(
            small, swap(small, "freq", small_bits[3]), counts, lags, hidden, width
        )
        sizes = {"down": (hidden, False), "up": (hidden, False), "out": (chans, False)}
        sizes |= {name: (chans, False) for name in ("query", "key", "value")}
        grads = collect(keeps, gots, [layout[0], layout[1], layout[2] + layout[3]], sizes)
    else:
        small = lax.psum(small, "freq")
        grads = {name: [] for name in ("down", "up", "out", "query", "key", "value")}
        for i, (cols, count) in enumerate(zip(layout, first_widths)):
            whole = [
                jnp.concatenate([jnp.concatenate([k, m], 1) for k, m in ((keeps[i], more_keeps[i]), (gives[i], more_gives[i]))], 0)
            ][0]
            total = lax.psum_scatter(whole, "freq", scatter_dimension=0, tiled=True)
            at = 0
            for name, _, columns in cols:
                grads[name].append(total[:, at : at + columns])
                at += columns
        grads = {name: jnp.concatenate(some, 1) for name, some in grads.items()}
        cuts = np.cumsum(counts)
        coef_sum, rate_sum, taps_sum, skip_sum, upbias_sum, downbias_sum, norms, _ = jnp.split(small, cuts)
        norms = norms.reshape(4, width)
        skip_sum, upbias_sum, downbias_sum = [x.reshape(-1) for x in (skip_sum, upbias_sum, downbias_sum)]
    return (
        layer_out,
        tokens_grad,
        norms[0],
        norms[1],
        grads["query"],
        grads["key"],
        grads["value"],
        taps_sum,
        coef_sum.T,
        rate_sum.T,
        skip_sum,
        grads["out"].T,
        norms[2],
        norms[3],
        grads["up"],
        upbias_sum,
        grads["down"].T,
        downbias_sum,
    )


def solution(mesh):
    in_specs = (
        P("freq", None),
        P("freq"),
        P(),
        P(),
        P(None, "tp"),
        P(None, "tp"),
        P(None, "tp"),
        P(None, "tp"),
        P("tp", None),
        P("tp", None),
        P("tp"),
        P("tp", None),
        P(),
        P(),
        P(None, "tp"),
        P("tp"),
        P("tp", None),
        P(),
        P("freq", None),
    )
    out_specs = (
        P("freq", None),
        P("freq", None),
        P(),
        P(),
        P("freq", "tp"),
        P("freq", "tp"),
        P("freq", "tp"),
        P(None, "tp"),
        P("tp", None),
        P("tp", None),
        P("tp"),
        P("tp", "freq"),
        P(),
        P(),
        P("freq", "tp"),
        P("tp"),
        P("tp", "freq"),
        P(),
    )
    return jax.shard_map(body, mesh=mesh, in_specs=in_specs, out_specs=out_specs, check_vma=False)
```

```python
import math

import jax
import jax.numpy as jnp
import numpy as np
from jax import lax
from jax.experimental import pallas as pl
from jax.experimental.pallas import tpu as pltpu
from jax.sharding import PartitionSpec as P

f32 = jnp.float32
bf16 = jnp.bfloat16
in_vmem = pl.BlockSpec(memory_space=pltpu.VMEM)
in_smem = pl.BlockSpec(memory_space=pltpu.SMEM)
anywhere = pl.BlockSpec(memory_space=pl.ANY)
pad = 8
most_vmem = (64 << 20) - (128 << 10)
small_cost = pl.CostEstimate(flops=1, bytes_accessed=1, transcendentals=0)


def shaped(shape, dtype):
    return jax.ShapeDtypeStruct(shape, dtype)


def size_of(item):
    return math.prod(item.shape) * jnp.dtype(item.dtype).itemsize


def call(run, ins, outs, name, scratch=(), flops=0, moved=0, specs=None):
    held = sum(size_of(item) for item in (*ins, *outs, *scratch))
    return pl.pallas_call(
        run,
        in_specs=specs or [in_vmem] * len(ins),
        out_specs=[in_vmem] * len(outs),
        out_shape=outs,
        scratch_shapes=list(scratch),
        compiler_params=pltpu.CompilerParams(vmem_limit_bytes=held + (6 << 20)),
        cost_estimate=small_cost,
        name=name,
    )(*ins)


def matmul(left, right):
    return jnp.dot(left, right, preferred_element_type=f32)


def times_transposed(left, right):
    return lax.dot_general(left, right, (((1,), (1,)), ((), ())), preferred_element_type=f32)


def swap(value, axis, bit):
    size = lax.axis_size(axis)
    return lax.ppermute(value, axis, [(i, i ^ (1 << bit)) for i in range(size)])


def dft_table(block):
    bins = np.arange(block)[:, None].astype(np.int64)
    times = np.arange(block)[None, :].astype(np.int64)
    angle = (bins * times % (2 * block)) * (math.pi / block)
    table = np.concatenate([np.cos(angle), np.sin(angle)], 0)
    table[block] = 1 - 2 * (np.arange(block) % 2)
    return table.astype(jnp.bfloat16)


def iota(shape, dim):
    return lax.broadcasted_iota(jnp.int32, shape, dim)


def row_mask(first, count, length):
    return (iota((count, 1), 0) + first < length).astype(f32)


def insert_bit(index, pos, bit):
    low = index & ((1 << pos) - 1)
    return ((index >> pos) << (pos + 1)) | (bit << pos) | low


def norm_rows(value):
    mean = jnp.mean(value, -1, keepdims=True)
    centered = value - mean
    inverse = lax.rsqrt(jnp.mean(centered * centered, -1, keepdims=True) + 1e-05)
    return centered * inverse, inverse


def norm_back(grad_out, scaled, inverse, gain):
    weighted = grad_out * gain
    return inverse * (
        weighted
        - jnp.mean(weighted, -1, keepdims=True)
        - scaled * jnp.mean(weighted * scaled, -1, keepdims=True)
    )


def column_sum(value):
    rows, width = value.shape
    return jnp.sum(value.reshape(rows // 8, 8, width), 0)


def shift_conv(taps, keypad, start, count):
    lags = taps.shape[0]
    return sum(
        taps[lag : lag + 1, :] * keypad[pl.ds(start + pad - lag, count), :] for lag in range(lags)
    )


def edge(first, real, imag):
    return jnp.where(first, imag, real), jnp.where(first, 0.0, imag)


class Coming:
    def __init__(self, source, held, sems, cuts=1):
        self.held, self.started, self.here = held, 0, 0
        if source.shape[-2:] != held.shape[-2:] and len(source.shape) > 1 and cuts == 1:
            last = pl.ds(source.shape[0] - held.shape[0], held.shape[0])
            self.copies = [pltpu.make_async_copy(source.at[last], held, sems.at[0])]
            return
        if len(source.shape) == 1:
            self.copies = [pltpu.make_async_copy(source, held.at[0], sems.at[0])]
            return
        rows = held.shape[0] // cuts
        self.copies = []
        for i in range(cuts):
            part = pl.ds(i * rows, rows) if cuts > 1 else pl.ds(0, held.shape[0])
            self.copies.append(pltpu.make_async_copy(source.at[part], held.at[part], sems.at[i]))

    def start(self, cuts=None):
        cuts = len(self.copies) if cuts is None else cuts
        while self.started < cuts:
            self.copies[self.started].start()
            self.started += 1

    def get(self, cut=None):
        self.start(None if cut is None else cut + 1)
        until = len(self.copies) if cut is None else cut + 1
        while self.here < until:
            self.copies[self.here].wait()
            self.here += 1
        return self.held


class Going:
    def __init__(self, target, held, sems):
        self.target, self.ref, self.sems, self.copies = target, held, sems, []

    def put(self, start=0, count=None, source=None):
        rows = pl.ds(start, self.ref.shape[0] if count is None else count)
        sem = self.sems.at[len(self.copies)]
        if len(self.target.shape) == 1:
            copy = pltpu.make_async_copy(self.ref.at[0], self.target, sem)
        else:
            source = self.ref.at[rows] if source is None else source
            copy = pltpu.make_async_copy(source, self.target.at[rows], sem)
        copy.start()
        self.copies.append(copy)


    def put_columns(self, start, count):
        cols = pl.ds(start, count)
        sem = self.sems.at[len(self.copies)]
        copy = pltpu.make_async_copy(self.ref.at[:, cols], self.target.at[:, cols], sem)
        copy.start()
        self.copies.append(copy)


most_puts = 16
most_cuts = 4
in_hbm = pl.BlockSpec(memory_space=pl.ANY)


def staged(run, ins, outs, name, scratch=(), aliases=None):
    spec = {"s": in_smem}
    plain = ("s", "a")
    shared = lambda kind: isinstance(kind, str) and kind[0] == "="
    top = lambda kind: isinstance(kind, tuple)

    def tail(x, kind):
        if kind == "t" or top(kind):
            return shaped((32 if kind == "t" else x.shape[0] - 32, x.shape[1]), x.dtype)
        return x

    held = [tail(x, kind) for x, kind in (*ins, *outs) if kind not in plain and not shared(kind)]
    held = [shaped(x.shape if len(x.shape) > 1 else (1, *x.shape), x.dtype) for x in held]
    n_in = sum(kind not in plain for _, kind in ins)
    n_out = sum(kind not in plain for _, kind in outs)

    def whole(*refs):
        refs = list(refs)
        given, made = refs[: len(ins)], refs[len(ins) : len(ins) + len(outs)]
        rest = refs[len(ins) + len(outs) :]
        own, bufs = rest[: len(scratch)], rest[len(scratch) :]
        in_sems, out_sems = bufs[-2:]
        bufs = list(bufs[:-2])
        views, at = [], 0
        for ref, (_, kind) in zip(given, ins):
            if kind not in plain:
                cuts = kind[1] if top(kind) else kind if isinstance(kind, int) else 1
                views.append(Coming(ref, bufs.pop(0), in_sems.at[at], cuts))
                at += 1
                if kind != "l" and cuts == 1:
                    views[-1].start()
            else:
                views.append(ref)
        going, at = [], 0
        for ref, (_, kind) in zip(made, outs):
            if kind not in plain:
                held_at = views[int(kind[1:])].held if shared(kind) else bufs.pop(0)
                going.append(Going(ref, held_at, out_sems.at[at]))
                at += 1
            else:
                going.append(ref)
        for view, (_, kind) in zip(views, ins):
            if kind in ("v", "t"):
                view.get()
        views = [view.held if kind in ("v", "t") else view for view, (_, kind) in zip(views, ins)]
        small = [item for item, (_, kind) in zip(going, outs) if kind == "v"]
        run(*views, *[item.ref if item in small else item for item in going], *own)
        for item in small:
            item.put()
        for view in views:
            if isinstance(view, Coming):
                view.get()
        for item in going:
            if isinstance(item, Going):
                for copy in item.copies:
                    copy.wait()

    return pl.pallas_call(
        whole,
        in_specs=[spec.get(kind, in_hbm) for _, kind in ins],
        out_specs=[spec.get(kind, in_hbm) for _, kind in outs],
        out_shape=[item for item, _ in outs],
        scratch_shapes=list(scratch)
        + [pltpu.VMEM(x.shape, x.dtype) for x in held]
        + [
            pltpu.SemaphoreType.DMA((max(n_in, 1), most_cuts)),
            pltpu.SemaphoreType.DMA((max(n_out, 1), most_puts)),
        ],
        input_output_aliases=aliases or {},
        compiler_params=pltpu.CompilerParams(vmem_limit_bytes=most_vmem),
        cost_estimate=small_cost,
        name=name,
    )(*[x for x, _ in ins])


def split_products(place_ref, bit, source, chosen, pairs, give, keep):
    groups, rows, _ = source.shape
    mine = (place_ref[0] >> bit) & 1
    for k, (out, side) in enumerate(((give, 1 - mine), (keep, mine))):
        for j in range(groups // 2):
            chosen[k, pl.ds(j * rows, rows), :] = source[insert_bit(j, bit, side)]
    for k, out in enumerate((give, keep)):
        for right, start, count, to in pairs:
            out[:, pl.ds(to, count)] = matmul(chosen[k], right[:, pl.ds(start, count)])


def mixer_forward(length, tokens, gain, bias, weights, taps, coef_t, rate_t, skip, out_weight, table, table_t):
    span, width = tokens.shape
    chans = out_weight.shape[0]
    states = coef_t.shape[0]
    block = table.shape[1]
    count = span // block
    step = 32
    far_steps = span // step
    group = 8
    lanes = 128

    def run(
        len_ref, tok, gain_ref, bias_ref, wq, wk, wv, taps_ref, coef_ref, rate_ref, skip_ref, wo, tab, tab_t,
        normed_o, query_o, keypad_o, value_o, mixed_o, gated_o, sig_o, ker_o, part_o,
        fine, coarse, signal, sig_bins, ker_bins, prod,
    ):
        size = len_ref[0]
        normed, query, keypad, value = normed_o.ref, query_o.ref, keypad_o.ref, value_o.ref
        sig16, ker16 = sig_o.ref, ker_o.ref

        within = iota((1, step, 1), 1).astype(f32)
        across = iota((1, group, 1), 1).astype(f32) * float(step)
        rate = rate_ref[...][:, None, :]
        fine[...] = jnp.exp(-rate * within)
        for k in range(far_steps // group):
            coarse[:, k] = coef_ref[...][:, None, :] * jnp.exp(-rate * (across + float(step * group * k)))
        keypad[pl.ds(0, pad), :] = jnp.zeros((pad, chans), f32)
        tok_ref, wq_ref, wk_ref, wv_ref = tok.get(), wq.get(), wk.get(), wv.get()
        for item in (wo, tab, tab_t):
            item.start()

        def first_part(i, _):
            start = pl.multiple_of(i * block, block)
            rows = pl.ds(start, block)
            scaled, _ = norm_rows(tok_ref[rows, :].astype(f32))
            norm = (scaled * gain_ref[...] + bias_ref[...]).astype(bf16)
            normed[rows, :] = norm
            key_rows = pl.ds(pl.multiple_of(start + pad, 8), block)
            products = [(query, rows, wq_ref), (keypad, key_rows, wk_ref), (value, rows, wv_ref)]
            for lane in range(0, chans, lanes):
                if products:
                    out, place, weight = products.pop(0)
                    out[place, :] = matmul(norm, weight[...])
                cols = pl.ds(lane, lanes)
                sums = [None] * group
                for n in range(states):
                    near = fine[n, :, cols]
                    for j in range(group):
                        term = coarse[n, i, pl.ds(j, 1), cols] * near
                        sums[j] = term if n == 0 else sums[j] + term
                for j in range(group):
                    place = pl.ds(pl.multiple_of(start + j * step, step), step)
                    ker16[place, cols] = sums[j].astype(bf16)
            return 0

        lax.fori_loop(0, count, first_part, 0)
        normed_o.put()
        for i in range(count):
            rows = pl.ds(i * block, block)
            shifted = shift_conv(taps_ref, keypad, i * block, block)
            sig = row_mask(i * block, block, size) * shifted * value[rows, :]
            signal[rows, :] = sig
            sig16[rows, :] = sig.astype(bf16)
        sig_o.put()
        ker_o.put()
        query_o.put()
        keypad_o.put()
        value_o.put()

        sign = 1.0 - 2.0 * (iota((2 * block, 1), 0) % 2).astype(f32)
        before = None
        for i in range(count):
            bins = pl.ds(i * 2 * block, 2 * block)
            rows = pl.ds(i * block, block)
            sig_bins[bins, :] = matmul(tab.get()[...], sig16[rows, :])
            ker = matmul(tab.get()[...], ker16[rows, :])
            ker_bins[bins, :] = ker if before is None else ker + sign * before
            before = ker

        def product(i, _):
            start = pl.multiple_of(i * 16, 16)
            first = (iota((16, 1), 0) + start) == 0
            scale = jnp.where(first, 0.5 / block, 1.0 / block)
            for lane in range(0, chans, lanes):
                cols = pl.ds(lane, lanes)

                def pair(ref, j):
                    return (
                        ref[pl.ds(j * 2 * block + start, 16), cols],
                        ref[pl.ds(j * 2 * block + block + start, 16), cols],
                    )

                sigs = [pair(sig_bins, j) for j in range(count)]
                kers = []
                for j in range(count):
                    c, d = pair(ker_bins, j)
                    other, d = edge(first, c, d)
                    kers.append((c, other, d))
                for j in range(count):
                    real = imag = None
                    for m in range(j + 1):
                        a, b = sigs[m]
                        c, other, d = kers[j - m]
                        r = a * c - b * d
                        s = a * d + b * other
                        real = r if real is None else real + r
                        imag = s if imag is None else imag + s
                    prod[pl.ds(j * 2 * block + start, 16), cols] = (real * scale).astype(bf16)
                    prod[pl.ds(j * 2 * block + block + start, 16), cols] = (imag * scale).astype(bf16)
            return 0

        lax.fori_loop(0, block // 16, product, 0)
        for i in range(count):
            rows = pl.ds(i * block, block)
            conv = matmul(tab_t.get()[...], prod[pl.ds(i * 2 * block, 2 * block), :])
            mixed = conv + skip_ref[...] * signal[rows, :]
            mixed_o.ref[rows, :] = mixed
            gated = (row_mask(i * block, block, size) * query[rows, :] * mixed).astype(bf16)
            gated_o.ref[rows, :] = gated
            part_o.ref[rows, :] = matmul(gated, wo.get()[...])
            for item in (part_o, mixed_o, gated_o):
                item.put(i * block, block)

    outs = [
        (shaped((span, width), bf16), "h"),
        (shaped((span, chans), f32), "h"),
        (shaped((span + pad, chans), f32), "h"),
        (shaped((span, chans), f32), "h"),
        (shaped((span, chans), f32), "h"),
        (shaped((span, chans), bf16), "h"),
        (shaped((span, chans), bf16), "h"),
        (shaped((span, chans), bf16), "h"),
        (shaped((span, width), f32), "h"),
    ]
    scratch = [
        pltpu.VMEM((states, step, chans), f32),
        pltpu.VMEM((states, far_steps // group, group, chans), f32),
        pltpu.VMEM((span, chans), f32),
        pltpu.VMEM((2 * span, chans), f32),
        pltpu.VMEM((2 * span, chans), f32),
        pltpu.VMEM((2 * span, chans), bf16),
    ]
    ins = [(length, "s"), (tokens, "h"), (gain, "v"), (bias, "v")]
    ins += [(weight, "h") for weight in weights]
    ins += [(taps, "v"), (coef_t, "v"), (rate_t, "v"), (skip, "v")]
    ins += [(out_weight, "l"), (table, "l"), (table_t, "l")]
    return staged(run, ins, outs, "mixer_forward", scratch)


def norm_sums(grad, value, start, gain_sum, bias_sum):
    rows = pl.ds(start, 128)
    scaled, _ = norm_rows(value[rows, :].astype(f32))
    part = grad[rows, :]
    return gain_sum + column_sum(part * scaled), bias_sum + column_sum(part)


def feed_prepare(length, cotangent, normed):
    span, width = cotangent.shape

    def run(len_ref, cot, normed_ref, down_o, down_t, normed_t, sums):
        size = len_ref[0]
        total = jnp.zeros((8, width), f32)
        for start in range(0, span, 256):
            rows = pl.ds(start, 256)
            grad = row_mask(start, 256, size) * cot.get()[rows, :].astype(f32)
            total = total + column_sum(grad)
            down_o.ref[rows, :] = grad.astype(bf16)
            down_o.put(start, 256)
            down_t.ref[:, rows] = grad.astype(bf16).T
        down_t.put()
        for start in range(0, span, 256):
            rows = pl.ds(start, 256)
            normed_t.ref[:, rows] = normed_ref.get()[rows, :].T
        normed_t.put()
        sums[...] = total

    outs = [
        (shaped((span, width), bf16), "h"),
        (shaped((width, span), bf16), "h"),
        (shaped((width, span), bf16), "h"),
        (shaped((8, width), f32), "v"),
    ]
    return staged(run, [(length, "s"), (cotangent, "h"), (normed, "h")], outs, "feed_prepare")


def feed_forward_back(place, tokens, mine, other, gain, bias, down, down_t, up_weight, up_bias, down_weight, cuts):
    span, width = tokens.shape
    hidden = up_weight.shape[1]
    groups, rows_each, _ = down_t.shape
    half = width // 2
    bits, widths, thirds = cuts
    size = hidden // 3
    parts = len(bits)
    step = 256

    def run(*refs):
        place_ref, tok, mine_ref, other_ref, gain_ref, bias_ref, dn, dn_t, up, upb, dw = refs[:11]
        resid_o, acts_o, part_o, sums, upb_sums = refs[11:16]
        gives, keeps = refs[16 : 16 + parts], refs[16 + parts : 16 + 2 * parts]
        second, second_t, grad_hid, hid_a, hid_b, pre_a, pre_b, hat, chosen_a, chosen_b = refs[16 + 2 * parts :]
        resid, acts = resid_o.ref, acts_o.ref
        cuts = span // step
        for k in range(cuts):
            for item in (tok, mine_ref, other_ref):
                item.start(k + 1)
        for item in (up, dw, dn, dn_t):
            item.start()
        for k in range(cuts):
            rows = pl.ds(k * step, step)
            value = tok.get(k)[rows, :].astype(f32) + (mine_ref.get(k)[rows, :] + other_ref.get(k)[rows, :])
            resid[rows, :] = value
            scaled, _ = norm_rows(value)
            hat[rows, :] = scaled
            norm = (scaled * gain_ref[...] + bias_ref[...]).astype(bf16)
            second[rows, :] = norm
            turned = norm.T
            for j in range(groups):
                second_t[j, :, rows] = turned[j * rows_each : (j + 1) * rows_each, :]
        up_ref, dw_ref, dn_ref = up.get(), dw.get(), dn.get()
        resid_o.put()
        slots = [(hid_a, pre_a), (hid_b, pre_b)]

        def rise(i, k):
            rows, cols = pl.ds(k * step, step), pl.ds(i * size, size)
            hid, pre = slots[k % 2]
            hid[...] = matmul(second[rows, :], up_ref[:, cols])
            pre[...] = times_transposed(dn_ref[rows, :], dw_ref[cols, :])

        def gelu(i, k):
            rows, cols = pl.ds(k * step, step), pl.ds(i * size, size)
            hid, pre = slots[k % 2]
            h = hid[...] + upb[:, cols]
            cdf = 0.5 + 0.5 * lax.erf(h * (1.0 / math.sqrt(2.0)))
            slope = cdf + h * jnp.exp(-0.5 * h * h) * (1.0 / math.sqrt(2.0 * math.pi))
            acts[rows, cols] = (h * cdf).astype(bf16)
            grad = (pre[...] * slope).astype(bf16)
            grad_hid[rows, cols] = grad
            return column_sum(grad.astype(f32))

        for i in range(3):
            total = jnp.zeros((8, size), f32)
            rise(i, 0)
            for k in range(cuts):
                if k + 1 < cuts:
                    rise(i, k + 1)
                total = total + gelu(i, k)
            upb_sums[:, pl.ds(i * size, size)] = total
            (down_part, down_at), (up_part, up_at) = thirds[i]
            for source, chosen, right, (which, at) in (
                (dn_t.get(), chosen_a, acts, (down_part, down_at)),
                (second_t, chosen_b, grad_hid, (up_part, up_at)),
            ):
                split_products(
                    place_ref, bits[which], source, chosen, [(right, i * size, size, at)], gives[which].ref, keeps[which].ref
                )
            for which in sorted({down_part, up_part}):
                gives[which].put()
                keeps[which].put()
            acts_o.put_columns(i * size, size)
        gain_sum = jnp.zeros((8, width), f32)
        bias_sum = jnp.zeros((8, width), f32)
        for k in range(cuts + 1):
            if k < cuts:
                rows = pl.ds(k * step, step)
                part_o.ref[rows, :] = times_transposed(grad_hid[rows, :], up_ref[...])
                part_o.put(k * step, step)
            if k:
                rows = pl.ds((k - 1) * step, step)
                part = part_o.ref[rows, :]
                gain_sum = gain_sum + column_sum(part * hat[rows, :])
                bias_sum = bias_sum + column_sum(part)
        sums[pl.ds(0, 8), :] = gain_sum
        sums[pl.ds(8, 8), :] = bias_sum

    outs = [
        (shaped((span, width), f32), "h"),
        (shaped((span, hidden), bf16), "h"),
        (shaped((span, width), f32), "h"),
        (shaped((16, width), f32), "v"),
        (shaped((8, hidden), f32), "v"),
    ]
    outs += [(shaped((half, w), f32), "h") for w in widths] * 2
    scratch = [
        pltpu.VMEM((span, width), bf16),
        pltpu.VMEM((groups, rows_each, span), bf16),
        pltpu.VMEM((span, hidden), bf16),
        pltpu.VMEM((step, size), f32),
        pltpu.VMEM((step, size), f32),
        pltpu.VMEM((step, size), f32),
        pltpu.VMEM((step, size), f32),
        pltpu.VMEM((span, width), f32),
        pltpu.VMEM((2, half, span), bf16),
        pltpu.VMEM((2, half, span), bf16),
    ]
    cut = span // step
    ins = [(place, "s"), (tokens, cut), (mine, cut), (other, cut), (gain, "v"), (bias, "v")]
    ins += [(down, "l"), (down_t, "l"), (up_weight, "l"), (up_bias, "v"), (down_weight, "l")]
    res = staged(run, ins, outs, "feed_forward_back", scratch)
    return res[:5], res[5 : 5 + parts], res[5 + parts :]


def mixer_back(
    length, place, down, mine, other, resid, feedgain, out_weight, mixed, query, sig16, ker16, table, table_t, skip,
    keypad, value, taps, normed_t, gated, weights, tokens, feed_sums, cuts,
):
    span, width = resid.shape
    chans = query.shape[1]
    groups, rows_each, _ = normed_t.shape
    half = width // 2
    block = table.shape[1]
    count = span // block
    lags = taps.shape[0]
    lanes = 128
    bits, pieces = cuts
    widths = [sum(n for _, _, n in part) for part in pieces]
    parts = len(bits)

    def run(*refs):
        len_ref, place_ref, dn, mine_ref, other_ref, resid_ref, gain_ref, wo, mixed_ref, query_ref = refs[:10]
        sig_ref, ker_ref, tab, tab_t, skip_ref, key, value_ref, taps_ref, norm_t, gated_ref = refs[10:20]
        wq, wk, wv, tok, feed_ref = refs[20:25]
        grad_resid_o, lag_o, part_o, skip_sums, taps_sums = refs[25:30]
        gives, keeps = refs[30 : 30 + parts], refs[30 + parts : 30 + 2 * parts]
        grad_mix, mix_t, mix_grad, bins, sigs, kers, back_prod, lag_prod, shifted_grad, shifted, grads, chosen, mix_sums, all_weights = refs[30 + 2 * parts :]
        size = len_ref[0]
        grad_resid = grad_resid_o.ref
        grad_query, grad_key, grad_value = [pl.ds(k * chans, chans) for k in range(3)]

        for item in (tab, sig_ref, ker_ref):
            item.start()
        for i in range(count):
            for item in (dn, mine_ref, other_ref, resid_ref):
                item.start(i + 1)
        before = None
        turn = 1.0 - 2.0 * (iota((2 * block, 1), 0) % 2).astype(f32)
        for i in range(count):
            rows, bin_rows = pl.ds(i * block, block), pl.ds(i * 2 * block, 2 * block)
            sigs[bin_rows, :] = matmul(tab.get()[...], sig_ref.get()[rows, :])
            ker = matmul(tab.get()[...], ker_ref.get()[rows, :])
            kers[bin_rows, :] = ker if before is None else ker + turn * before
            before = ker
        for i in range(count):
            rows = pl.ds(i * block, block)
            scaled, inverse = norm_rows(resid_ref.get(i)[rows, :])
            grad = norm_back(mine_ref.get(i)[rows, :] + other_ref.get(i)[rows, :], scaled, inverse, gain_ref[...])
            grad = dn.get(i)[rows, :].astype(f32) + grad
            if i == 0:
                for item in (wo, query_ref, mixed_ref, key, value_ref):
                    item.start()
            grad_resid[rows, :] = grad
            grad = grad.astype(bf16)
            grad_mix[rows, :] = grad
            turned = grad.T
            for j in range(groups):
                mix_t[j, :, rows] = turned[j * rows_each : (j + 1) * rows_each, :]
        keypad, val = key.get(), value_ref.get()
        for item in (tab_t, norm_t, gated_ref):
            item.start()
        total = jnp.zeros((8, chans), f32)
        for i in range(count):
            rows, bin_rows = pl.ds(i * block, block), pl.ds(i * 2 * block, 2 * block)
            mask = row_mask(i * block, block, size)
            grad_gated = mask * times_transposed(grad_mix[rows, :], wo.get()[...])
            grads[rows, grad_query] = (grad_gated * mixed_ref.get()[rows, :]).astype(bf16)
            grad = grad_gated * query_ref.get()[rows, :]
            mix_grad[rows, :] = grad
            moved = shift_conv(taps_ref, keypad, i * block, block)
            shifted[rows, :] = moved
            total = total + column_sum(grad * (mask * moved * val[rows, :]))
            bins[bin_rows, :] = matmul(tab.get()[...], grad.astype(bf16))
        skip_sums[...] = total
        grad_resid_o.put()
        for item in (wq, wk, wv, tok):
            item.start()

        def product(i, _):
            start = pl.multiple_of(i * 16, 16)
            row = iota((16, 1), 0) + start
            first = row == 0
            scale = jnp.where(first, 0.5 / block, 1.0 / block)
            sign = 1.0 - 2.0 * (row % 2).astype(f32)
            for lane in range(0, chans, lanes):
                cols = pl.ds(lane, lanes)

                def pair(ref, j):
                    return (
                        ref[pl.ds(j * 2 * block + start, 16), cols],
                        ref[pl.ds(j * 2 * block + block + start, 16), cols],
                    )

                def put(ref, j, real, imag):
                    ref[pl.ds(j * 2 * block + start, 16), cols] = (real * scale).astype(bf16)
                    ref[pl.ds(j * 2 * block + block + start, 16), cols] = (imag * scale).astype(bf16)

                grad_pairs = [pair(bins, j) for j in range(count)]

                def correlate(ref, pairs):
                    real = imag = None
                    for g, j in pairs:
                        a, b = grad_pairs[g]
                        c, d = pair(ref, j)
                        other, d = edge(first, c, d)
                        r = a * c + b * d
                        s = b * other - a * d
                        real = r if real is None else real + r
                        imag = s if imag is None else imag + s
                    return real, imag

                for j in range(count):
                    real, imag = correlate(kers, [(m, m - j) for m in range(j, count)])
                    put(back_prod, j, real, imag)
                later = None
                for j in reversed(range(count)):
                    real, imag = correlate(sigs, [(m + j, m) for m in range(count - j)])
                    if later is None:
                        put(lag_prod, j, real, imag)
                    else:
                        put(lag_prod, j, real + sign * later[0], imag + sign * later[1])
                    later = (real, imag)
            return 0

        lax.fori_loop(0, block // 16, product, 0)
        shifted_grad[pl.ds(span, pad), :] = jnp.zeros((pad, chans), f32)
        totals = [jnp.zeros((8, chans), f32)] * lags
        for i in range(count):
            rows = pl.ds(i * block, block)
            bin_rows = pl.ds(i * 2 * block, 2 * block)
            mask = row_mask(i * block, block, size)
            signal_grad = matmul(tab_t.get()[...], back_prod[bin_rows, :])
            lag_o.ref[rows, :] = matmul(tab_t.get()[...], lag_prod[bin_rows, :])
            signal_grad = mask * (signal_grad + skip_ref[...] * mix_grad[rows, :])
            grads[rows, grad_value] = (signal_grad * shifted[rows, :]).astype(bf16)
            shifted_grad[rows, :] = signal_grad * val[rows, :]
        lag_o.put()
        for i in range(count):
            rows = pl.ds(i * block, block)
            here = keypad[pl.ds(i * block + pad, block), :]
            grad = None
            for lag in range(lags):
                moved = shifted_grad[pl.ds(i * block + lag, block), :]
                totals[lag] = totals[lag] + column_sum(moved * here)
                term = taps_ref[lag : lag + 1, :] * moved
                grad = term if grad is None else grad + term
            grads[rows, grad_key] = grad.astype(bf16)
        for lag in range(lags):
            taps_sums[pl.ds(lag * 8, 8), :] = totals[lag]

        for i in range(parts):
            at, pairs = 0, ([], [])
            for which, start, n in pieces[i]:
                if which == 0:
                    pairs[0].append((gated_ref.get(), start, n, at))
                else:
                    pairs[1].append((grads, (which - 1) * chans + start, n, at))
                at += n
            for source, some in ((mix_t, pairs[0]), (norm_t.get(), pairs[1])):
                if some:
                    split_products(place_ref, bits[i], source, chosen, some, gives[i].ref, keeps[i].ref)
            gives[i].put()
            keeps[i].put()

        gain_sum = jnp.zeros((8, width), f32)
        bias_sum = jnp.zeros((8, width), f32)
        for k, w in enumerate((wq, wk, wv)):
            all_weights[:, pl.ds(k * chans, chans)] = w.get()[...]
        for i in range(count + 1):
            if i < count:
                rows = pl.ds(i * block, block)
                part_o.ref[rows, :] = times_transposed(grads[rows, :], all_weights[...])
                part_o.put(i * block, block)
            if i:
                rows = pl.ds((i - 1) * block, block)
                scaled, _ = norm_rows(tok.get()[rows, :].astype(f32))
                part = part_o.ref[rows, :]
                gain_sum = gain_sum + column_sum(part * scaled)
                bias_sum = bias_sum + column_sum(part)
        mix_sums[pl.ds(0, 8), :] = gain_sum
        mix_sums[pl.ds(8, 8), :] = bias_sum
        mix_sums[pl.ds(16, 16), :] = feed_ref[...]
        part_o.put(span, 32, mix_sums)

    outs = [
        (shaped((span, width), f32), "=5"),
        (shaped((span, chans), f32), "h"),
        (shaped((span + 32, width), f32), "=3"),
        (shaped((8, chans), f32), "v"),
        (shaped((8 * lags, chans), f32), "v"),
    ]
    outs += [(shaped((half, w), f32), "h") for w in widths] * 2
    scratch = [
        pltpu.VMEM((span, width), bf16),
        pltpu.VMEM((groups, rows_each, span), bf16),
        pltpu.VMEM((span, chans), f32),
        pltpu.VMEM((2 * span, chans), f32),
        pltpu.VMEM((2 * span, chans), f32),
        pltpu.VMEM((2 * span, chans), f32),
        pltpu.VMEM((2 * span, chans), bf16),
        pltpu.VMEM((2 * span, chans), bf16),
        pltpu.VMEM((span + pad, chans), f32),
        pltpu.VMEM((span, chans), f32),
        pltpu.VMEM((span, 3 * chans), bf16),
        pltpu.VMEM((2, half, span), bf16),
        pltpu.VMEM((32, width), f32),
        pltpu.VMEM((width, 3 * chans), bf16),
    ]
    ins = [(length, "s"), (place, "s"), (down, count), (mine, count), (other, count), (resid, count), (feedgain, "v")]
    ins += [(x, "l") for x in (out_weight, mixed, query, sig16, ker16, table, table_t)] + [(skip, "v")]
    ins += [(keypad, "l"), (value, "l"), (taps, "v"), (normed_t, "l"), (gated, "l")]
    ins += [(weight, "l") for weight in weights] + [(tokens, "l"), (feed_sums, "v")]
    res = staged(run, ins, outs, "mixer_back", scratch)
    return res[:5], res[5 : 5 + parts], res[5 + parts :]


def feed_down(acts, down_weight):
    span = acts.shape[0]
    width = down_weight.shape[1]

    def run(act, down, out):
        for start in range(0, span, 128):
            out.ref[pl.ds(start, 128), :] = matmul(act.get()[pl.ds(start, 128), :], down.get()[...])
            out.put(start, 128)

    outs = [(shaped((span, width), f32), "h")]
    return staged(run, [(acts, "h"), (down_weight, "h")], outs, "feed_down")[0]


def finish_tokens(tokens, grad_resid, mine, other, gain):
    span, width = tokens.shape
    cuts = 4
    step = span // cuts

    def run(tok, grad_ref, mine_ref, other_ref, gain_ref, out):
        items = (tok, mine_ref, other_ref, grad_ref)
        for k in range(cuts):
            for item in items:
                item.start(k + 1)
        for k in range(cuts):
            rows = pl.ds(k * step, step)
            scaled, inverse = norm_rows(tok.get(k)[rows, :].astype(f32))
            grad = mine_ref.get(k)[rows, :] + other_ref.get(k)[rows, :]
            out.ref[rows, :] = grad_ref.get(k)[rows, :] + norm_back(grad, scaled, inverse, gain_ref[...])
            out.put(k * step, step)

    ins = [(tokens, cuts), (grad_resid, cuts), (mine, ("top", cuts)), (other, ("top", cuts)), (gain, "v")]
    return staged(run, ins, [(shaped((span, width), f32), "h")], "finish_tokens")[0]


def finish_layer(length, resid, mine, other, bias):
    span, width = resid.shape
    cuts = 4
    step = span // cuts

    def run(len_ref, resid_ref, a, b, bias_ref, out):
        for k in range(cuts):
            for item in (resid_ref, a, b):
                item.start(k + 1)
        for k in range(cuts):
            rows = pl.ds(k * step, step)
            value = resid_ref.get(k)[rows, :] + ((a.get(k)[rows, :] + b.get(k)[rows, :]) + bias_ref[...])
            out.ref[rows, :] = (row_mask(k * step, step, len_ref[0]) * value).astype(bf16)
            out.put(k * step, step)

    ins = [(length, "s"), (resid, cuts), (mine, cuts), (other, cuts), (bias, "v")]
    return staged(run, ins, [(shaped((span, width), bf16), "h")], "finish_layer")[0]


def halve(place, keeps, gots, cuts, rows, widths, theirs, before=None):
    n, n_cuts, n_out = len(keeps), len(cuts), len(widths)
    half = keeps[0].shape[0] // 2
    runs = [1 << cut[3] for cut in cuts]
    copies_each = [half // rows // size for size in runs]

    def run(place_ref, *refs):
        keep_refs, got_refs = refs[:n], refs[n : 2 * n]
        refs = refs[2 * n + (0 if before is None else n_out) :]
        outs, refs = refs[:n_out], refs[n_out:]
        sums, adds, sems = refs[:n_cuts], refs[n_cuts : 2 * n_cuts], refs[2 * n_cuts]
        waits, at = [], 0
        for i, (which, start, count, pos, bit, _, _) in enumerate(cuts):
            mine = (place_ref[0] >> bit) & 1
            side = 1 - mine if theirs else mine
            cols = pl.ds(start, count)
            waits.append([])
            for j in range(copies_each[i]):
                first = insert_bit(j * runs[i], pos, side) * rows
                source = pl.ds(pl.multiple_of(first, rows), runs[i] * rows)
                target = pl.ds(j * runs[i] * rows, runs[i] * rows)
                for array, held in ((keep_refs[which], sums[i]), (got_refs[which], adds[i])):
                    copy = pltpu.make_async_copy(array.at[source, cols], held.at[target], sems.at[at])
                    copy.start()
                    waits[i].append(copy)
                    at += 1
        copies = []
        for i, (_, _, count, _, _, out, start) in enumerate(cuts):
            for copy in waits[i]:
                copy.wait()
            sums[i][...] = sums[i][...] + adds[i][...]
            copies.append(pltpu.make_async_copy(sums[i], outs[out].at[:, pl.ds(start, count)], sems.at[at]))
            copies[-1].start()
            at += 1
        for copy in copies:
            copy.wait()

    ins = [(place, "s")] + [(x, "a") for x in (*keeps, *gots)]
    aliases = None
    if before is not None:
        aliases = {len(ins) + k: k for k in range(n_out)}
        ins += [(item, "a") for item in before]
    outs = [(shaped((half, w), f32), "a") for w in widths]
    scratch = [pltpu.VMEM((half, cut[2]), f32) for cut in cuts] * 2
    scratch.append(pltpu.SemaphoreType.DMA((2 * sum(copies_each) + n_cuts,)))
    return staged(run, ins, outs, "halve", scratch, aliases)


def pack_small(coef, rate, taps, skip, upbias, downbias, norms, norms_other):
    states, chans = coef.shape
    lags = taps.shape[0] // 8
    wide = [(upbias, None), (downbias, None)]
    counts = [states, states, lags, 1, upbias.shape[1] // chans, downbias.shape[1] // chans]
    counts.append(4 * (norms.shape[1] // chans))
    total = -(-sum(counts) // 16) * 16

    def run(coef_ref, rate_ref, taps_ref, skip_ref, up_ref, down_ref, norm_a, norm_b, out):
        out[...] = jnp.zeros_like(out)
        out[pl.ds(0, states), :] = coef_ref[...]
        out[pl.ds(states, states), :] = rate_ref[...]
        at = 2 * states

        def lay(value, at):
            row = jnp.sum(value, 0, keepdims=True)
            for start in range(0, row.shape[1], chans):
                out[pl.ds(at, 1), :] = row[:, start : start + chans]
                at += 1
            return at

        for lag in range(lags):
            at = lay(taps_ref[pl.ds(8 * lag, 8), :], at)
        at = lay(skip_ref[...], at)
        at = lay(up_ref[...], at)
        at = lay(down_ref[...], at)
        for start in range(0, 32, 8):
            rows = pl.ds(start, 8)
            at = lay(norm_a[rows, :] + norm_b[rows, :], at)

    ins = [coef, rate, taps, skip, upbias, downbias, norms, norms_other]
    ins = [(x, "v") for x in ins[:6]] + [(x, "t") for x in ins[6:]]
    out = staged(run, ins, [(shaped((total, chans), f32), "v")], "pack_small")[0]
    return out, counts


def unpack_small(place, bit, mine, other, counts, lags, hidden, width):
    half, chans = mine.shape

    def run(place_ref, a, b, coef, rate, taps, skip, up, down, *rest):
        norms, whole = rest[:-1], rest[-1]
        side = (place_ref[0] >> bit) & 1
        whole[pl.ds(pl.multiple_of(side * half, 8), half), :] = a[...]
        whole[pl.ds(pl.multiple_of((1 - side) * half, 8), half), :] = b[...]
        at = 0
        for out in (coef, rate, taps):
            out[...] = whole[pl.ds(at, out.shape[0]), :]
            at += out.shape[0]
        for out in (skip, up, down, *norms):
            for start in range(0, out.shape[1], chans):
                out[:, pl.ds(start, chans)] = whole[pl.ds(at, 1), :]
                at += 1

    states = counts[0]
    outs = [(shaped((n, chans), f32), "v") for n in (states, states, lags)]
    outs += [(shaped((n,), f32), "v") for n in (chans, hidden, width, width, width, width, width)]
    ins = [(place, "s"), (mine, "v"), (other, "v")]
    return staged(run, ins, outs, "unpack_small", [pltpu.VMEM((2 * half, chans), f32)])


def collect(keeps, gots, layout, sizes):
    n = len(keeps)
    rows = keeps[0].shape[0]
    names = list(sizes)

    def run(*refs):
        outs = dict(zip(names, refs[2 * n :]))
        for i in range(n):
            total = refs[i][...] + refs[n + i][...]
            at = 0
            for name, start, count in layout[i]:
                piece = total[:, at : at + count]
                if sizes[name][1]:
                    outs[name][pl.ds(start, count), :] = piece.T
                else:
                    outs[name][:, pl.ds(start, count)] = piece
                at += count

    outs = []
    for columns, turned in sizes.values():
        outs.append((shaped((columns, rows) if turned else (rows, columns), f32), "v"))
    res = staged(run, [(x, "v") for x in (*keeps, *gots)], outs, "collect")
    return dict(zip(names, res))


def state_grads(coef_t, rate_t, lag_grad):
    states, chans = coef_t.shape
    span = lag_grad.shape[0]
    step = 32
    blocks = span // step
    lanes = 128
    group = 8
    tiles = step // 8

    def run(coef_ref, rate_ref, lag_ref, coef_out, rate_out, fine, coarse, plain, place, ramp):
        rate = rate_ref[...][:, None, :]
        within = lax.broadcasted_iota(jnp.int32, (1, step, 1), 1).astype(f32)
        across = lax.broadcasted_iota(jnp.int32, (1, blocks, 1), 1).astype(f32)
        fine[...] = jnp.exp(-rate * within)
        coarse[...] = jnp.exp(-rate * (step * across))
        plain[...] = jnp.zeros_like(plain)
        place[...] = jnp.zeros_like(place)
        ramp[...] = jnp.zeros_like(ramp)
        for base in range(0, blocks, group):
            lag = [
                [
                    lag_ref[pl.ds((base + j) * step + 8 * a, 8), :]
                    for a in range(tiles)
                ]
                for j in range(group)
            ]

            def add(n, _):
                near = [fine[n, pl.ds(8 * a, 8), :] for a in range(tiles)]
                suffix = None
                later = None
                tilted = None
                for j in reversed(range(group)):
                    far = coarse[n, pl.ds(base + j, 1), :]
                    total = None
                    slope = None
                    for a in reversed(range(tiles)):
                        term = lag[j][a] * near[a]
                        if total is None:
                            total = term
                        else:
                            slope = total if slope is None else slope + total
                            total = total + term
                    weighted = far * total
                    bent = far * slope
                    tilted = bent if tilted is None else tilted + bent
                    if suffix is None:
                        suffix = weighted
                    else:
                        later = suffix if later is None else later + suffix
                        suffix = suffix + weighted
                plain[n] = plain[n] + suffix
                place[n] = place[n] + (later + float(base) * suffix)
                ramp[n] = ramp[n] + tilted
                return 0

            lax.fori_loop(0, states, add, 0, unroll=4)
        rows = lax.broadcasted_iota(jnp.int32, (1, 8, 1), 1).astype(f32)
        whole = plain[...]
        coef_out[...] = jnp.sum(whole, 1)
        times = float(step) * place[...] + 8.0 * ramp[...] + rows * whole
        rate_out[...] = -coef_ref[...] * jnp.sum(times, 1)

    shape = jax.ShapeDtypeStruct((states, chans), f32)
    block = pl.BlockSpec((states, lanes), lambda i: (0, i))
    return pl.pallas_call(
        run,
        grid=(chans // lanes,),
        in_specs=[block, block, pl.BlockSpec((span, lanes), lambda i: (0, i))],
        out_specs=[block, block],
        out_shape=[shape, shape],
        scratch_shapes=[
            pltpu.VMEM((states, step, lanes), f32),
            pltpu.VMEM((states, blocks, lanes), f32),
        ]
        + [pltpu.VMEM((states, 8, lanes), f32)] * 3,
        compiler_params=pltpu.CompilerParams(vmem_limit_bytes=most_vmem),
        cost_estimate=small_cost,
        name="state_grads",
    )(coef_t, rate_t, lag_grad)


def follow(values, *before):
    held = lax.optimization_barrier((list(values), before))[0]
    return held


def take_columns(cols, start, count):
    taken = []
    for name, first, columns in cols:
        low, high = max(start, 0), min(start + count, columns)
        if low < high:
            taken.append((name, first + low, high - low))
        start -= columns
    return taken


def body(
    tokens,
    lengths,
    mixgain,
    mixbias,
    query_weight,
    key_weight,
    value_weight,
    shift_taps,
    state_coef,
    state_rate,
    state_skip,
    out_weight,
    feedgain,
    feedbias,
    up_weight,
    up_bias,
    down_weight,
    down_bias,
    cotangent,
):
    assert lengths.shape[0] == 1
    span, width = tokens.shape
    chans = query_weight.shape[1]
    hidden = up_weight.shape[1]
    lags = shift_taps.shape[0]
    places = lax.axis_size("freq")
    halving = places == 16 and width % (16 * places) == 0
    groups = places if halving else 2
    rows = width // groups
    place = lax.axis_index("freq").astype(jnp.int32).reshape(1)
    third, part = hidden // 3, chans // 3
    feed_cols = [[("down", i * third, third), ("up", i * third, third)] for i in range(3)]
    mixer_cols = [
        [("out", 0, 3 * part), ("query", 0, part)],
        [("query", part, 2 * part), ("key", 0, 2 * part)],
        [("key", 2 * part, part), ("value", 0, 3 * part)],
    ]
    order_of = {"out": 0, "query": 1, "key": 2, "value": 3}
    pieces = [[(order_of[n], s, c) for n, s, c in cols] for cols in mixer_cols]
    thirds = [((i, 0), (i, third)) for i in range(3)]
    if halving:
        orders = [[(0, 1, 2, 3), (0, 1, 3, 2)], [(1, 2, 0, 3), (1, 3, 0, 2)], [(2, 0, 1, 3)]]
        bits = [order[0][0] for order in orders]
    else:
        place = jnp.zeros_like(place)
        bits = [0] * 3

    block = 256
    table_np = dft_table(block)
    table, table_t = jnp.asarray(table_np), jnp.asarray(np.ascontiguousarray(table_np.T))
    coef_t, rate_t = state_coef.T, state_rate.T

    normed, query, keypad, value, mixed, gated, sig16, ker16, out_part = mixer_forward(
        lengths,
        tokens,
        mixgain,
        mixbias,
        (query_weight, key_weight, value_weight),
        shift_taps,
        coef_t,
        rate_t,
        state_skip,
        out_weight,
        table,
        table_t,
    )
    out_other = swap(out_part, "tp", 0)
    down, down_t, normed_t, downbias_part = feed_prepare(lengths, cotangent, normed)
    down_t = down_t.reshape(groups, rows, span)
    normed_t = normed_t.reshape(groups, rows, span)
    (resid, acts, second_part, feed_sums, upbias_part), gives, keeps = feed_forward_back(
        place, tokens, out_part, out_other, feedgain, feedbias, down, down_t, up_weight, up_bias, down_weight, (bits, [2 * third] * 3, thirds)
    )
    second_other = swap(second_part, "tp", 0)
    if halving:
        gots = [swap(give, "freq", bit) for give, bit in zip(gives, bits)]
    (grad_resid, lag_grad, normed_part, skip_part, taps_part), more_gives, more_keeps = mixer_back(
        lengths, place, down, second_part, second_other, resid, feedgain, out_weight, mixed, query, sig16, ker16, table, table_t, state_skip,
        keypad, value, shift_taps, normed_t, gated, (query_weight, key_weight, value_weight), tokens, feed_sums, (bits, pieces)
    )
    if halving:

        items = []
        for source, all_cols in enumerate((feed_cols, mixer_cols)):
            for cols, some in zip(all_cols, orders):
                size = sum(count for _, _, count in cols) // len(some)
                for k, order in enumerate(some):
                    items.append((order, take_columns(cols, k * size, size), source))

        def arrange(step, source=None):
            arrays, starts = {}, {}
            for item in items:
                if source is None or item[2] == source:
                    arrays.setdefault(item[0][step], []).append(item)
            for some in arrays.values():
                at = 0
                for item in some:
                    starts[id(item)] = at
                    at += width_of(item)
            links = sorted(arrays)
            return links, [sum(map(width_of, arrays[link])) for link in links], arrays, starts

        def width_of(item):
            return sum(count for _, _, count in item[1])

        def cuts_to(step, source=None):
            links, _, _, starts = arrange(step - 1, source)
            next_links, widths, _, next_starts = arrange(step)
            cuts = []
            for item in items:
                if source is None or item[2] == source:
                    order = item[0]
                    pos = sorted(order[step:]).index(order[step])
                    cuts.append(
                        (
                            links.index(order[step - 1]),
                            starts[id(item)],
                            width_of(item),
                            pos,
                            order[step],
                            next_links.index(order[step]),
                            next_starts[id(item)],
                        )
                    )
            return cuts, rows, widths

        def exchange(gives, step):
            return [swap(give, "freq", link) for give, link in zip(gives, arrange(step)[0])]

        def add_swapped(value, bit):
            return value + swap(value, "freq", bit)

        gots = follow(gots, *more_gives)
        more_gives, lag_grad, normed_part = follow([more_gives, lag_grad, normed_part], *gots)
        more_gots = exchange(more_gives, 0)
        held_gives = halve(place, keeps, gots, *cuts_to(1, 0), True)
        held_keeps = halve(place, keeps, gots, *cuts_to(1, 0), False)
        (acts,) = follow([acts], held_keeps[0], held_gives[0])
    normed_other = swap(normed_part, "tp", 0)
    down_part = feed_down(acts, down_weight)
    if halving:
        more_gots = follow(more_gots, down_part, normed_other)
        gives = halve(place, more_keeps, more_gots, *cuts_to(1, 1), True, held_gives)
        gots = exchange(gives, 1)
        down_part, lag_grad, more_gots[0] = follow([down_part, lag_grad, more_gots[0]], *gives)
        keeps = halve(place, more_keeps, more_gots, *cuts_to(1, 1), False, held_keeps)
        (lag_grad,) = follow([lag_grad], *keeps)
    down_other = swap(down_part, "tp", 0)
    coef_part, rate_part = state_grads(coef_t, rate_t, lag_grad)
    small, counts = pack_small(
        coef_part, rate_part, taps_part, skip_part, upbias_part, downbias_part, normed_part, normed_other
    )
    if halving:
        old = follow(gots, down_other, small)
        gives = halve(place, keeps, old, *cuts_to(2), True)
        (small,) = follow([small], *gives)
        gots = exchange(gives, 2)
        half = small.shape[0] // 2
        side = place[0] & 1
        give = lax.dynamic_slice_in_dim(small, (1 - side) * half, half, 0)
        small = lax.dynamic_slice_in_dim(small, side * half, half, 0)
        small = small + swap(give, "freq", 0)
        other = swap(small, "freq", 2)
        (down_part,) = follow([down_part], small)
        layer_out = finish_layer(lengths, resid, down_part, down_other, down_bias)
        (other,) = follow([other], layer_out)
        small = small + other
        other = swap(small, "freq", 3)
        (old[0],) = follow([old[0]], small)
        keeps = halve(place, keeps, old, *cuts_to(2), False)
        (other,) = follow([other], *keeps)
        small = small + other
        old = follow(gots, small, *keeps)
        gives = halve(place, keeps, old, *cuts_to(3), True)
        (small,) = follow([small], *gives)
        gots = exchange(gives, 3)
        other = swap(small, "freq", 1)
        (old[0],) = follow([old[0]], *gives)
        keeps = halve(place, keeps, old, *cuts_to(3), False)
        (other,) = follow([other], *keeps)
        small = small + other
        other = swap(small, "freq", 0)
        (normed_part,) = follow([normed_part], small)
        tokens_grad = finish_tokens(tokens, grad_resid, normed_part, normed_other, mixgain)
        (other,) = follow([other], tokens_grad)
        coef_sum, rate_sum, taps_sum, skip_sum, upbias_sum, downbias_sum, *norms = unpack_small(
            place, 0, small, other, counts, lags, hidden, width
        )
        gots = follow(gots, coef_sum)
        sizes = {"down": (hidden, False), "up": (hidden, False), "out": (chans, False)}
        sizes |= {name: (chans, False) for name in ("query", "key", "value")}
        links, _, arrays, _ = arrange(3)
        grads = collect(keeps, gots, [sum((item[1] for item in arrays[link]), []) for link in links], sizes)
    else:
        tokens_grad = finish_tokens(tokens, grad_resid, normed_part, normed_other, mixgain)
        layer_out = finish_layer(lengths, resid, down_part, down_other, down_bias)
        small = lax.psum(small, "freq")
        grads = {name: [] for name in ("down", "up", "out", "query", "key", "value")}
        for i in range(3):
            whole = jnp.concatenate(
                [
                    jnp.concatenate([keeps[i], more_keeps[i]], 1),
                    jnp.concatenate([gives[i], more_gives[i]], 1),
                ],
                0,
            )
            total = lax.psum_scatter(whole, "freq", scatter_dimension=0, tiled=True)
            at = 0
            for name, _, columns in feed_cols[i] + mixer_cols[i]:
                grads[name].append(total[:, at : at + columns])
                at += columns
        grads = {name: jnp.concatenate(some, 1) for name, some in grads.items()}
        cuts = np.cumsum(counts)
        coef_sum, rate_sum, taps_sum, skip_sum, upbias_sum, downbias_sum, norms, _ = jnp.split(small, cuts)
        norms = norms.reshape(4, width)
        skip_sum, upbias_sum, downbias_sum = [x.reshape(-1) for x in (skip_sum, upbias_sum, downbias_sum)]
    return (
        layer_out,
        tokens_grad,
        norms[0],
        norms[1],
        grads["query"],
        grads["key"],
        grads["value"],
        taps_sum,
        coef_sum.T,
        rate_sum.T,
        skip_sum,
        grads["out"].T,
        norms[2],
        norms[3],
        grads["up"],
        upbias_sum,
        grads["down"].T,
        downbias_sum,
    )


def solution(mesh):
    in_specs = (
        P("freq", None),
        P("freq"),
        P(),
        P(),
        P(None, "tp"),
        P(None, "tp"),
        P(None, "tp"),
        P(None, "tp"),
        P("tp", None),
        P("tp", None),
        P("tp"),
        P("tp", None),
        P(),
        P(),
        P(None, "tp"),
        P("tp"),
        P("tp", None),
        P(),
        P("freq", None),
    )
    out_specs = (
        P("freq", None),
        P("freq", None),
        P(),
        P(),
        P("freq", "tp"),
        P("freq", "tp"),
        P("freq", "tp"),
        P(None, "tp"),
        P("tp", None),
        P("tp", None),
        P("tp"),
        P("tp", "freq"),
        P(),
        P(),
        P("freq", "tp"),
        P("tp"),
        P("tp", "freq"),
        P(),
    )
    return jax.shard_map(body, mesh=mesh, in_specs=in_specs, out_specs=out_specs, check_vma=False)
```

```python
import math

import jax
import jax.numpy as jnp
import numpy as np
from jax import lax
from jax.experimental import pallas as pl
from jax.experimental.pallas import tpu as pltpu
from jax.sharding import PartitionSpec as P

f32 = jnp.float32
bf16 = jnp.bfloat16
in_vmem = pl.BlockSpec(memory_space=pltpu.VMEM)
in_smem = pl.BlockSpec(memory_space=pltpu.SMEM)
anywhere = pl.BlockSpec(memory_space=pl.ANY)
pad = 8
most_vmem = (64 << 20) - (128 << 10)
small_cost = pl.CostEstimate(flops=1, bytes_accessed=1, transcendentals=0)


def shaped(shape, dtype):
    return jax.ShapeDtypeStruct(shape, dtype)


def size_of(item):
    return math.prod(item.shape) * jnp.dtype(item.dtype).itemsize


def call(run, ins, outs, name, scratch=(), flops=0, moved=0, specs=None):
    held = sum(size_of(item) for item in (*ins, *outs, *scratch))
    return pl.pallas_call(
        run,
        in_specs=specs or [in_vmem] * len(ins),
        out_specs=[in_vmem] * len(outs),
        out_shape=outs,
        scratch_shapes=list(scratch),
        compiler_params=pltpu.CompilerParams(vmem_limit_bytes=held + (6 << 20)),
        cost_estimate=small_cost,
        name=name,
    )(*ins)


def matmul(left, right):
    return jnp.dot(left, right, preferred_element_type=f32)


def times_transposed(left, right):
    return lax.dot_general(left, right, (((1,), (1,)), ((), ())), preferred_element_type=f32)


def swap(value, axis, bit):
    size = lax.axis_size(axis)
    return lax.ppermute(value, axis, [(i, i ^ (1 << bit)) for i in range(size)])


def dft_table(block):
    bins = np.arange(block)[:, None].astype(np.int64)
    times = np.arange(block)[None, :].astype(np.int64)
    angle = (bins * times % (2 * block)) * (math.pi / block)
    table = np.concatenate([np.cos(angle), np.sin(angle)], 0)
    table[block] = 1 - 2 * (np.arange(block) % 2)
    return table.astype(jnp.bfloat16)


def iota(shape, dim):
    return lax.broadcasted_iota(jnp.int32, shape, dim)


def row_mask(first, count, length):
    return (iota((count, 1), 0) + first < length).astype(f32)


def insert_bit(index, pos, bit):
    low = index & ((1 << pos) - 1)
    return ((index >> pos) << (pos + 1)) | (bit << pos) | low


def norm_rows(value):
    mean = jnp.mean(value, -1, keepdims=True)
    centered = value - mean
    inverse = lax.rsqrt(jnp.mean(centered * centered, -1, keepdims=True) + 1e-05)
    return centered * inverse, inverse


def norm_back(grad_out, scaled, inverse, gain):
    weighted = grad_out * gain
    return inverse * (
        weighted
        - jnp.mean(weighted, -1, keepdims=True)
        - scaled * jnp.mean(weighted * scaled, -1, keepdims=True)
    )


def column_sum(value):
    rows, width = value.shape
    return jnp.sum(value.reshape(rows // 8, 8, width), 0)


def shift_conv(taps, keypad, start, count):
    lags = taps.shape[0]
    return sum(
        taps[lag : lag + 1, :] * keypad[pl.ds(start + pad - lag, count), :] for lag in range(lags)
    )


def edge(first, real, imag):
    return jnp.where(first, imag, real), jnp.where(first, 0.0, imag)


class Coming:
    def __init__(self, source, held, sems, cuts=1):
        self.held, self.started, self.here = held, 0, 0
        if source.shape[-2:] != held.shape[-2:] and len(source.shape) > 1 and cuts == 1:
            last = pl.ds(source.shape[0] - held.shape[0], held.shape[0])
            self.copies = [pltpu.make_async_copy(source.at[last], held, sems.at[0])]
            return
        if len(source.shape) == 1:
            self.copies = [pltpu.make_async_copy(source, held.at[0], sems.at[0])]
            return
        rows = held.shape[0] // cuts
        self.copies = []
        for i in range(cuts):
            part = pl.ds(i * rows, rows) if cuts > 1 else pl.ds(0, held.shape[0])
            self.copies.append(pltpu.make_async_copy(source.at[part], held.at[part], sems.at[i]))

    def start(self, cuts=None):
        cuts = len(self.copies) if cuts is None else cuts
        while self.started < cuts:
            self.copies[self.started].start()
            self.started += 1

    def get(self, cut=None):
        self.start(None if cut is None else cut + 1)
        until = len(self.copies) if cut is None else cut + 1
        while self.here < until:
            self.copies[self.here].wait()
            self.here += 1
        return self.held


class Going:
    def __init__(self, target, held, sems):
        self.target, self.ref, self.sems, self.copies = target, held, sems, []

    def put(self, start=0, count=None, source=None):
        rows = pl.ds(start, self.ref.shape[0] if count is None else count)
        sem = self.sems.at[len(self.copies)]
        if len(self.target.shape) == 1:
            copy = pltpu.make_async_copy(self.ref.at[0], self.target, sem)
        else:
            source = self.ref.at[rows] if source is None else source
            copy = pltpu.make_async_copy(source, self.target.at[rows], sem)
        copy.start()
        self.copies.append(copy)


    def put_columns(self, start, count):
        cols = pl.ds(start, count)
        sem = self.sems.at[len(self.copies)]
        copy = pltpu.make_async_copy(self.ref.at[:, cols], self.target.at[:, cols], sem)
        copy.start()
        self.copies.append(copy)


most_puts = 16
most_cuts = 4
in_hbm = pl.BlockSpec(memory_space=pl.ANY)


def staged(run, ins, outs, name, scratch=(), aliases=None):
    spec = {"s": in_smem}
    plain = ("s", "a")
    shared = lambda kind: isinstance(kind, str) and kind[0] == "="
    top = lambda kind: isinstance(kind, tuple)

    def tail(x, kind):
        if kind == "t" or top(kind):
            return shaped((32 if kind == "t" else x.shape[0] - 32, x.shape[1]), x.dtype)
        return x

    held = [tail(x, kind) for x, kind in (*ins, *outs) if kind not in plain and not shared(kind)]
    held = [shaped(x.shape if len(x.shape) > 1 else (1, *x.shape), x.dtype) for x in held]
    n_in = sum(kind not in plain for _, kind in ins)
    n_out = sum(kind not in plain for _, kind in outs)

    def whole(*refs):
        refs = list(refs)
        given, made = refs[: len(ins)], refs[len(ins) : len(ins) + len(outs)]
        rest = refs[len(ins) + len(outs) :]
        own, bufs = rest[: len(scratch)], rest[len(scratch) :]
        in_sems, out_sems = bufs[-2:]
        bufs = list(bufs[:-2])
        views, at = [], 0
        for ref, (_, kind) in zip(given, ins):
            if kind not in plain:
                cuts = kind[1] if top(kind) else kind if isinstance(kind, int) else 1
                views.append(Coming(ref, bufs.pop(0), in_sems.at[at], cuts))
                at += 1
                if kind != "l" and cuts == 1:
                    views[-1].start()
            else:
                views.append(ref)
        going, at = [], 0
        for ref, (_, kind) in zip(made, outs):
            if kind not in plain:
                held_at = views[int(kind[1:])].held if shared(kind) else bufs.pop(0)
                going.append(Going(ref, held_at, out_sems.at[at]))
                at += 1
            else:
                going.append(ref)
        for view, (_, kind) in zip(views, ins):
            if kind in ("v", "t"):
                view.get()
        views = [view.held if kind in ("v", "t") else view for view, (_, kind) in zip(views, ins)]
        small = [item for item, (_, kind) in zip(going, outs) if kind == "v"]
        run(*views, *[item.ref if item in small else item for item in going], *own)
        for item in small:
            item.put()
        for view in views:
            if isinstance(view, Coming):
                view.get()
        for item in going:
            if isinstance(item, Going):
                for copy in item.copies:
                    copy.wait()

    return pl.pallas_call(
        whole,
        in_specs=[spec.get(kind, in_hbm) for _, kind in ins],
        out_specs=[spec.get(kind, in_hbm) for _, kind in outs],
        out_shape=[item for item, _ in outs],
        scratch_shapes=list(scratch)
        + [pltpu.VMEM(x.shape, x.dtype) for x in held]
        + [
            pltpu.SemaphoreType.DMA((max(n_in, 1), most_cuts)),
            pltpu.SemaphoreType.DMA((max(n_out, 1), most_puts)),
        ],
        input_output_aliases=aliases or {},
        compiler_params=pltpu.CompilerParams(vmem_limit_bytes=most_vmem),
        cost_estimate=small_cost,
        name=name,
    )(*[x for x, _ in ins])


def split_products(place_ref, bit, source, chosen, pairs, give, keep):
    groups, rows, _ = source.shape
    mine = (place_ref[0] >> bit) & 1
    for k, (out, side) in enumerate(((give, 1 - mine), (keep, mine))):
        for j in range(groups // 2):
            chosen[k, pl.ds(j * rows, rows), :] = source[insert_bit(j, bit, side)]
    for k, out in enumerate((give, keep)):
        for right, start, count, to in pairs:
            out[:, pl.ds(to, count)] = matmul(chosen[k], right[:, pl.ds(start, count)])


def mixer_forward(length, tokens, gain, bias, weights, taps, coef_t, rate_t, skip, out_weight, table, table_t):
    span, width = tokens.shape
    chans = out_weight.shape[0]
    states = coef_t.shape[0]
    block = table.shape[1]
    count = span // block
    step = 32
    far_steps = span // step
    group = 8
    lanes = 128

    def run(
        len_ref, tok, gain_ref, bias_ref, wq, wk, wv, taps_ref, coef_ref, rate_ref, skip_ref, wo, tab, tab_t,
        normed_o, query_o, keypad_o, value_o, mixed_o, gated_o, sig_o, ker_o, part_o,
        fine, coarse, signal, sig_bins, ker_bins, prod,
    ):
        size = len_ref[0]
        normed, query, keypad, value = normed_o.ref, query_o.ref, keypad_o.ref, value_o.ref
        sig16, ker16 = sig_o.ref, ker_o.ref

        within = iota((1, step, 1), 1).astype(f32)
        across = iota((1, group, 1), 1).astype(f32) * float(step)
        rate = rate_ref[...][:, None, :]
        fine[...] = jnp.exp(-rate * within)
        for k in range(far_steps // group):
            coarse[:, k] = coef_ref[...][:, None, :] * jnp.exp(-rate * (across + float(step * group * k)))
        keypad[pl.ds(0, pad), :] = jnp.zeros((pad, chans), f32)
        tok_ref, wq_ref, wk_ref, wv_ref = tok.get(), wq.get(), wk.get(), wv.get()
        for item in (wo, tab, tab_t):
            item.start()

        sign = 1.0 - 2.0 * (iota((2 * block, 1), 0) % 2).astype(f32)
        before = None
        for i in range(count):
            start = i * block
            rows = pl.ds(start, block)
            key_rows = pl.ds(start + pad, block)
            scaled, _ = norm_rows(tok_ref[rows, :].astype(f32))
            norm = (scaled * gain_ref[...] + bias_ref[...]).astype(bf16)
            normed[rows, :] = norm
            products = [(query, rows, wq_ref), (keypad, key_rows, wk_ref), (value, rows, wv_ref)]
            for lane in range(0, chans, lanes):
                if products:
                    out, place, weight = products.pop(0)
                    out[place, :] = matmul(norm, weight[...])
                cols = pl.ds(lane, lanes)
                sums = [None] * group
                for n in range(states):
                    near = fine[n, :, cols]
                    for j in range(group):
                        term = coarse[n, i, pl.ds(j, 1), cols] * near
                        sums[j] = term if n == 0 else sums[j] + term
                for j in range(group):
                    ker16[pl.ds(start + j * step, step), cols] = sums[j].astype(bf16)
        for i in range(count):
            start = i * block
            rows, bins = pl.ds(start, block), pl.ds(2 * start, 2 * block)
            shifted = shift_conv(taps_ref, keypad, start, block)
            sig = row_mask(start, block, size) * shifted * value[rows, :]
            signal[rows, :] = sig
            sig16[rows, :] = sig.astype(bf16)
            sig_bins[bins, :] = matmul(tab.get()[...], sig16[rows, :])
            ker = matmul(tab.get()[...], ker16[rows, :])
            ker_bins[bins, :] = ker if before is None else ker + sign * before
            before = ker
        for item in (normed_o, query_o, value_o, sig_o, ker_o, keypad_o):
            item.put()

        def product(i, _):
            start = pl.multiple_of(i * 16, 16)
            first = (iota((16, 1), 0) + start) == 0
            scale = jnp.where(first, 0.5 / block, 1.0 / block)
            for lane in range(0, chans, lanes):
                cols = pl.ds(lane, lanes)

                def pair(ref, j):
                    return (
                        ref[pl.ds(j * 2 * block + start, 16), cols],
                        ref[pl.ds(j * 2 * block + block + start, 16), cols],
                    )

                sigs = [pair(sig_bins, j) for j in range(count)]
                kers = []
                for j in range(count):
                    c, d = pair(ker_bins, j)
                    other, d = edge(first, c, d)
                    kers.append((c, other, d))
                for j in range(count):
                    real = imag = None
                    for m in range(j + 1):
                        a, b = sigs[m]
                        c, other, d = kers[j - m]
                        r = a * c - b * d
                        s = a * d + b * other
                        real = r if real is None else real + r
                        imag = s if imag is None else imag + s
                    prod[pl.ds(j * 2 * block + start, 16), cols] = (real * scale).astype(bf16)
                    prod[pl.ds(j * 2 * block + block + start, 16), cols] = (imag * scale).astype(bf16)
            return 0

        lax.fori_loop(0, block // 16, product, 0, unroll=2)
        for i in range(count):
            rows = pl.ds(i * block, block)
            conv = matmul(tab_t.get()[...], prod[pl.ds(i * 2 * block, 2 * block), :])
            mixed = conv + skip_ref[...] * signal[rows, :]
            mixed_o.ref[rows, :] = mixed
            gated = (row_mask(i * block, block, size) * query[rows, :] * mixed).astype(bf16)
            gated_o.ref[rows, :] = gated
            part_o.ref[rows, :] = matmul(gated, wo.get()[...]) + 0.5 * tok_ref[rows, :].astype(f32)
            for item in (part_o, mixed_o, gated_o):
                item.put(i * block, block)

    outs = [
        (shaped((span, width), bf16), "h"),
        (shaped((span, chans), f32), "h"),
        (shaped((span + pad, chans), f32), "h"),
        (shaped((span, chans), f32), "h"),
        (shaped((span, chans), f32), "h"),
        (shaped((span, chans), bf16), "h"),
        (shaped((span, chans), bf16), "h"),
        (shaped((span, chans), bf16), "h"),
        (shaped((span, width), f32), "h"),
    ]
    scratch = [
        pltpu.VMEM((states, step, chans), f32),
        pltpu.VMEM((states, far_steps // group, group, chans), f32),
        pltpu.VMEM((span, chans), f32),
        pltpu.VMEM((2 * span, chans), f32),
        pltpu.VMEM((2 * span, chans), f32),
        pltpu.VMEM((2 * span, chans), bf16),
    ]
    ins = [(length, "s"), (tokens, "h"), (gain, "v"), (bias, "v")]
    ins += [(weight, "h") for weight in weights]
    ins += [(taps, "v"), (coef_t, "v"), (rate_t, "v"), (skip, "v")]
    ins += [(out_weight, "l"), (table, "l"), (table_t, "l")]
    return staged(run, ins, outs, "mixer_forward", scratch)


def norm_sums(grad, value, start, gain_sum, bias_sum):
    rows = pl.ds(start, 128)
    scaled, _ = norm_rows(value[rows, :].astype(f32))
    part = grad[rows, :]
    return gain_sum + column_sum(part * scaled), bias_sum + column_sum(part)


def feed_prepare(length, cotangent, normed):
    span, width = cotangent.shape

    def run(len_ref, cot, normed_ref, down_o, down_t, normed_t, sums):
        size = len_ref[0]
        total = jnp.zeros((8, width), f32)
        for start in range(0, span, 256):
            rows = pl.ds(start, 256)
            grad = row_mask(start, 256, size) * cot.get()[rows, :].astype(f32)
            total = total + column_sum(grad)
            down_o.ref[rows, :] = grad.astype(bf16)
            down_o.put(start, 256)
            down_t.ref[:, rows] = grad.astype(bf16).T
        down_t.put()
        for start in range(0, span, 256):
            rows = pl.ds(start, 256)
            normed_t.ref[:, rows] = normed_ref.get()[rows, :].T
        normed_t.put()
        sums[...] = total

    outs = [
        (shaped((span, width), bf16), "h"),
        (shaped((width, span), bf16), "h"),
        (shaped((width, span), bf16), "h"),
        (shaped((8, width), f32), "v"),
    ]
    return staged(run, [(length, "s"), (cotangent, "h"), (normed, "h")], outs, "feed_prepare")


def feed_forward_back(place, mine, other, gain, bias, down, down_t, up_weight, up_bias, down_weight, cuts):
    span, width = mine.shape
    hidden = up_weight.shape[1]
    groups, rows_each, _ = down_t.shape
    half = width // 2
    bits, widths, thirds = cuts
    size = hidden // 3
    parts = len(bits)
    step = 256

    def run(*refs):
        place_ref, mine_ref, other_ref, gain_ref, bias_ref, dn, dn_t, up, upb, dw = refs[:10]
        resid_o, acts_o, part_o, sums, upb_sums = refs[10:15]
        gives, keeps = refs[15 : 15 + parts], refs[15 + parts : 15 + 2 * parts]
        second, second_t, grad_hid, hid_a, hid_b, pre_a, pre_b, hat, chosen_a, chosen_b = refs[15 + 2 * parts :]
        resid, acts = resid_o.ref, acts_o.ref
        cuts = span // step
        for k in range(cuts):
            for item in (mine_ref, other_ref):
                item.start(k + 1)
        for item in (up, dw, dn, dn_t):
            item.start()
        for k in range(cuts):
            rows = pl.ds(k * step, step)
            value = mine_ref.get(k)[rows, :] + other_ref.get(k)[rows, :]
            resid[rows, :] = value
            scaled, _ = norm_rows(value)
            hat[rows, :] = scaled
            norm = (scaled * gain_ref[...] + bias_ref[...]).astype(bf16)
            second[rows, :] = norm
            turned = norm.T
            for j in range(groups):
                second_t[j, :, rows] = turned[j * rows_each : (j + 1) * rows_each, :]
        up_ref, dw_ref, dn_ref = up.get(), dw.get(), dn.get()
        resid_o.put()
        slots = [(hid_a, pre_a), (hid_b, pre_b)]

        def rise(i, k):
            rows, cols = pl.ds(k * step, step), pl.ds(i * size, size)
            hid, pre = slots[k % 2]
            hid[...] = matmul(second[rows, :], up_ref[:, cols])
            pre[...] = times_transposed(dn_ref[rows, :], dw_ref[cols, :])

        def gelu(i, k):
            rows, cols = pl.ds(k * step, step), pl.ds(i * size, size)
            hid, pre = slots[k % 2]
            h = hid[...] + upb[:, cols]
            cdf = 0.5 + 0.5 * lax.erf(h * (1.0 / math.sqrt(2.0)))
            slope = cdf + h * jnp.exp(-0.5 * h * h) * (1.0 / math.sqrt(2.0 * math.pi))
            acts[rows, cols] = (h * cdf).astype(bf16)
            grad = (pre[...] * slope).astype(bf16)
            grad_hid[rows, cols] = grad
            return column_sum(grad.astype(f32))

        for i in range(3):
            total = jnp.zeros((8, size), f32)
            rise(i, 0)
            for k in range(cuts):
                if k + 1 < cuts:
                    rise(i, k + 1)
                total = total + gelu(i, k)
            upb_sums[:, pl.ds(i * size, size)] = total
            (down_part, down_at), (up_part, up_at) = thirds[i]
            for source, chosen, right, (which, at) in (
                (dn_t.get(), chosen_a, acts, (down_part, down_at)),
                (second_t, chosen_b, grad_hid, (up_part, up_at)),
            ):
                split_products(
                    place_ref, bits[which], source, chosen, [(right, i * size, size, at)], gives[which].ref, keeps[which].ref
                )
            for which in sorted({down_part, up_part}):
                gives[which].put()
                keeps[which].put()
            acts_o.put_columns(i * size, size)
        gain_sum = jnp.zeros((8, width), f32)
        bias_sum = jnp.zeros((8, width), f32)
        for k in range(cuts + 1):
            if k < cuts:
                rows = pl.ds(k * step, step)
                part_o.ref[rows, :] = times_transposed(grad_hid[rows, :], up_ref[...])
                part_o.put(k * step, step)
            if k:
                rows = pl.ds((k - 1) * step, step)
                part = part_o.ref[rows, :]
                gain_sum = gain_sum + column_sum(part * hat[rows, :])
                bias_sum = bias_sum + column_sum(part)
        sums[pl.ds(0, 8), :] = gain_sum
        sums[pl.ds(8, 8), :] = bias_sum

    outs = [
        (shaped((span, width), f32), "h"),
        (shaped((span, hidden), bf16), "h"),
        (shaped((span, width), f32), "h"),
        (shaped((16, width), f32), "v"),
        (shaped((8, hidden), f32), "v"),
    ]
    outs += [(shaped((half, w), f32), "h") for w in widths] * 2
    scratch = [
        pltpu.VMEM((span, width), bf16),
        pltpu.VMEM((groups, rows_each, span), bf16),
        pltpu.VMEM((span, hidden), bf16),
        pltpu.VMEM((step, size), f32),
        pltpu.VMEM((step, size), f32),
        pltpu.VMEM((step, size), f32),
        pltpu.VMEM((step, size), f32),
        pltpu.VMEM((span, width), f32),
        pltpu.VMEM((2, half, span), bf16),
        pltpu.VMEM((2, half, span), bf16),
    ]
    cut = span // step
    ins = [(place, "s"), (mine, cut), (other, cut), (gain, "v"), (bias, "v")]
    ins += [(down, "l"), (down_t, "l"), (up_weight, "l"), (up_bias, "v"), (down_weight, "l")]
    res = staged(run, ins, outs, "feed_forward_back", scratch)
    return res[:5], res[5 : 5 + parts], res[5 + parts :]


def mixer_back(
    length, place, down, mine, other, resid, feedgain, out_weight, mixed, query, sig16, ker16, table, table_t, skip,
    keypad, value, taps, normed_t, gated, weights, tokens, feed_sums, cuts,
):
    span, width = resid.shape
    chans = query.shape[1]
    groups, rows_each, _ = normed_t.shape
    half = width // 2
    block = table.shape[1]
    count = span // block
    lags = taps.shape[0]
    lanes = 128
    bits, pieces = cuts
    widths = [sum(n for _, _, n in part) for part in pieces]
    parts = len(bits)

    def run(*refs):
        len_ref, place_ref, dn, mine_ref, other_ref, resid_ref, gain_ref, wo, mixed_ref, query_ref = refs[:10]
        sig_ref, ker_ref, tab, tab_t, skip_ref, key, value_ref, taps_ref, norm_t, gated_ref = refs[10:20]
        wq, wk, wv, tok, feed_ref = refs[20:25]
        grad_resid_o, lag_o, part_o, skip_sums, taps_sums = refs[25:30]
        gives, keeps = refs[30 : 30 + parts], refs[30 + parts : 30 + 2 * parts]
        grad_mix, mix_t, mix_grad, bins, sigs, kers, back_prod, lag_prod, shifted_grad, shifted, grads, chosen, mix_sums, all_weights = refs[30 + 2 * parts :]
        size = len_ref[0]
        grad_resid = grad_resid_o.ref
        grad_query, grad_key, grad_value = [pl.ds(k * chans, chans) for k in range(3)]

        for item in (tab, sig_ref, ker_ref):
            item.start()
        for i in range(count):
            for item in (dn, mine_ref, other_ref, resid_ref):
                item.start(i + 1)
        before = None
        turn = 1.0 - 2.0 * (iota((2 * block, 1), 0) % 2).astype(f32)
        for i in range(count):
            rows, bin_rows = pl.ds(i * block, block), pl.ds(i * 2 * block, 2 * block)
            sigs[bin_rows, :] = matmul(tab.get()[...], sig_ref.get()[rows, :])
            ker = matmul(tab.get()[...], ker_ref.get()[rows, :])
            kers[bin_rows, :] = ker if before is None else ker + turn * before
            before = ker
        for i in range(count):
            rows = pl.ds(i * block, block)
            scaled, inverse = norm_rows(resid_ref.get(i)[rows, :])
            grad = norm_back(mine_ref.get(i)[rows, :] + other_ref.get(i)[rows, :], scaled, inverse, gain_ref[...])
            grad = dn.get(i)[rows, :].astype(f32) + grad
            if i == 0:
                for item in (wo, query_ref, mixed_ref, key, value_ref):
                    item.start()
            grad_resid[rows, :] = grad
            grad = grad.astype(bf16)
            grad_mix[rows, :] = grad
            turned = grad.T
            for j in range(groups):
                mix_t[j, :, rows] = turned[j * rows_each : (j + 1) * rows_each, :]
        keypad, val = key.get(), value_ref.get()
        for item in (tab_t, norm_t, gated_ref):
            item.start()
        total = jnp.zeros((8, chans), f32)
        for i in range(count):
            rows, bin_rows = pl.ds(i * block, block), pl.ds(i * 2 * block, 2 * block)
            mask = row_mask(i * block, block, size)
            grad_gated = mask * times_transposed(grad_mix[rows, :], wo.get()[...])
            grads[rows, grad_query] = (grad_gated * mixed_ref.get()[rows, :]).astype(bf16)
            grad = grad_gated * query_ref.get()[rows, :]
            mix_grad[rows, :] = grad
            moved = shift_conv(taps_ref, keypad, i * block, block)
            shifted[rows, :] = moved
            total = total + column_sum(grad * (mask * moved * val[rows, :]))
            bins[bin_rows, :] = matmul(tab.get()[...], grad.astype(bf16))
        skip_sums[...] = total
        grad_resid_o.put()
        for item in (wq, wk, wv, tok):
            item.start()

        def product(i, _):
            start = pl.multiple_of(i * 16, 16)
            row = iota((16, 1), 0) + start
            first = row == 0
            scale = jnp.where(first, 0.5 / block, 1.0 / block)
            sign = 1.0 - 2.0 * (row % 2).astype(f32)
            for lane in range(0, chans, lanes):
                cols = pl.ds(lane, lanes)

                def pair(ref, j):
                    return (
                        ref[pl.ds(j * 2 * block + start, 16), cols],
                        ref[pl.ds(j * 2 * block + block + start, 16), cols],
                    )

                def put(ref, j, real, imag):
                    ref[pl.ds(j * 2 * block + start, 16), cols] = (real * scale).astype(bf16)
                    ref[pl.ds(j * 2 * block + block + start, 16), cols] = (imag * scale).astype(bf16)

                grad_pairs = [pair(bins, j) for j in range(count)]

                def correlate(ref, pairs):
                    real = imag = None
                    for g, j in pairs:
                        a, b = grad_pairs[g]
                        c, d = pair(ref, j)
                        other, d = edge(first, c, d)
                        r = a * c + b * d
                        s = b * other - a * d
                        real = r if real is None else real + r
                        imag = s if imag is None else imag + s
                    return real, imag

                for j in range(count):
                    real, imag = correlate(kers, [(m, m - j) for m in range(j, count)])
                    put(back_prod, j, real, imag)
                later = None
                for j in reversed(range(count)):
                    real, imag = correlate(sigs, [(m + j, m) for m in range(count - j)])
                    if later is None:
                        put(lag_prod, j, real, imag)
                    else:
                        put(lag_prod, j, real + sign * later[0], imag + sign * later[1])
                    later = (real, imag)
            return 0

        lax.fori_loop(0, block // 16, product, 0, unroll=2)
        shifted_grad[pl.ds(span, pad), :] = jnp.zeros((pad, chans), f32)
        totals = [jnp.zeros((8, chans), f32)] * lags
        for i in range(count):
            rows = pl.ds(i * block, block)
            bin_rows = pl.ds(i * 2 * block, 2 * block)
            mask = row_mask(i * block, block, size)
            signal_grad = matmul(tab_t.get()[...], back_prod[bin_rows, :])
            lag_o.ref[rows, :] = matmul(tab_t.get()[...], lag_prod[bin_rows, :])
            signal_grad = mask * (signal_grad + skip_ref[...] * mix_grad[rows, :])
            grads[rows, grad_value] = (signal_grad * shifted[rows, :]).astype(bf16)
            shifted_grad[rows, :] = signal_grad * val[rows, :]
        lag_o.put()
        for i in range(count):
            rows = pl.ds(i * block, block)
            here = keypad[pl.ds(i * block + pad, block), :]
            grad = None
            for lag in range(lags):
                moved = shifted_grad[pl.ds(i * block + lag, block), :]
                totals[lag] = totals[lag] + column_sum(moved * here)
                term = taps_ref[lag : lag + 1, :] * moved
                grad = term if grad is None else grad + term
            grads[rows, grad_key] = grad.astype(bf16)
        for lag in range(lags):
            taps_sums[pl.ds(lag * 8, 8), :] = totals[lag]

        for i in range(parts):
            at, pairs = 0, ([], [])
            for which, start, n in pieces[i]:
                if which == 0:
                    pairs[0].append((gated_ref.get(), start, n, at))
                else:
                    pairs[1].append((grads, (which - 1) * chans + start, n, at))
                at += n
            for source, some in ((mix_t, pairs[0]), (norm_t.get(), pairs[1])):
                if some:
                    split_products(place_ref, bits[i], source, chosen, some, gives[i].ref, keeps[i].ref)
            gives[i].put()
            keeps[i].put()

        gain_sum = jnp.zeros((8, width), f32)
        bias_sum = jnp.zeros((8, width), f32)
        for k, w in enumerate((wq, wk, wv)):
            all_weights[:, pl.ds(k * chans, chans)] = w.get()[...]
        for i in range(count + 1):
            if i < count:
                rows = pl.ds(i * block, block)
                part_o.ref[rows, :] = times_transposed(grads[rows, :], all_weights[...])
                part_o.put(i * block, block)
            if i:
                rows = pl.ds((i - 1) * block, block)
                scaled, _ = norm_rows(tok.get()[rows, :].astype(f32))
                part = part_o.ref[rows, :]
                gain_sum = gain_sum + column_sum(part * scaled)
                bias_sum = bias_sum + column_sum(part)
        mix_sums[pl.ds(0, 8), :] = gain_sum
        mix_sums[pl.ds(8, 8), :] = bias_sum
        mix_sums[pl.ds(16, 16), :] = feed_ref[...]
        part_o.put(span, 32, mix_sums)

    outs = [
        (shaped((span, width), f32), "=5"),
        (shaped((span, chans), f32), "h"),
        (shaped((span + 32, width), f32), "=3"),
        (shaped((8, chans), f32), "v"),
        (shaped((8 * lags, chans), f32), "v"),
    ]
    outs += [(shaped((half, w), f32), "h") for w in widths] * 2
    scratch = [
        pltpu.VMEM((span, width), bf16),
        pltpu.VMEM((groups, rows_each, span), bf16),
        pltpu.VMEM((span, chans), f32),
        pltpu.VMEM((2 * span, chans), f32),
        pltpu.VMEM((2 * span, chans), f32),
        pltpu.VMEM((2 * span, chans), f32),
        pltpu.VMEM((2 * span, chans), bf16),
        pltpu.VMEM((2 * span, chans), bf16),
        pltpu.VMEM((span + pad, chans), f32),
        pltpu.VMEM((span, chans), f32),
        pltpu.VMEM((span, 3 * chans), bf16),
        pltpu.VMEM((2, half, span), bf16),
        pltpu.VMEM((32, width), f32),
        pltpu.VMEM((width, 3 * chans), bf16),
    ]
    ins = [(length, "s"), (place, "s"), (down, count), (mine, count), (other, count), (resid, count), (feedgain, "v")]
    ins += [(x, "l") for x in (out_weight, mixed, query, sig16, ker16, table, table_t)] + [(skip, "v")]
    ins += [(keypad, "l"), (value, "l"), (taps, "v"), (normed_t, "l"), (gated, "l")]
    ins += [(weight, "l") for weight in weights] + [(tokens, "l"), (feed_sums, "v")]
    res = staged(run, ins, outs, "mixer_back", scratch)
    return res[:5], res[5 : 5 + parts], res[5 + parts :]


def feed_down(acts, down_weight):
    span = acts.shape[0]
    width = down_weight.shape[1]

    def run(act, down, out):
        for start in range(0, span, 128):
            out.ref[pl.ds(start, 128), :] = matmul(act.get()[pl.ds(start, 128), :], down.get()[...])
            out.put(start, 128)

    outs = [(shaped((span, width), f32), "h")]
    return staged(run, [(acts, "h"), (down_weight, "h")], outs, "feed_down")[0]


def finish_tokens(tokens, grad_resid, mine, other, gain):
    span, width = tokens.shape
    cuts = 4
    step = span // cuts

    def run(tok, grad_ref, mine_ref, other_ref, gain_ref, out):
        items = (tok, mine_ref, other_ref, grad_ref)
        for k in range(cuts):
            for item in items:
                item.start(k + 1)
        for k in range(cuts):
            rows = pl.ds(k * step, step)
            scaled, inverse = norm_rows(tok.get(k)[rows, :].astype(f32))
            grad = mine_ref.get(k)[rows, :] + other_ref.get(k)[rows, :]
            out.ref[rows, :] = grad_ref.get(k)[rows, :] + norm_back(grad, scaled, inverse, gain_ref[...])
            out.put(k * step, step)

    ins = [(tokens, cuts), (grad_resid, cuts), (mine, ("top", cuts)), (other, ("top", cuts)), (gain, "v")]
    return staged(run, ins, [(shaped((span, width), f32), "h")], "finish_tokens")[0]


def finish_layer(length, resid, mine, other, bias):
    span, width = resid.shape
    cuts = 4
    step = span // cuts

    def run(len_ref, resid_ref, a, b, bias_ref, out):
        for k in range(cuts):
            for item in (resid_ref, a, b):
                item.start(k + 1)
        for k in range(cuts):
            rows = pl.ds(k * step, step)
            value = resid_ref.get(k)[rows, :] + ((a.get(k)[rows, :] + b.get(k)[rows, :]) + bias_ref[...])
            out.ref[rows, :] = (row_mask(k * step, step, len_ref[0]) * value).astype(bf16)
            out.put(k * step, step)

    ins = [(length, "s"), (resid, cuts), (mine, cuts), (other, cuts), (bias, "v")]
    return staged(run, ins, [(shaped((span, width), bf16), "h")], "finish_layer")[0]


def halve(place, keeps, gots, cuts, rows, widths, theirs, before=None):
    n, n_cuts, n_out = len(keeps), len(cuts), len(widths)
    half = keeps[0].shape[0] // 2
    runs = [1 << cut[3] for cut in cuts]
    copies_each = [half // rows // size for size in runs]

    def run(place_ref, *refs):
        keep_refs, got_refs = refs[:n], refs[n : 2 * n]
        refs = refs[2 * n + (0 if before is None else n_out) :]
        outs, refs = refs[:n_out], refs[n_out:]
        sums, adds, sems = refs[:n_cuts], refs[n_cuts : 2 * n_cuts], refs[2 * n_cuts]
        waits, at = [], 0
        for i, (which, start, count, pos, bit, _, _) in enumerate(cuts):
            mine = (place_ref[0] >> bit) & 1
            side = 1 - mine if theirs else mine
            cols = pl.ds(start, count)
            waits.append([])
            for j in range(copies_each[i]):
                first = insert_bit(j * runs[i], pos, side) * rows
                source = pl.ds(pl.multiple_of(first, rows), runs[i] * rows)
                target = pl.ds(j * runs[i] * rows, runs[i] * rows)
                for array, held in ((keep_refs[which], sums[i]), (got_refs[which], adds[i])):
                    copy = pltpu.make_async_copy(array.at[source, cols], held.at[target], sems.at[at])
                    copy.start()
                    waits[i].append(copy)
                    at += 1
        copies = []
        for i, (_, _, count, _, _, out, start) in enumerate(cuts):
            for copy in waits[i]:
                copy.wait()
            sums[i][...] = sums[i][...] + adds[i][...]
            copies.append(pltpu.make_async_copy(sums[i], outs[out].at[:, pl.ds(start, count)], sems.at[at]))
            copies[-1].start()
            at += 1
        for copy in copies:
            copy.wait()

    ins = [(place, "s")] + [(x, "a") for x in (*keeps, *gots)]
    aliases = None
    if before is not None:
        aliases = {len(ins) + k: k for k in range(n_out)}
        ins += [(item, "a") for item in before]
    outs = [(shaped((half, w), f32), "a") for w in widths]
    scratch = [pltpu.VMEM((half, cut[2]), f32) for cut in cuts] * 2
    scratch.append(pltpu.SemaphoreType.DMA((2 * sum(copies_each) + n_cuts,)))
    return staged(run, ins, outs, "halve", scratch, aliases)


def pack_small(coef, rate, taps, skip, upbias, downbias, norms, norms_other):
    states, chans = coef.shape
    lags = taps.shape[0] // 8
    wide = [(upbias, None), (downbias, None)]
    counts = [states, states, lags, 1, upbias.shape[1] // chans, downbias.shape[1] // chans]
    counts.append(4 * (norms.shape[1] // chans))
    total = -(-sum(counts) // 16) * 16

    def run(coef_ref, rate_ref, taps_ref, skip_ref, up_ref, down_ref, norm_a, norm_b, out):
        out[...] = jnp.zeros_like(out)
        out[pl.ds(0, states), :] = coef_ref[...]
        out[pl.ds(states, states), :] = rate_ref[...]
        at = 2 * states

        def lay(value, at):
            row = jnp.sum(value, 0, keepdims=True)
            for start in range(0, row.shape[1], chans):
                out[pl.ds(at, 1), :] = row[:, start : start + chans]
                at += 1
            return at

        for lag in range(lags):
            at = lay(taps_ref[pl.ds(8 * lag, 8), :], at)
        at = lay(skip_ref[...], at)
        at = lay(up_ref[...], at)
        at = lay(down_ref[...], at)
        for start in range(0, 32, 8):
            rows = pl.ds(start, 8)
            at = lay(norm_a[rows, :] + norm_b[rows, :], at)

    ins = [coef, rate, taps, skip, upbias, downbias, norms, norms_other]
    ins = [(x, "v") for x in ins[:6]] + [(x, "t") for x in ins[6:]]
    out = staged(run, ins, [(shaped((total, chans), f32), "v")], "pack_small")[0]
    return out, counts


def unpack_small(place, bit, mine, other, counts, lags, hidden, width):
    half, chans = mine.shape

    def run(place_ref, a, b, coef, rate, taps, skip, up, down, *rest):
        norms, whole = rest[:-1], rest[-1]
        side = (place_ref[0] >> bit) & 1
        whole[pl.ds(pl.multiple_of(side * half, 8), half), :] = a[...]
        whole[pl.ds(pl.multiple_of((1 - side) * half, 8), half), :] = b[...]
        at = 0
        for out in (coef, rate, taps):
            out[...] = whole[pl.ds(at, out.shape[0]), :]
            at += out.shape[0]
        for out in (skip, up, down, *norms):
            for start in range(0, out.shape[1], chans):
                out[:, pl.ds(start, chans)] = whole[pl.ds(at, 1), :]
                at += 1

    states = counts[0]
    outs = [(shaped((n, chans), f32), "v") for n in (states, states, lags)]
    outs += [(shaped((n,), f32), "v") for n in (chans, hidden, width, width, width, width, width)]
    ins = [(place, "s"), (mine, "v"), (other, "v")]
    return staged(run, ins, outs, "unpack_small", [pltpu.VMEM((2 * half, chans), f32)])


def collect(keeps, gots, layout, sizes):
    n = len(keeps)
    rows = keeps[0].shape[0]
    names = list(sizes)

    def run(*refs):
        outs = dict(zip(names, refs[2 * n :]))
        for i in range(n):
            total = refs[i][...] + refs[n + i][...]
            at = 0
            for name, start, count in layout[i]:
                piece = total[:, at : at + count]
                if sizes[name][1]:
                    outs[name][pl.ds(start, count), :] = piece.T
                else:
                    outs[name][:, pl.ds(start, count)] = piece
                at += count

    outs = []
    for columns, turned in sizes.values():
        outs.append((shaped((columns, rows) if turned else (rows, columns), f32), "v"))
    res = staged(run, [(x, "v") for x in (*keeps, *gots)], outs, "collect")
    return dict(zip(names, res))


def state_grads(coef_t, rate_t, lag_grad):
    states, chans = coef_t.shape
    span = lag_grad.shape[0]
    step = 32
    blocks = span // step
    lanes = 128
    group = 8
    tiles = step // 8

    def run(coef_ref, rate_ref, lag_ref, coef_out, rate_out, fine, coarse, plain, place, ramp):
        rate = rate_ref[...][:, None, :]
        within = lax.broadcasted_iota(jnp.int32, (1, step, 1), 1).astype(f32)
        across = lax.broadcasted_iota(jnp.int32, (1, blocks, 1), 1).astype(f32)
        fine[...] = jnp.exp(-rate * within)
        coarse[...] = jnp.exp(-rate * (step * across))
        plain[...] = jnp.zeros_like(plain)
        place[...] = jnp.zeros_like(place)
        ramp[...] = jnp.zeros_like(ramp)
        for base in range(0, blocks, group):
            lag = [
                [
                    lag_ref[pl.ds((base + j) * step + 8 * a, 8), :]
                    for a in range(tiles)
                ]
                for j in range(group)
            ]

            def add(n, _):
                near = [fine[n, pl.ds(8 * a, 8), :] for a in range(tiles)]
                suffix = None
                later = None
                tilted = None
                for j in reversed(range(group)):
                    far = coarse[n, pl.ds(base + j, 1), :]
                    total = None
                    slope = None
                    for a in reversed(range(tiles)):
                        term = lag[j][a] * near[a]
                        if total is None:
                            total = term
                        else:
                            slope = total if slope is None else slope + total
                            total = total + term
                    weighted = far * total
                    bent = far * slope
                    tilted = bent if tilted is None else tilted + bent
                    if suffix is None:
                        suffix = weighted
                    else:
                        later = suffix if later is None else later + suffix
                        suffix = suffix + weighted
                plain[n] = plain[n] + suffix
                place[n] = place[n] + (later + float(base) * suffix)
                ramp[n] = ramp[n] + tilted
                return 0

            lax.fori_loop(0, states, add, 0, unroll=4)
        rows = lax.broadcasted_iota(jnp.int32, (1, 8, 1), 1).astype(f32)
        whole = plain[...]
        coef_out[...] = jnp.sum(whole, 1)
        times = float(step) * place[...] + 8.0 * ramp[...] + rows * whole
        rate_out[...] = -coef_ref[...] * jnp.sum(times, 1)

    shape = jax.ShapeDtypeStruct((states, chans), f32)
    block = pl.BlockSpec((states, lanes), lambda i: (0, i))
    return pl.pallas_call(
        run,
        grid=(chans // lanes,),
        in_specs=[block, block, pl.BlockSpec((span, lanes), lambda i: (0, i))],
        out_specs=[block, block],
        out_shape=[shape, shape],
        scratch_shapes=[
            pltpu.VMEM((states, step, lanes), f32),
            pltpu.VMEM((states, blocks, lanes), f32),
        ]
        + [pltpu.VMEM((states, 8, lanes), f32)] * 3,
        compiler_params=pltpu.CompilerParams(vmem_limit_bytes=most_vmem),
        cost_estimate=small_cost,
        name="state_grads",
    )(coef_t, rate_t, lag_grad)


def follow(values, *before):
    held = lax.optimization_barrier((list(values), before))[0]
    return held


def take_columns(cols, start, count):
    taken = []
    for name, first, columns in cols:
        low, high = max(start, 0), min(start + count, columns)
        if low < high:
            taken.append((name, first + low, high - low))
        start -= columns
    return taken


def body(
    tokens,
    lengths,
    mixgain,
    mixbias,
    query_weight,
    key_weight,
    value_weight,
    shift_taps,
    state_coef,
    state_rate,
    state_skip,
    out_weight,
    feedgain,
    feedbias,
    up_weight,
    up_bias,
    down_weight,
    down_bias,
    cotangent,
):
    assert lengths.shape[0] == 1
    span, width = tokens.shape
    chans = query_weight.shape[1]
    hidden = up_weight.shape[1]
    lags = shift_taps.shape[0]
    places = lax.axis_size("freq")
    halving = places == 16 and width % (16 * places) == 0
    groups = places if halving else 2
    rows = width // groups
    place = lax.axis_index("freq").astype(jnp.int32).reshape(1)
    third, part = hidden // 3, chans // 3
    feed_cols = [[("down", i * third, third), ("up", i * third, third)] for i in range(3)]
    mixer_cols = [
        [("out", 0, 3 * part), ("query", 0, part)],
        [("query", part, 2 * part), ("key", 0, 2 * part)],
        [("key", 2 * part, part), ("value", 0, 3 * part)],
    ]
    order_of = {"out": 0, "query": 1, "key": 2, "value": 3}
    pieces = [[(order_of[n], s, c) for n, s, c in cols] for cols in mixer_cols]
    thirds = [((i, 0), (i, third)) for i in range(3)]
    if halving:
        orders = [[(0, 1, 2, 3), (0, 1, 3, 2)], [(1, 2, 0, 3), (1, 3, 0, 2)], [(2, 0, 1, 3)]]
        bits = [order[0][0] for order in orders]
    else:
        place = jnp.zeros_like(place)
        bits = [0] * 3

    block = 256
    table_np = dft_table(block)
    table, table_t = jnp.asarray(table_np), jnp.asarray(np.ascontiguousarray(table_np.T))
    coef_t, rate_t = state_coef.T, state_rate.T

    normed, query, keypad, value, mixed, gated, sig16, ker16, out_part = mixer_forward(
        lengths,
        tokens,
        mixgain,
        mixbias,
        (query_weight, key_weight, value_weight),
        shift_taps,
        coef_t,
        rate_t,
        state_skip,
        out_weight,
        table,
        table_t,
    )
    out_other = swap(out_part, "tp", 0)
    down, down_t, normed_t, downbias_part = feed_prepare(lengths, cotangent, normed)
    down_t = down_t.reshape(groups, rows, span)
    normed_t = normed_t.reshape(groups, rows, span)
    (resid, acts, second_part, feed_sums, upbias_part), gives, keeps = feed_forward_back(
        place, out_part, out_other, feedgain, feedbias, down, down_t, up_weight, up_bias, down_weight, (bits, [2 * third] * 3, thirds)
    )
    second_other = swap(second_part, "tp", 0)
    if halving:
        gots = [swap(give, "freq", bit) for give, bit in zip(gives, bits)]
    (grad_resid, lag_grad, normed_part, skip_part, taps_part), more_gives, more_keeps = mixer_back(
        lengths, place, down, second_part, second_other, resid, feedgain, out_weight, mixed, query, sig16, ker16, table, table_t, state_skip,
        keypad, value, shift_taps, normed_t, gated, (query_weight, key_weight, value_weight), tokens, feed_sums, (bits, pieces)
    )
    (acts,) = follow([acts], normed_part)
    down_part = feed_down(acts, down_weight)
    if halving:

        items = []
        for source, all_cols in enumerate((feed_cols, mixer_cols)):
            for cols, some in zip(all_cols, orders):
                size = sum(count for _, _, count in cols) // len(some)
                for k, order in enumerate(some):
                    items.append((order, take_columns(cols, k * size, size), source))

        def arrange(step, source=None):
            arrays, starts = {}, {}
            for item in items:
                if source is None or item[2] == source:
                    arrays.setdefault(item[0][step], []).append(item)
            for some in arrays.values():
                at = 0
                for item in some:
                    starts[id(item)] = at
                    at += width_of(item)
            links = sorted(arrays)
            return links, [sum(map(width_of, arrays[link])) for link in links], arrays, starts

        def width_of(item):
            return sum(count for _, _, count in item[1])

        def cuts_to(step, source=None):
            links, _, _, starts = arrange(step - 1, source)
            next_links, widths, _, next_starts = arrange(step)
            cuts = []
            for item in items:
                if source is None or item[2] == source:
                    order = item[0]
                    pos = sorted(order[step:]).index(order[step])
                    cuts.append(
                        (
                            links.index(order[step - 1]),
                            starts[id(item)],
                            width_of(item),
                            pos,
                            order[step],
                            next_links.index(order[step]),
                            next_starts[id(item)],
                        )
                    )
            return cuts, rows, widths

        def exchange(gives, step):
            return [swap(give, "freq", link) for give, link in zip(gives, arrange(step)[0])]

        def add_swapped(value, bit):
            return value + swap(value, "freq", bit)

        gots = follow(gots, down_part)
        more_gives, lag_grad, normed_part, down_part = follow(
            [more_gives, lag_grad, normed_part, down_part], *gots
        )
        more_gots = exchange(more_gives, 0)
        held_gives = halve(place, keeps, gots, *cuts_to(1, 0), True)
        held_keeps = halve(place, keeps, gots, *cuts_to(1, 0), False)
    normed_other = swap(normed_part, "tp", 0)
    down_other = swap(down_part, "tp", 0)
    if halving:
        more_gots = follow(more_gots, normed_other, down_other, held_gives[0], held_keeps[0])
        gives = halve(place, more_keeps, more_gots, *cuts_to(1, 1), True, held_gives)
        gots = exchange(gives, 1)
        (lag_grad,) = follow([lag_grad], *gives)
    coef_part, rate_part = state_grads(coef_t, rate_t, lag_grad)
    small, counts = pack_small(
        coef_part, rate_part, taps_part, skip_part, upbias_part, downbias_part, normed_part, normed_other
    )
    if halving:
        half = small.shape[0] // 2
        side = place[0] & 1
        give = lax.dynamic_slice_in_dim(small, (1 - side) * half, half, 0)
        small = lax.dynamic_slice_in_dim(small, side * half, half, 0)
        other = swap(give, "freq", 0)
        (more_gots[0],) = follow([more_gots[0]], give)
        keeps = halve(place, more_keeps, more_gots, *cuts_to(1, 1), False, held_keeps)
        (other,) = follow([other], *keeps)
        old = follow(gots, other, small)
        gives = halve(place, keeps, old, *cuts_to(2), True)
        (small,) = follow([small], *gives)
        gots = exchange(gives, 2)
        small = small + other
        other = swap(small, "freq", 2)
        (down_part,) = follow([down_part], small)
        layer_out = finish_layer(lengths, resid, down_part, down_other, down_bias)
        (other,) = follow([other], layer_out)
        small = small + other
        other = swap(small, "freq", 3)
        (old[0],) = follow([old[0]], small)
        keeps = halve(place, keeps, old, *cuts_to(2), False)
        (other,) = follow([other], *keeps)
        small = small + other
        old = follow(gots, small, *keeps)
        gives = halve(place, keeps, old, *cuts_to(3), True)
        (small,) = follow([small], *gives)
        gots = exchange(gives, 3)
        other = swap(small, "freq", 1)
        (old[0],) = follow([old[0]], *gives)
        keeps = halve(place, keeps, old, *cuts_to(3), False)
        (other,) = follow([other], *keeps)
        small = small + other
        other = swap(small, "freq", 0)
        (normed_part,) = follow([normed_part], small)
        tokens_grad = finish_tokens(tokens, grad_resid, normed_part, normed_other, mixgain)
        (other,) = follow([other], tokens_grad)
        coef_sum, rate_sum, taps_sum, skip_sum, upbias_sum, downbias_sum, *norms = unpack_small(
            place, 0, small, other, counts, lags, hidden, width
        )
        gots = follow(gots, coef_sum)
        sizes = {"down": (hidden, False), "up": (hidden, False), "out": (chans, False)}
        sizes |= {name: (chans, False) for name in ("query", "key", "value")}
        links, _, arrays, _ = arrange(3)
        grads = collect(keeps, gots, [sum((item[1] for item in arrays[link]), []) for link in links], sizes)
    else:
        tokens_grad = finish_tokens(tokens, grad_resid, normed_part, normed_other, mixgain)
        layer_out = finish_layer(lengths, resid, down_part, down_other, down_bias)
        small = lax.psum(small, "freq")
        grads = {name: [] for name in ("down", "up", "out", "query", "key", "value")}
        for i in range(3):
            whole = jnp.concatenate(
                [
                    jnp.concatenate([keeps[i], more_keeps[i]], 1),
                    jnp.concatenate([gives[i], more_gives[i]], 1),
                ],
                0,
            )
            total = lax.psum_scatter(whole, "freq", scatter_dimension=0, tiled=True)
            at = 0
            for name, _, columns in feed_cols[i] + mixer_cols[i]:
                grads[name].append(total[:, at : at + columns])
                at += columns
        grads = {name: jnp.concatenate(some, 1) for name, some in grads.items()}
        cuts = np.cumsum(counts)
        coef_sum, rate_sum, taps_sum, skip_sum, upbias_sum, downbias_sum, norms, _ = jnp.split(small, cuts)
        norms = norms.reshape(4, width)
        skip_sum, upbias_sum, downbias_sum = [x.reshape(-1) for x in (skip_sum, upbias_sum, downbias_sum)]
    return (
        layer_out,
        tokens_grad,
        norms[0],
        norms[1],
        grads["query"],
        grads["key"],
        grads["value"],
        taps_sum,
        coef_sum.T,
        rate_sum.T,
        skip_sum,
        grads["out"].T,
        norms[2],
        norms[3],
        grads["up"],
        upbias_sum,
        grads["down"].T,
        downbias_sum,
    )


def solution(mesh):
    in_specs = (
        P("freq", None),
        P("freq"),
        P(),
        P(),
        P(None, "tp"),
        P(None, "tp"),
        P(None, "tp"),
        P(None, "tp"),
        P("tp", None),
        P("tp", None),
        P("tp"),
        P("tp", None),
        P(),
        P(),
        P(None, "tp"),
        P("tp"),
        P("tp", None),
        P(),
        P("freq", None),
    )
    out_specs = (
        P("freq", None),
        P("freq", None),
        P(),
        P(),
        P("freq", "tp"),
        P("freq", "tp"),
        P("freq", "tp"),
        P(None, "tp"),
        P("tp", None),
        P("tp", None),
        P("tp"),
        P("tp", "freq"),
        P(),
        P(),
        P("freq", "tp"),
        P("tp"),
        P("tp", "freq"),
        P(),
    )
    return jax.shard_map(body, mesh=mesh, in_specs=in_specs, out_specs=out_specs, check_vma=False)
```

```python
import math

import jax
import jax.numpy as jnp
import numpy as np
from jax import lax
from jax.experimental import pallas as pl
from jax.experimental.pallas import tpu as pltpu
from jax.sharding import PartitionSpec as P

f32 = jnp.float32
bf16 = jnp.bfloat16
in_vmem = pl.BlockSpec(memory_space=pltpu.VMEM)
in_smem = pl.BlockSpec(memory_space=pltpu.SMEM)
anywhere = pl.BlockSpec(memory_space=pl.ANY)
pad = 8
most_vmem = (64 << 20) - (128 << 10)
small_cost = pl.CostEstimate(flops=1, bytes_accessed=1, transcendentals=0)


def shaped(shape, dtype):
    return jax.ShapeDtypeStruct(shape, dtype)


def size_of(item):
    return math.prod(item.shape) * jnp.dtype(item.dtype).itemsize


def call(run, ins, outs, name, scratch=(), flops=0, moved=0, specs=None):
    held = sum(size_of(item) for item in (*ins, *outs, *scratch))
    return pl.pallas_call(
        run,
        in_specs=specs or [in_vmem] * len(ins),
        out_specs=[in_vmem] * len(outs),
        out_shape=outs,
        scratch_shapes=list(scratch),
        compiler_params=pltpu.CompilerParams(vmem_limit_bytes=held + (6 << 20)),
        cost_estimate=small_cost,
        name=name,
    )(*ins)


def matmul(left, right):
    return jnp.dot(left, right, preferred_element_type=f32)


def times_transposed(left, right):
    return lax.dot_general(left, right, (((1,), (1,)), ((), ())), preferred_element_type=f32)


def swap(value, axis, bit):
    size = lax.axis_size(axis)
    return lax.ppermute(value, axis, [(i, i ^ (1 << bit)) for i in range(size)])


def dft_table(block):
    bins = np.arange(block)[:, None].astype(np.int64)
    times = np.arange(block)[None, :].astype(np.int64)
    angle = (bins * times % (2 * block)) * (math.pi / block)
    table = np.concatenate([np.cos(angle), np.sin(angle)], 0)
    table[block] = 1 - 2 * (np.arange(block) % 2)
    return table.astype(jnp.bfloat16)


def iota(shape, dim):
    return lax.broadcasted_iota(jnp.int32, shape, dim)


def row_mask(first, count, length):
    return (iota((count, 1), 0) + first < length).astype(f32)


def insert_bit(index, pos, bit):
    low = index & ((1 << pos) - 1)
    return ((index >> pos) << (pos + 1)) | (bit << pos) | low


def norm_rows(value):
    mean = jnp.mean(value, -1, keepdims=True)
    centered = value - mean
    inverse = lax.rsqrt(jnp.mean(centered * centered, -1, keepdims=True) + 1e-05)
    return centered * inverse, inverse


def norm_back(grad_out, scaled, inverse, gain):
    weighted = grad_out * gain
    return inverse * (
        weighted
        - jnp.mean(weighted, -1, keepdims=True)
        - scaled * jnp.mean(weighted * scaled, -1, keepdims=True)
    )


def column_sum(value):
    rows, width = value.shape
    return jnp.sum(value.reshape(rows // 8, 8, width), 0)


def shift_conv(taps, keypad, start, count):
    lags = taps.shape[0]
    return sum(
        taps[lag : lag + 1, :] * keypad[pl.ds(start + pad - lag, count), :] for lag in range(lags)
    )


def edge(first, real, imag):
    return jnp.where(first, imag, real), jnp.where(first, 0.0, imag)


class Coming:
    def __init__(self, source, held, sems, cuts=1):
        self.held, self.started, self.here = held, 0, 0
        if source.shape[-2:] != held.shape[-2:] and len(source.shape) > 1 and cuts == 1:
            last = pl.ds(source.shape[0] - held.shape[0], held.shape[0])
            self.copies = [pltpu.make_async_copy(source.at[last], held, sems.at[0])]
            return
        if len(source.shape) == 1:
            self.copies = [pltpu.make_async_copy(source, held.at[0], sems.at[0])]
            return
        rows = held.shape[0] // cuts
        self.copies = []
        for i in range(cuts):
            part = pl.ds(i * rows, rows) if cuts > 1 else pl.ds(0, held.shape[0])
            self.copies.append(pltpu.make_async_copy(source.at[part], held.at[part], sems.at[i]))

    def start(self, cuts=None):
        cuts = len(self.copies) if cuts is None else cuts
        while self.started < cuts:
            self.copies[self.started].start()
            self.started += 1

    def get(self, cut=None):
        self.start(None if cut is None else cut + 1)
        until = len(self.copies) if cut is None else cut + 1
        while self.here < until:
            self.copies[self.here].wait()
            self.here += 1
        return self.held


class Going:
    def __init__(self, target, held, sems):
        self.target, self.ref, self.sems, self.copies = target, held, sems, []

    def put(self, start=0, count=None, source=None):
        rows = pl.ds(start, self.ref.shape[0] if count is None else count)
        sem = self.sems.at[len(self.copies)]
        if len(self.target.shape) == 1:
            copy = pltpu.make_async_copy(self.ref.at[0], self.target, sem)
        else:
            source = self.ref.at[rows] if source is None else source
            copy = pltpu.make_async_copy(source, self.target.at[rows], sem)
        copy.start()
        self.copies.append(copy)


    def put_columns(self, start, count):
        cols = pl.ds(start, count)
        sem = self.sems.at[len(self.copies)]
        copy = pltpu.make_async_copy(self.ref.at[:, cols], self.target.at[:, cols], sem)
        copy.start()
        self.copies.append(copy)


most_puts = 16
most_cuts = 4
in_hbm = pl.BlockSpec(memory_space=pl.ANY)


def staged(run, ins, outs, name, scratch=(), aliases=None):
    spec = {"s": in_smem}
    plain = ("s", "a")
    shared = lambda kind: isinstance(kind, str) and kind[0] == "="
    top = lambda kind: isinstance(kind, tuple)

    def tail(x, kind):
        if kind == "t" or top(kind):
            return shaped((32 if kind == "t" else x.shape[0] - 32, x.shape[1]), x.dtype)
        return x

    held = [tail(x, kind) for x, kind in (*ins, *outs) if kind not in plain and not shared(kind)]
    held = [shaped(x.shape if len(x.shape) > 1 else (1, *x.shape), x.dtype) for x in held]
    n_in = sum(kind not in plain for _, kind in ins)
    n_out = sum(kind not in plain for _, kind in outs)

    def whole(*refs):
        refs = list(refs)
        given, made = refs[: len(ins)], refs[len(ins) : len(ins) + len(outs)]
        rest = refs[len(ins) + len(outs) :]
        own, bufs = rest[: len(scratch)], rest[len(scratch) :]
        in_sems, out_sems = bufs[-2:]
        bufs = list(bufs[:-2])
        views, at = [], 0
        for ref, (_, kind) in zip(given, ins):
            if kind not in plain:
                cuts = kind[1] if top(kind) else kind if isinstance(kind, int) else 1
                views.append(Coming(ref, bufs.pop(0), in_sems.at[at], cuts))
                at += 1
                if kind != "l" and cuts == 1:
                    views[-1].start()
            else:
                views.append(ref)
        going, at = [], 0
        for ref, (_, kind) in zip(made, outs):
            if kind not in plain:
                held_at = views[int(kind[1:])].held if shared(kind) else bufs.pop(0)
                going.append(Going(ref, held_at, out_sems.at[at]))
                at += 1
            else:
                going.append(ref)
        for view, (_, kind) in zip(views, ins):
            if kind in ("v", "t"):
                view.get()
        views = [view.held if kind in ("v", "t") else view for view, (_, kind) in zip(views, ins)]
        small = [item for item, (_, kind) in zip(going, outs) if kind == "v"]
        run(*views, *[item.ref if item in small else item for item in going], *own)
        for item in small:
            item.put()
        for view in views:
            if isinstance(view, Coming):
                view.get()
        for item in going:
            if isinstance(item, Going):
                for copy in item.copies:
                    copy.wait()

    return pl.pallas_call(
        whole,
        in_specs=[spec.get(kind, in_hbm) for _, kind in ins],
        out_specs=[spec.get(kind, in_hbm) for _, kind in outs],
        out_shape=[item for item, _ in outs],
        scratch_shapes=list(scratch)
        + [pltpu.VMEM(x.shape, x.dtype) for x in held]
        + [
            pltpu.SemaphoreType.DMA((max(n_in, 1), most_cuts)),
            pltpu.SemaphoreType.DMA((max(n_out, 1), most_puts)),
        ],
        input_output_aliases=aliases or {},
        compiler_params=pltpu.CompilerParams(vmem_limit_bytes=most_vmem),
        cost_estimate=small_cost,
        name=name,
    )(*[x for x, _ in ins])


def split_products(place_ref, bit, source, chosen, pairs, give, keep):
    groups, rows, _ = source.shape
    mine = (place_ref[0] >> bit) & 1
    for k, (out, side) in enumerate(((give, 1 - mine), (keep, mine))):
        for j in range(groups // 2):
            chosen[k, pl.ds(j * rows, rows), :] = source[insert_bit(j, bit, side)]
    for k, out in enumerate((give, keep)):
        for right, start, count, to in pairs:
            out[:, pl.ds(to, count)] = matmul(chosen[k], right[:, pl.ds(start, count)])


def mixer_forward(length, tokens, gain, bias, weights, taps, coef_t, rate_t, skip, out_weight, table, table_t):
    span, width = tokens.shape
    chans = out_weight.shape[0]
    states = coef_t.shape[0]
    block = table.shape[1]
    count = span // block
    step = 32
    far_steps = span // step
    group = 8
    lanes = 128

    def run(
        len_ref, tok, gain_ref, bias_ref, wq, wk, wv, taps_ref, coef_ref, rate_ref, skip_ref, wo, tab, tab_t,
        normed_o, query_o, keypad_o, value_o, mixed_o, gated_o, sig_o, ker_o, part_o,
        fine, coarse, signal, sig_bins, ker_bins, prod,
    ):
        size = len_ref[0]
        normed, query, keypad, value = normed_o.ref, query_o.ref, keypad_o.ref, value_o.ref
        sig16, ker16 = sig_o.ref, ker_o.ref

        within = iota((1, step, 1), 1).astype(f32)
        across = iota((1, group, 1), 1).astype(f32) * float(step)
        rate = rate_ref[...][:, None, :]
        fine[...] = jnp.exp(-rate * within)
        for k in range(far_steps // group):
            coarse[:, k] = coef_ref[...][:, None, :] * jnp.exp(-rate * (across + float(step * group * k)))
        keypad[pl.ds(0, pad), :] = jnp.zeros((pad, chans), f32)
        tok_ref, wq_ref, wk_ref, wv_ref = tok.get(), wq.get(), wk.get(), wv.get()
        for item in (wo, tab, tab_t):
            item.start()

        for i in range(count):
            rows = pl.ds(i * block, block)
            scaled, _ = norm_rows(tok_ref[rows, :].astype(f32))
            norm = (scaled * gain_ref[...] + bias_ref[...]).astype(bf16)
            normed[rows, :] = norm
            query[rows, :] = matmul(norm, wq_ref[...])
            keypad[pl.ds(i * block + pad, block), :] = matmul(norm, wk_ref[...])
            value[rows, :] = matmul(norm, wv_ref[...])
        for i in range(count):
            rows = pl.ds(i * block, block)
            shifted = shift_conv(taps_ref, keypad, i * block, block)
            sig = row_mask(i * block, block, size) * shifted * value[rows, :]
            signal[rows, :] = sig
            sig16[rows, :] = sig.astype(bf16)
            sig_bins[pl.ds(i * 2 * block, 2 * block), :] = matmul(tab.get()[...], sig16[rows, :])
        for item in (normed_o, query_o, keypad_o, value_o, sig_o):
            item.put()

        def some_taps(u, _):
            i = u // (chans // lanes)
            cols = pl.ds(pl.multiple_of((u - i * (chans // lanes)) * lanes, lanes), lanes)
            sums = [None] * group
            for n in range(states):
                near = fine[n, :, cols]
                for j in range(group):
                    term = coarse[n, i, pl.ds(j, 1), cols] * near
                    sums[j] = term if n == 0 else sums[j] + term
            for j in range(group):
                place = pl.ds(pl.multiple_of(i * block + j * step, step), step)
                ker16[place, cols] = sums[j].astype(bf16)
            return 0

        lax.fori_loop(0, far_steps // group * (chans // lanes), some_taps, 0)
        ker_o.put()
        sign = 1.0 - 2.0 * (iota((2 * block, 1), 0) % 2).astype(f32)
        before = None
        for i in range(count):
            ker = matmul(tab.get()[...], ker16[pl.ds(i * block, block), :])
            ker_bins[pl.ds(i * 2 * block, 2 * block), :] = ker if before is None else ker + sign * before
            before = ker

        def product(i, _):
            start = pl.multiple_of(i * 16, 16)
            first = (iota((16, 1), 0) + start) == 0
            scale = jnp.where(first, 0.5 / block, 1.0 / block)
            for lane in range(0, chans, lanes):
                cols = pl.ds(lane, lanes)

                def pair(ref, j):
                    return (
                        ref[pl.ds(j * 2 * block + start, 16), cols],
                        ref[pl.ds(j * 2 * block + block + start, 16), cols],
                    )

                sigs = [pair(sig_bins, j) for j in range(count)]
                kers = []
                for j in range(count):
                    c, d = pair(ker_bins, j)
                    other, d = edge(first, c, d)
                    kers.append((c, other, d))
                for j in range(count):
                    real = imag = None
                    for m in range(j + 1):
                        a, b = sigs[m]
                        c, other, d = kers[j - m]
                        r = a * c - b * d
                        s = a * d + b * other
                        real = r if real is None else real + r
                        imag = s if imag is None else imag + s
                    prod[pl.ds(j * 2 * block + start, 16), cols] = (real * scale).astype(bf16)
                    prod[pl.ds(j * 2 * block + block + start, 16), cols] = (imag * scale).astype(bf16)
            return 0

        lax.fori_loop(0, block // 16, product, 0)
        for i in range(count):
            rows = pl.ds(i * block, block)
            conv = matmul(tab_t.get()[...], prod[pl.ds(i * 2 * block, 2 * block), :])
            mixed = conv + skip_ref[...] * signal[rows, :]
            mixed_o.ref[rows, :] = mixed
            gated = (row_mask(i * block, block, size) * query[rows, :] * mixed).astype(bf16)
            gated_o.ref[rows, :] = gated
            part_o.ref[rows, :] = matmul(gated, wo.get()[...]) + 0.5 * tok_ref[rows, :].astype(f32)
            for item in (part_o, mixed_o, gated_o):
                item.put(i * block, block)

    outs = [
        (shaped((span, width), bf16), "h"),
        (shaped((span, chans), f32), "h"),
        (shaped((span + pad, chans), f32), "h"),
        (shaped((span, chans), f32), "h"),
        (shaped((span, chans), f32), "h"),
        (shaped((span, chans), bf16), "h"),
        (shaped((span, chans), bf16), "h"),
        (shaped((span, chans), bf16), "h"),
        (shaped((span, width), f32), "h"),
    ]
    scratch = [
        pltpu.VMEM((states, step, chans), f32),
        pltpu.VMEM((states, far_steps // group, group, chans), f32),
        pltpu.VMEM((span, chans), f32),
        pltpu.VMEM((2 * span, chans), f32),
        pltpu.VMEM((2 * span, chans), f32),
        pltpu.VMEM((2 * span, chans), bf16),
    ]
    ins = [(length, "s"), (tokens, "h"), (gain, "v"), (bias, "v")]
    ins += [(weight, "h") for weight in weights]
    ins += [(taps, "v"), (coef_t, "v"), (rate_t, "v"), (skip, "v")]
    ins += [(out_weight, "l"), (table, "l"), (table_t, "l")]
    return staged(run, ins, outs, "mixer_forward", scratch)


def norm_sums(grad, value, start, gain_sum, bias_sum):
    rows = pl.ds(start, 128)
    scaled, _ = norm_rows(value[rows, :].astype(f32))
    part = grad[rows, :]
    return gain_sum + column_sum(part * scaled), bias_sum + column_sum(part)


def feed_prepare(length, cotangent, normed):
    span, width = cotangent.shape

    def run(len_ref, cot, normed_ref, down_o, down_t, normed_t, sums):
        size = len_ref[0]
        total = jnp.zeros((8, width), f32)
        for start in range(0, span, 256):
            rows = pl.ds(start, 256)
            grad = row_mask(start, 256, size) * cot.get()[rows, :].astype(f32)
            total = total + column_sum(grad)
            down_o.ref[rows, :] = grad.astype(bf16)
            down_o.put(start, 256)
            down_t.ref[:, rows] = grad.astype(bf16).T
        down_t.put()
        for start in range(0, span, 256):
            rows = pl.ds(start, 256)
            normed_t.ref[:, rows] = normed_ref.get()[rows, :].T
        normed_t.put()
        sums[...] = total

    outs = [
        (shaped((span, width), bf16), "h"),
        (shaped((width, span), bf16), "h"),
        (shaped((width, span), bf16), "h"),
        (shaped((8, width), f32), "v"),
    ]
    return staged(run, [(length, "s"), (cotangent, "h"), (normed, "h")], outs, "feed_prepare")


def feed_forward_back(place, mine, other, gain, bias, down, down_t, up_weight, up_bias, down_weight, cuts):
    span, width = mine.shape
    hidden = up_weight.shape[1]
    groups, rows_each, _ = down_t.shape
    half = width // 2
    bits, widths, thirds = cuts
    size = hidden // 3
    parts = len(bits)
    step = 256

    def run(*refs):
        place_ref, mine_ref, other_ref, gain_ref, bias_ref, dn, dn_t, up, upb, dw = refs[:10]
        resid_o, acts_o, part_o, sums, upb_sums = refs[10:15]
        gives, keeps = refs[15 : 15 + parts], refs[15 + parts : 15 + 2 * parts]
        second, second_t, grad_hid, hid_a, hid_b, pre_a, pre_b, hat, chosen_a, chosen_b = refs[15 + 2 * parts :]
        resid, acts = resid_o.ref, acts_o.ref
        cuts = span // step
        for k in range(cuts):
            for item in (mine_ref, other_ref):
                item.start(k + 1)
        for item in (up, dw, dn, dn_t):
            item.start()
        for k in range(cuts):
            rows = pl.ds(k * step, step)
            value = mine_ref.get(k)[rows, :] + other_ref.get(k)[rows, :]
            resid[rows, :] = value
            scaled, _ = norm_rows(value)
            hat[rows, :] = scaled
            norm = (scaled * gain_ref[...] + bias_ref[...]).astype(bf16)
            second[rows, :] = norm
            turned = norm.T
            for j in range(groups):
                second_t[j, :, rows] = turned[j * rows_each : (j + 1) * rows_each, :]
        up_ref, dw_ref, dn_ref = up.get(), dw.get(), dn.get()
        resid_o.put()
        slots = [(hid_a, pre_a), (hid_b, pre_b)]

        def rise(i, k):
            rows, cols = pl.ds(k * step, step), pl.ds(i * size, size)
            hid, pre = slots[k % 2]
            hid[...] = matmul(second[rows, :], up_ref[:, cols])
            pre[...] = times_transposed(dn_ref[rows, :], dw_ref[cols, :])

        def gelu(i, k):
            rows, cols = pl.ds(k * step, step), pl.ds(i * size, size)
            hid, pre = slots[k % 2]
            h = hid[...] + upb[:, cols]
            cdf = 0.5 + 0.5 * lax.erf(h * (1.0 / math.sqrt(2.0)))
            slope = cdf + h * jnp.exp(-0.5 * h * h) * (1.0 / math.sqrt(2.0 * math.pi))
            acts[rows, cols] = (h * cdf).astype(bf16)
            grad = (pre[...] * slope).astype(bf16)
            grad_hid[rows, cols] = grad
            return column_sum(grad.astype(f32))

        for i in range(3):
            total = jnp.zeros((8, size), f32)
            rise(i, 0)
            for k in range(cuts):
                if k + 1 < cuts:
                    rise(i, k + 1)
                total = total + gelu(i, k)
            upb_sums[:, pl.ds(i * size, size)] = total
            (down_part, down_at), (up_part, up_at) = thirds[i]
            for source, chosen, right, (which, at) in (
                (dn_t.get(), chosen_a, acts, (down_part, down_at)),
                (second_t, chosen_b, grad_hid, (up_part, up_at)),
            ):
                split_products(
                    place_ref, bits[which], source, chosen, [(right, i * size, size, at)], gives[which].ref, keeps[which].ref
                )
            for which in sorted({down_part, up_part}):
                gives[which].put()
                keeps[which].put()
            acts_o.put_columns(i * size, size)
        gain_sum = jnp.zeros((8, width), f32)
        bias_sum = jnp.zeros((8, width), f32)
        for k in range(cuts + 1):
            if k < cuts:
                rows = pl.ds(k * step, step)
                part_o.ref[rows, :] = times_transposed(grad_hid[rows, :], up_ref[...])
                part_o.put(k * step, step)
            if k:
                rows = pl.ds((k - 1) * step, step)
                part = part_o.ref[rows, :]
                gain_sum = gain_sum + column_sum(part * hat[rows, :])
                bias_sum = bias_sum + column_sum(part)
        sums[pl.ds(0, 8), :] = gain_sum
        sums[pl.ds(8, 8), :] = bias_sum

    outs = [
        (shaped((span, width), f32), "h"),
        (shaped((span, hidden), bf16), "h"),
        (shaped((span, width), f32), "h"),
        (shaped((16, width), f32), "v"),
        (shaped((8, hidden), f32), "v"),
    ]
    outs += [(shaped((half, w), f32), "h") for w in widths] * 2
    scratch = [
        pltpu.VMEM((span, width), bf16),
        pltpu.VMEM((groups, rows_each, span), bf16),
        pltpu.VMEM((span, hidden), bf16),
        pltpu.VMEM((step, size), f32),
        pltpu.VMEM((step, size), f32),
        pltpu.VMEM((step, size), f32),
        pltpu.VMEM((step, size), f32),
        pltpu.VMEM((span, width), f32),
        pltpu.VMEM((2, half, span), bf16),
        pltpu.VMEM((2, half, span), bf16),
    ]
    cut = span // step
    ins = [(place, "s"), (mine, cut), (other, cut), (gain, "v"), (bias, "v")]
    ins += [(down, "l"), (down_t, "l"), (up_weight, "l"), (up_bias, "v"), (down_weight, "l")]
    res = staged(run, ins, outs, "feed_forward_back", scratch)
    return res[:5], res[5 : 5 + parts], res[5 + parts :]


def mixer_back(
    length, place, down, mine, other, resid, feedgain, out_weight, mixed, query, sig16, ker16, table, table_t, skip,
    keypad, value, taps, normed_t, gated, weights, tokens, feed_sums, cuts,
):
    span, width = resid.shape
    chans = query.shape[1]
    groups, rows_each, _ = normed_t.shape
    half = width // 2
    block = table.shape[1]
    count = span // block
    lags = taps.shape[0]
    lanes = 128
    bits, pieces = cuts
    widths = [sum(n for _, _, n in part) for part in pieces]
    parts = len(bits)

    def run(*refs):
        len_ref, place_ref, dn, mine_ref, other_ref, resid_ref, gain_ref, wo, mixed_ref, query_ref = refs[:10]
        sig_ref, ker_ref, tab, tab_t, skip_ref, key, value_ref, taps_ref, norm_t, gated_ref = refs[10:20]
        wq, wk, wv, tok, feed_ref = refs[20:25]
        grad_resid_o, lag_o, part_o, skip_sums, taps_sums = refs[25:30]
        gives, keeps = refs[30 : 30 + parts], refs[30 + parts : 30 + 2 * parts]
        grad_mix, mix_t, mix_grad, bins, sigs, kers, back_prod, lag_prod, shifted_grad, shifted, grads, chosen, mix_sums, all_weights = refs[30 + 2 * parts :]
        size = len_ref[0]
        grad_resid = grad_resid_o.ref
        grad_query, grad_key, grad_value = [pl.ds(k * chans, chans) for k in range(3)]

        for item in (tab, sig_ref, ker_ref):
            item.start()
        for i in range(count):
            for item in (dn, mine_ref, other_ref, resid_ref):
                item.start(i + 1)
        before = None
        turn = 1.0 - 2.0 * (iota((2 * block, 1), 0) % 2).astype(f32)
        for i in range(count):
            rows, bin_rows = pl.ds(i * block, block), pl.ds(i * 2 * block, 2 * block)
            sigs[bin_rows, :] = matmul(tab.get()[...], sig_ref.get()[rows, :])
            ker = matmul(tab.get()[...], ker_ref.get()[rows, :])
            kers[bin_rows, :] = ker if before is None else ker + turn * before
            before = ker
        for i in range(count):
            rows = pl.ds(i * block, block)
            scaled, inverse = norm_rows(resid_ref.get(i)[rows, :])
            grad = norm_back(mine_ref.get(i)[rows, :] + other_ref.get(i)[rows, :], scaled, inverse, gain_ref[...])
            grad = dn.get(i)[rows, :].astype(f32) + grad
            if i == 0:
                for item in (wo, query_ref, mixed_ref, key, value_ref):
                    item.start()
            grad_resid[rows, :] = grad
            grad = grad.astype(bf16)
            grad_mix[rows, :] = grad
            turned = grad.T
            for j in range(groups):
                mix_t[j, :, rows] = turned[j * rows_each : (j + 1) * rows_each, :]
        keypad, val = key.get(), value_ref.get()
        for item in (tab_t, norm_t, gated_ref):
            item.start()
        total = jnp.zeros((8, chans), f32)
        for i in range(count):
            rows, bin_rows = pl.ds(i * block, block), pl.ds(i * 2 * block, 2 * block)
            mask = row_mask(i * block, block, size)
            grad_gated = mask * times_transposed(grad_mix[rows, :], wo.get()[...])
            grads[rows, grad_query] = (grad_gated * mixed_ref.get()[rows, :]).astype(bf16)
            grad = grad_gated * query_ref.get()[rows, :]
            mix_grad[rows, :] = grad
            moved = shift_conv(taps_ref, keypad, i * block, block)
            shifted[rows, :] = moved
            total = total + column_sum(grad * (mask * moved * val[rows, :]))
            bins[bin_rows, :] = matmul(tab.get()[...], grad.astype(bf16))
        skip_sums[...] = total
        grad_resid_o.put()
        for item in (wq, wk, wv, tok):
            item.start()

        def product(i, _):
            start = pl.multiple_of(i * 16, 16)
            row = iota((16, 1), 0) + start
            first = row == 0
            scale = jnp.where(first, 0.5 / block, 1.0 / block)
            sign = 1.0 - 2.0 * (row % 2).astype(f32)
            for lane in range(0, chans, lanes):
                cols = pl.ds(lane, lanes)

                def pair(ref, j):
                    return (
                        ref[pl.ds(j * 2 * block + start, 16), cols],
                        ref[pl.ds(j * 2 * block + block + start, 16), cols],
                    )

                def put(ref, j, real, imag):
                    ref[pl.ds(j * 2 * block + start, 16), cols] = (real * scale).astype(bf16)
                    ref[pl.ds(j * 2 * block + block + start, 16), cols] = (imag * scale).astype(bf16)

                grad_pairs = [pair(bins, j) for j in range(count)]

                def correlate(ref, pairs):
                    real = imag = None
                    for g, j in pairs:
                        a, b = grad_pairs[g]
                        c, d = pair(ref, j)
                        other, d = edge(first, c, d)
                        r = a * c + b * d
                        s = b * other - a * d
                        real = r if real is None else real + r
                        imag = s if imag is None else imag + s
                    return real, imag

                for j in range(count):
                    real, imag = correlate(kers, [(m, m - j) for m in range(j, count)])
                    put(back_prod, j, real, imag)
                later = None
                for j in reversed(range(count)):
                    real, imag = correlate(sigs, [(m + j, m) for m in range(count - j)])
                    if later is None:
                        put(lag_prod, j, real, imag)
                    else:
                        put(lag_prod, j, real + sign * later[0], imag + sign * later[1])
                    later = (real, imag)
            return 0

        lax.fori_loop(0, block // 16, product, 0)
        shifted_grad[pl.ds(span, pad), :] = jnp.zeros((pad, chans), f32)
        totals = [jnp.zeros((8, chans), f32)] * lags
        for i in range(count):
            rows = pl.ds(i * block, block)
            bin_rows = pl.ds(i * 2 * block, 2 * block)
            mask = row_mask(i * block, block, size)
            signal_grad = matmul(tab_t.get()[...], back_prod[bin_rows, :])
            lag_o.ref[rows, :] = matmul(tab_t.get()[...], lag_prod[bin_rows, :])
            signal_grad = mask * (signal_grad + skip_ref[...] * mix_grad[rows, :])
            grads[rows, grad_value] = (signal_grad * shifted[rows, :]).astype(bf16)
            shifted_grad[rows, :] = signal_grad * val[rows, :]
        lag_o.put()
        for i in range(count):
            rows = pl.ds(i * block, block)
            here = keypad[pl.ds(i * block + pad, block), :]
            grad = None
            for lag in range(lags):
                moved = shifted_grad[pl.ds(i * block + lag, block), :]
                totals[lag] = totals[lag] + column_sum(moved * here)
                term = taps_ref[lag : lag + 1, :] * moved
                grad = term if grad is None else grad + term
            grads[rows, grad_key] = grad.astype(bf16)
        for lag in range(lags):
            taps_sums[pl.ds(lag * 8, 8), :] = totals[lag]

        for i in range(parts):
            at, pairs = 0, ([], [])
            for which, start, n in pieces[i]:
                if which == 0:
                    pairs[0].append((gated_ref.get(), start, n, at))
                else:
                    pairs[1].append((grads, (which - 1) * chans + start, n, at))
                at += n
            for source, some in ((mix_t, pairs[0]), (norm_t.get(), pairs[1])):
                if some:
                    split_products(place_ref, bits[i], source, chosen, some, gives[i].ref, keeps[i].ref)
            gives[i].put()
            keeps[i].put()

        gain_sum = jnp.zeros((8, width), f32)
        bias_sum = jnp.zeros((8, width), f32)
        for k, w in enumerate((wq, wk, wv)):
            all_weights[:, pl.ds(k * chans, chans)] = w.get()[...]
        for i in range(count + 1):
            if i < count:
                rows = pl.ds(i * block, block)
                part_o.ref[rows, :] = times_transposed(grads[rows, :], all_weights[...])
                part_o.put(i * block, block)
            if i:
                rows = pl.ds((i - 1) * block, block)
                scaled, _ = norm_rows(tok.get()[rows, :].astype(f32))
                part = part_o.ref[rows, :]
                gain_sum = gain_sum + column_sum(part * scaled)
                bias_sum = bias_sum + column_sum(part)
        mix_sums[pl.ds(0, 8), :] = gain_sum
        mix_sums[pl.ds(8, 8), :] = bias_sum
        mix_sums[pl.ds(16, 16), :] = feed_ref[...]
        part_o.put(span, 32, mix_sums)

    outs = [
        (shaped((span, width), f32), "=5"),
        (shaped((span, chans), f32), "h"),
        (shaped((span + 32, width), f32), "=3"),
        (shaped((8, chans), f32), "v"),
        (shaped((8 * lags, chans), f32), "v"),
    ]
    outs += [(shaped((half, w), f32), "h") for w in widths] * 2
    scratch = [
        pltpu.VMEM((span, width), bf16),
        pltpu.VMEM((groups, rows_each, span), bf16),
        pltpu.VMEM((span, chans), f32),
        pltpu.VMEM((2 * span, chans), f32),
        pltpu.VMEM((2 * span, chans), f32),
        pltpu.VMEM((2 * span, chans), f32),
        pltpu.VMEM((2 * span, chans), bf16),
        pltpu.VMEM((2 * span, chans), bf16),
        pltpu.VMEM((span + pad, chans), f32),
        pltpu.VMEM((span, chans), f32),
        pltpu.VMEM((span, 3 * chans), bf16),
        pltpu.VMEM((2, half, span), bf16),
        pltpu.VMEM((32, width), f32),
        pltpu.VMEM((width, 3 * chans), bf16),
    ]
    ins = [(length, "s"), (place, "s"), (down, count), (mine, count), (other, count), (resid, count), (feedgain, "v")]
    ins += [(x, "l") for x in (out_weight, mixed, query, sig16, ker16, table, table_t)] + [(skip, "v")]
    ins += [(keypad, "l"), (value, "l"), (taps, "v"), (normed_t, "l"), (gated, "l")]
    ins += [(weight, "l") for weight in weights] + [(tokens, "l"), (feed_sums, "v")]
    res = staged(run, ins, outs, "mixer_back", scratch)
    return res[:5], res[5 : 5 + parts], res[5 + parts :]


def feed_down(acts, down_weight):
    span = acts.shape[0]
    width = down_weight.shape[1]

    def run(act, down, out):
        for start in range(0, span, 128):
            out.ref[pl.ds(start, 128), :] = matmul(act.get()[pl.ds(start, 128), :], down.get()[...])
            out.put(start, 128)

    outs = [(shaped((span, width), f32), "h")]
    return staged(run, [(acts, "h"), (down_weight, "h")], outs, "feed_down")[0]


def finish_tokens(tokens, grad_resid, mine, other, gain):
    span, width = tokens.shape
    cuts = 4
    step = span // cuts

    def run(tok, grad_ref, mine_ref, other_ref, gain_ref, out):
        items = (tok, mine_ref, other_ref, grad_ref)
        for k in range(cuts):
            for item in items:
                item.start(k + 1)
        for k in range(cuts):
            rows = pl.ds(k * step, step)
            scaled, inverse = norm_rows(tok.get(k)[rows, :].astype(f32))
            grad = mine_ref.get(k)[rows, :] + other_ref.get(k)[rows, :]
            out.ref[rows, :] = grad_ref.get(k)[rows, :] + norm_back(grad, scaled, inverse, gain_ref[...])
            out.put(k * step, step)

    ins = [(tokens, cuts), (grad_resid, cuts), (mine, ("top", cuts)), (other, ("top", cuts)), (gain, "v")]
    return staged(run, ins, [(shaped((span, width), f32), "h")], "finish_tokens")[0]


def finish_layer(length, resid, mine, other, bias):
    span, width = resid.shape
    cuts = 4
    step = span // cuts

    def run(len_ref, resid_ref, a, b, bias_ref, out):
        for k in range(cuts):
            for item in (resid_ref, a, b):
                item.start(k + 1)
        for k in range(cuts):
            rows = pl.ds(k * step, step)
            value = resid_ref.get(k)[rows, :] + ((a.get(k)[rows, :] + b.get(k)[rows, :]) + bias_ref[...])
            out.ref[rows, :] = (row_mask(k * step, step, len_ref[0]) * value).astype(bf16)
            out.put(k * step, step)

    ins = [(length, "s"), (resid, cuts), (mine, cuts), (other, cuts), (bias, "v")]
    return staged(run, ins, [(shaped((span, width), bf16), "h")], "finish_layer")[0]


def halve(place, keeps, gots, cuts, rows, widths, theirs, before=None):
    n, n_cuts, n_out = len(keeps), len(cuts), len(widths)
    half = keeps[0].shape[0] // 2
    runs = [1 << cut[3] for cut in cuts]
    copies_each = [half // rows // size for size in runs]

    def run(place_ref, *refs):
        keep_refs, got_refs = refs[:n], refs[n : 2 * n]
        refs = refs[2 * n + (0 if before is None else n_out) :]
        outs, refs = refs[:n_out], refs[n_out:]
        sums, adds, sems = refs[:n_cuts], refs[n_cuts : 2 * n_cuts], refs[2 * n_cuts]
        waits, at = [], 0
        for i, (which, start, count, pos, bit, _, _) in enumerate(cuts):
            mine = (place_ref[0] >> bit) & 1
            side = 1 - mine if theirs else mine
            cols = pl.ds(start, count)
            waits.append([])
            for j in range(copies_each[i]):
                first = insert_bit(j * runs[i], pos, side) * rows
                source = pl.ds(pl.multiple_of(first, rows), runs[i] * rows)
                target = pl.ds(j * runs[i] * rows, runs[i] * rows)
                for array, held in ((keep_refs[which], sums[i]), (got_refs[which], adds[i])):
                    copy = pltpu.make_async_copy(array.at[source, cols], held.at[target], sems.at[at])
                    copy.start()
                    waits[i].append(copy)
                    at += 1
        copies = []
        for i, (_, _, count, _, _, out, start) in enumerate(cuts):
            for copy in waits[i]:
                copy.wait()
            sums[i][...] = sums[i][...] + adds[i][...]
            copies.append(pltpu.make_async_copy(sums[i], outs[out].at[:, pl.ds(start, count)], sems.at[at]))
            copies[-1].start()
            at += 1
        for copy in copies:
            copy.wait()

    ins = [(place, "s")] + [(x, "a") for x in (*keeps, *gots)]
    aliases = None
    if before is not None:
        aliases = {len(ins) + k: k for k in range(n_out)}
        ins += [(item, "a") for item in before]
    outs = [(shaped((half, w), f32), "a") for w in widths]
    scratch = [pltpu.VMEM((half, cut[2]), f32) for cut in cuts] * 2
    scratch.append(pltpu.SemaphoreType.DMA((2 * sum(copies_each) + n_cuts,)))
    return staged(run, ins, outs, "halve", scratch, aliases)


def pack_small(coef, rate, taps, skip, upbias, downbias, norms, norms_other):
    states, chans = coef.shape
    lags = taps.shape[0] // 8
    wide = [(upbias, None), (downbias, None)]
    counts = [states, states, lags, 1, upbias.shape[1] // chans, downbias.shape[1] // chans]
    counts.append(4 * (norms.shape[1] // chans))
    total = -(-sum(counts) // 16) * 16

    def run(coef_ref, rate_ref, taps_ref, skip_ref, up_ref, down_ref, norm_a, norm_b, out):
        out[...] = jnp.zeros_like(out)
        out[pl.ds(0, states), :] = coef_ref[...]
        out[pl.ds(states, states), :] = rate_ref[...]
        at = 2 * states

        def lay(value, at):
            row = jnp.sum(value, 0, keepdims=True)
            for start in range(0, row.shape[1], chans):
                out[pl.ds(at, 1), :] = row[:, start : start + chans]
                at += 1
            return at

        for lag in range(lags):
            at = lay(taps_ref[pl.ds(8 * lag, 8), :], at)
        at = lay(skip_ref[...], at)
        at = lay(up_ref[...], at)
        at = lay(down_ref[...], at)
        for start in range(0, 32, 8):
            rows = pl.ds(start, 8)
            at = lay(norm_a[rows, :] + norm_b[rows, :], at)

    ins = [coef, rate, taps, skip, upbias, downbias, norms, norms_other]
    ins = [(x, "v") for x in ins[:6]] + [(x, "t") for x in ins[6:]]
    out = staged(run, ins, [(shaped((total, chans), f32), "v")], "pack_small")[0]
    return out, counts


def unpack_small(place, bit, mine, other, counts, lags, hidden, width):
    half, chans = mine.shape

    def run(place_ref, a, b, coef, rate, taps, skip, up, down, *rest):
        norms, whole = rest[:-1], rest[-1]
        side = (place_ref[0] >> bit) & 1
        whole[pl.ds(pl.multiple_of(side * half, 8), half), :] = a[...]
        whole[pl.ds(pl.multiple_of((1 - side) * half, 8), half), :] = b[...]
        at = 0
        for out in (coef, rate, taps):
            out[...] = whole[pl.ds(at, out.shape[0]), :]
            at += out.shape[0]
        for out in (skip, up, down, *norms):
            for start in range(0, out.shape[1], chans):
                out[:, pl.ds(start, chans)] = whole[pl.ds(at, 1), :]
                at += 1

    states = counts[0]
    outs = [(shaped((n, chans), f32), "v") for n in (states, states, lags)]
    outs += [(shaped((n,), f32), "v") for n in (chans, hidden, width, width, width, width, width)]
    ins = [(place, "s"), (mine, "v"), (other, "v")]
    return staged(run, ins, outs, "unpack_small", [pltpu.VMEM((2 * half, chans), f32)])


def collect(keeps, gots, layout, sizes):
    n = len(keeps)
    rows = keeps[0].shape[0]
    names = list(sizes)

    def run(*refs):
        outs = dict(zip(names, refs[2 * n :]))
        for i in range(n):
            total = refs[i][...] + refs[n + i][...]
            at = 0
            for name, start, count in layout[i]:
                piece = total[:, at : at + count]
                if sizes[name][1]:
                    outs[name][pl.ds(start, count), :] = piece.T
                else:
                    outs[name][:, pl.ds(start, count)] = piece
                at += count

    outs = []
    for columns, turned in sizes.values():
        outs.append((shaped((columns, rows) if turned else (rows, columns), f32), "v"))
    res = staged(run, [(x, "v") for x in (*keeps, *gots)], outs, "collect")
    return dict(zip(names, res))


def state_grads(coef_t, rate_t, lag_grad):
    states, chans = coef_t.shape
    span = lag_grad.shape[0]
    step = 32
    blocks = span // step
    lanes = 128
    group = 8
    tiles = step // 8

    def run(coef_ref, rate_ref, lag_ref, coef_out, rate_out, fine, coarse, plain, place, ramp):
        rate = rate_ref[...][:, None, :]
        within = lax.broadcasted_iota(jnp.int32, (1, step, 1), 1).astype(f32)
        across = lax.broadcasted_iota(jnp.int32, (1, blocks, 1), 1).astype(f32)
        fine[...] = jnp.exp(-rate * within)
        coarse[...] = jnp.exp(-rate * (step * across))
        plain[...] = jnp.zeros_like(plain)
        place[...] = jnp.zeros_like(place)
        ramp[...] = jnp.zeros_like(ramp)
        for base in range(0, blocks, group):
            lag = [
                [
                    lag_ref[pl.ds((base + j) * step + 8 * a, 8), :]
                    for a in range(tiles)
                ]
                for j in range(group)
            ]

            def add(n, _):
                near = [fine[n, pl.ds(8 * a, 8), :] for a in range(tiles)]
                suffix = None
                later = None
                tilted = None
                for j in reversed(range(group)):
                    far = coarse[n, pl.ds(base + j, 1), :]
                    total = None
                    slope = None
                    for a in reversed(range(tiles)):
                        term = lag[j][a] * near[a]
                        if total is None:
                            total = term
                        else:
                            slope = total if slope is None else slope + total
                            total = total + term
                    weighted = far * total
                    bent = far * slope
                    tilted = bent if tilted is None else tilted + bent
                    if suffix is None:
                        suffix = weighted
                    else:
                        later = suffix if later is None else later + suffix
                        suffix = suffix + weighted
                plain[n] = plain[n] + suffix
                place[n] = place[n] + (later + float(base) * suffix)
                ramp[n] = ramp[n] + tilted
                return 0

            lax.fori_loop(0, states, add, 0, unroll=4)
        rows = lax.broadcasted_iota(jnp.int32, (1, 8, 1), 1).astype(f32)
        whole = plain[...]
        coef_out[...] = jnp.sum(whole, 1)
        times = float(step) * place[...] + 8.0 * ramp[...] + rows * whole
        rate_out[...] = -coef_ref[...] * jnp.sum(times, 1)

    shape = jax.ShapeDtypeStruct((states, chans), f32)
    block = pl.BlockSpec((states, lanes), lambda i: (0, i))
    return pl.pallas_call(
        run,
        grid=(chans // lanes,),
        in_specs=[block, block, pl.BlockSpec((span, lanes), lambda i: (0, i))],
        out_specs=[block, block],
        out_shape=[shape, shape],
        scratch_shapes=[
            pltpu.VMEM((states, step, lanes), f32),
            pltpu.VMEM((states, blocks, lanes), f32),
        ]
        + [pltpu.VMEM((states, 8, lanes), f32)] * 3,
        compiler_params=pltpu.CompilerParams(vmem_limit_bytes=most_vmem),
        cost_estimate=small_cost,
        name="state_grads",
    )(coef_t, rate_t, lag_grad)


def follow(values, *before):
    held = lax.optimization_barrier((list(values), before))[0]
    return held


def take_columns(cols, start, count):
    taken = []
    for name, first, columns in cols:
        low, high = max(start, 0), min(start + count, columns)
        if low < high:
            taken.append((name, first + low, high - low))
        start -= columns
    return taken


def body(
    tokens,
    lengths,
    mixgain,
    mixbias,
    query_weight,
    key_weight,
    value_weight,
    shift_taps,
    state_coef,
    state_rate,
    state_skip,
    out_weight,
    feedgain,
    feedbias,
    up_weight,
    up_bias,
    down_weight,
    down_bias,
    cotangent,
):
    assert lengths.shape[0] == 1
    span, width = tokens.shape
    chans = query_weight.shape[1]
    hidden = up_weight.shape[1]
    lags = shift_taps.shape[0]
    places = lax.axis_size("freq")
    halving = places == 16 and width % (16 * places) == 0
    groups = places if halving else 2
    rows = width // groups
    place = lax.axis_index("freq").astype(jnp.int32).reshape(1)
    third, part = hidden // 3, chans // 3
    feed_cols = [[("down", i * third, third), ("up", i * third, third)] for i in range(3)]
    mixer_cols = [
        [("out", 0, 3 * part), ("query", 0, part)],
        [("query", part, 2 * part), ("key", 0, 2 * part)],
        [("key", 2 * part, part), ("value", 0, 3 * part)],
    ]
    order_of = {"out": 0, "query": 1, "key": 2, "value": 3}
    pieces = [[(order_of[n], s, c) for n, s, c in cols] for cols in mixer_cols]
    thirds = [((i, 0), (i, third)) for i in range(3)]
    if halving:
        orders = [[(0, 1, 2, 3), (0, 1, 3, 2)], [(1, 2, 0, 3), (1, 3, 0, 2)], [(2, 0, 1, 3)]]
        bits = [order[0][0] for order in orders]
    else:
        place = jnp.zeros_like(place)
        bits = [0] * 3

    block = 256
    table_np = dft_table(block)
    table, table_t = jnp.asarray(table_np), jnp.asarray(np.ascontiguousarray(table_np.T))
    coef_t, rate_t = state_coef.T, state_rate.T

    normed, query, keypad, value, mixed, gated, sig16, ker16, out_part = mixer_forward(
        lengths,
        tokens,
        mixgain,
        mixbias,
        (query_weight, key_weight, value_weight),
        shift_taps,
        coef_t,
        rate_t,
        state_skip,
        out_weight,
        table,
        table_t,
    )
    out_other = swap(out_part, "tp", 0)
    down, down_t, normed_t, downbias_part = feed_prepare(lengths, cotangent, normed)
    down_t = down_t.reshape(groups, rows, span)
    normed_t = normed_t.reshape(groups, rows, span)
    (resid, acts, second_part, feed_sums, upbias_part), gives, keeps = feed_forward_back(
        place, out_part, out_other, feedgain, feedbias, down, down_t, up_weight, up_bias, down_weight, (bits, [2 * third] * 3, thirds)
    )
    second_other = swap(second_part, "tp", 0)
    if halving:
        gots = [swap(give, "freq", bit) for give, bit in zip(gives, bits)]
    (grad_resid, lag_grad, normed_part, skip_part, taps_part), more_gives, more_keeps = mixer_back(
        lengths, place, down, second_part, second_other, resid, feedgain, out_weight, mixed, query, sig16, ker16, table, table_t, state_skip,
        keypad, value, shift_taps, normed_t, gated, (query_weight, key_weight, value_weight), tokens, feed_sums, (bits, pieces)
    )
    (acts,) = follow([acts], normed_part)
    down_part = feed_down(acts, down_weight)
    if halving:

        items = []
        for source, all_cols in enumerate((feed_cols, mixer_cols)):
            for cols, some in zip(all_cols, orders):
                size = sum(count for _, _, count in cols) // len(some)
                for k, order in enumerate(some):
                    items.append((order, take_columns(cols, k * size, size), source))

        def arrange(step, source=None):
            arrays, starts = {}, {}
            for item in items:
                if source is None or item[2] == source:
                    arrays.setdefault(item[0][step], []).append(item)
            for some in arrays.values():
                at = 0
                for item in some:
                    starts[id(item)] = at
                    at += width_of(item)
            links = sorted(arrays)
            return links, [sum(map(width_of, arrays[link])) for link in links], arrays, starts

        def width_of(item):
            return sum(count for _, _, count in item[1])

        def cuts_to(step, source=None):
            links, _, _, starts = arrange(step - 1, source)
            next_links, widths, _, next_starts = arrange(step)
            cuts = []
            for item in items:
                if source is None or item[2] == source:
                    order = item[0]
                    pos = sorted(order[step:]).index(order[step])
                    cuts.append(
                        (
                            links.index(order[step - 1]),
                            starts[id(item)],
                            width_of(item),
                            pos,
                            order[step],
                            next_links.index(order[step]),
                            next_starts[id(item)],
                        )
                    )
            return cuts, rows, widths

        def exchange(gives, step):
            return [swap(give, "freq", link) for give, link in zip(gives, arrange(step)[0])]

        def add_swapped(value, bit):
            return value + swap(value, "freq", bit)

        gots = follow(gots, down_part)
        more_gives, lag_grad, normed_part, down_part = follow(
            [more_gives, lag_grad, normed_part, down_part], *gots
        )
        more_gots = exchange(more_gives, 0)
        held_gives = halve(place, keeps, gots, *cuts_to(1, 0), True)
        held_keeps = halve(place, keeps, gots, *cuts_to(1, 0), False)
    normed_other = swap(normed_part, "tp", 0)
    down_other = swap(down_part, "tp", 0)
    if halving:
        more_gots = follow(more_gots, normed_other, down_other, held_gives[0], held_keeps[0])
        gives = halve(place, more_keeps, more_gots, *cuts_to(1, 1), True, held_gives)
        gots = exchange(gives, 1)
        (lag_grad,) = follow([lag_grad], *gives)
    coef_part, rate_part = state_grads(coef_t, rate_t, lag_grad)
    small, counts = pack_small(
        coef_part, rate_part, taps_part, skip_part, upbias_part, downbias_part, normed_part, normed_other
    )
    if halving:
        half = small.shape[0] // 2
        side = place[0] & 1
        give = lax.dynamic_slice_in_dim(small, (1 - side) * half, half, 0)
        small = lax.dynamic_slice_in_dim(small, side * half, half, 0)
        other = swap(give, "freq", 0)
        (more_gots[0],) = follow([more_gots[0]], give)
        keeps = halve(place, more_keeps, more_gots, *cuts_to(1, 1), False, held_keeps)
        (other,) = follow([other], *keeps)
        old = follow(gots, other, small)
        gives = halve(place, keeps, old, *cuts_to(2), True)
        (small,) = follow([small], *gives)
        gots = exchange(gives, 2)
        small = small + other
        other = swap(small, "freq", 2)
        (down_part,) = follow([down_part], small)
        layer_out = finish_layer(lengths, resid, down_part, down_other, down_bias)
        (other,) = follow([other], layer_out)
        small = small + other
        other = swap(small, "freq", 3)
        (old[0],) = follow([old[0]], small)
        keeps = halve(place, keeps, old, *cuts_to(2), False)
        (other,) = follow([other], *keeps)
        small = small + other
        old = follow(gots, small, *keeps)
        gives = halve(place, keeps, old, *cuts_to(3), True)
        (small,) = follow([small], *gives)
        gots = exchange(gives, 3)
        other = swap(small, "freq", 1)
        (old[0],) = follow([old[0]], *gives)
        keeps = halve(place, keeps, old, *cuts_to(3), False)
        (other,) = follow([other], *keeps)
        small = small + other
        other = swap(small, "freq", 0)
        (normed_part,) = follow([normed_part], small)
        tokens_grad = finish_tokens(tokens, grad_resid, normed_part, normed_other, mixgain)
        (other,) = follow([other], tokens_grad)
        coef_sum, rate_sum, taps_sum, skip_sum, upbias_sum, downbias_sum, *norms = unpack_small(
            place, 0, small, other, counts, lags, hidden, width
        )
        gots = follow(gots, coef_sum)
        sizes = {"down": (hidden, False), "up": (hidden, False), "out": (chans, False)}
        sizes |= {name: (chans, False) for name in ("query", "key", "value")}
        links, _, arrays, _ = arrange(3)
        grads = collect(keeps, gots, [sum((item[1] for item in arrays[link]), []) for link in links], sizes)
    else:
        tokens_grad = finish_tokens(tokens, grad_resid, normed_part, normed_other, mixgain)
        layer_out = finish_layer(lengths, resid, down_part, down_other, down_bias)
        small = lax.psum(small, "freq")
        grads = {name: [] for name in ("down", "up", "out", "query", "key", "value")}
        for i in range(3):
            whole = jnp.concatenate(
                [
                    jnp.concatenate([keeps[i], more_keeps[i]], 1),
                    jnp.concatenate([gives[i], more_gives[i]], 1),
                ],
                0,
            )
            total = lax.psum_scatter(whole, "freq", scatter_dimension=0, tiled=True)
            at = 0
            for name, _, columns in feed_cols[i] + mixer_cols[i]:
                grads[name].append(total[:, at : at + columns])
                at += columns
        grads = {name: jnp.concatenate(some, 1) for name, some in grads.items()}
        cuts = np.cumsum(counts)
        coef_sum, rate_sum, taps_sum, skip_sum, upbias_sum, downbias_sum, norms, _ = jnp.split(small, cuts)
        norms = norms.reshape(4, width)
        skip_sum, upbias_sum, downbias_sum = [x.reshape(-1) for x in (skip_sum, upbias_sum, downbias_sum)]
    return (
        layer_out,
        tokens_grad,
        norms[0],
        norms[1],
        grads["query"],
        grads["key"],
        grads["value"],
        taps_sum,
        coef_sum.T,
        rate_sum.T,
        skip_sum,
        grads["out"].T,
        norms[2],
        norms[3],
        grads["up"],
        upbias_sum,
        grads["down"].T,
        downbias_sum,
    )


def solution(mesh):
    in_specs = (
        P("freq", None),
        P("freq"),
        P(),
        P(),
        P(None, "tp"),
        P(None, "tp"),
        P(None, "tp"),
        P(None, "tp"),
        P("tp", None),
        P("tp", None),
        P("tp"),
        P("tp", None),
        P(),
        P(),
        P(None, "tp"),
        P("tp"),
        P("tp", None),
        P(),
        P("freq", None),
    )
    out_specs = (
        P("freq", None),
        P("freq", None),
        P(),
        P(),
        P("freq", "tp"),
        P("freq", "tp"),
        P("freq", "tp"),
        P(None, "tp"),
        P("tp", None),
        P("tp", None),
        P("tp"),
        P("tp", "freq"),
        P(),
        P(),
        P("freq", "tp"),
        P("tp"),
        P("tp", "freq"),
        P(),
    )
    return jax.shard_map(body, mesh=mesh, in_specs=in_specs, out_specs=out_specs, check_vma=False)
```

```python
import math

import jax
import jax.numpy as jnp
import numpy as np
from jax import lax
from jax.experimental import pallas as pl
from jax.experimental.pallas import tpu as pltpu
from jax.sharding import PartitionSpec as P

f32 = jnp.float32
bf16 = jnp.bfloat16
in_vmem = pl.BlockSpec(memory_space=pltpu.VMEM)
in_smem = pl.BlockSpec(memory_space=pltpu.SMEM)
anywhere = pl.BlockSpec(memory_space=pl.ANY)
pad = 8
most_vmem = (64 << 20) - (128 << 10)
small_cost = pl.CostEstimate(flops=1, bytes_accessed=1, transcendentals=0)


def shaped(shape, dtype):
    return jax.ShapeDtypeStruct(shape, dtype)


def size_of(item):
    return math.prod(item.shape) * jnp.dtype(item.dtype).itemsize


def call(run, ins, outs, name, scratch=(), flops=0, moved=0, specs=None):
    held = sum(size_of(item) for item in (*ins, *outs, *scratch))
    return pl.pallas_call(
        run,
        in_specs=specs or [in_vmem] * len(ins),
        out_specs=[in_vmem] * len(outs),
        out_shape=outs,
        scratch_shapes=list(scratch),
        compiler_params=pltpu.CompilerParams(vmem_limit_bytes=held + (6 << 20)),
        cost_estimate=small_cost,
        name=name,
    )(*ins)


def matmul(left, right):
    return jnp.dot(left, right, preferred_element_type=f32)


def times_transposed(left, right):
    return lax.dot_general(left, right, (((1,), (1,)), ((), ())), preferred_element_type=f32)


def swap(value, axis, bit):
    size = lax.axis_size(axis)
    return lax.ppermute(value, axis, [(i, i ^ (1 << bit)) for i in range(size)])


def dft_table(block):
    bins = np.arange(block)[:, None].astype(np.int64)
    times = np.arange(block)[None, :].astype(np.int64)
    angle = (bins * times % (2 * block)) * (math.pi / block)
    table = np.concatenate([np.cos(angle), np.sin(angle)], 0)
    table[block] = 1 - 2 * (np.arange(block) % 2)
    return table.astype(jnp.bfloat16)


def iota(shape, dim):
    return lax.broadcasted_iota(jnp.int32, shape, dim)


def row_mask(first, count, length):
    return (iota((count, 1), 0) + first < length).astype(f32)


def insert_bit(index, pos, bit):
    low = index & ((1 << pos) - 1)
    return ((index >> pos) << (pos + 1)) | (bit << pos) | low


def norm_rows(value):
    mean = jnp.mean(value, -1, keepdims=True)
    centered = value - mean
    inverse = lax.rsqrt(jnp.mean(centered * centered, -1, keepdims=True) + 1e-05)
    return centered * inverse, inverse


def norm_back(grad_out, scaled, inverse, gain):
    weighted = grad_out * gain
    return inverse * (
        weighted
        - jnp.mean(weighted, -1, keepdims=True)
        - scaled * jnp.mean(weighted * scaled, -1, keepdims=True)
    )


def column_sum(value):
    rows, width = value.shape
    return jnp.sum(value.reshape(rows // 8, 8, width), 0)


def shift_conv(taps, keypad, start, count):
    lags = taps.shape[0]
    return sum(
        taps[lag : lag + 1, :] * keypad[pl.ds(start + pad - lag, count), :] for lag in range(lags)
    )


def edge(first, real, imag):
    return jnp.where(first, imag, real), jnp.where(first, 0.0, imag)


class Coming:
    def __init__(self, source, held, sems, cuts=1):
        self.held, self.started, self.here = held, 0, 0
        if source.shape[-2:] != held.shape[-2:] and len(source.shape) > 1 and cuts == 1:
            last = pl.ds(source.shape[0] - held.shape[0], held.shape[0])
            self.copies = [pltpu.make_async_copy(source.at[last], held, sems.at[0])]
            return
        if len(source.shape) == 1:
            self.copies = [pltpu.make_async_copy(source, held.at[0], sems.at[0])]
            return
        rows = held.shape[0] // cuts
        self.copies = []
        for i in range(cuts):
            part = pl.ds(i * rows, rows) if cuts > 1 else pl.ds(0, held.shape[0])
            self.copies.append(pltpu.make_async_copy(source.at[part], held.at[part], sems.at[i]))

    def start(self, cuts=None):
        cuts = len(self.copies) if cuts is None else cuts
        while self.started < cuts:
            self.copies[self.started].start()
            self.started += 1

    def get(self, cut=None):
        self.start(None if cut is None else cut + 1)
        until = len(self.copies) if cut is None else cut + 1
        while self.here < until:
            self.copies[self.here].wait()
            self.here += 1
        return self.held


class Going:
    def __init__(self, target, held, sems):
        self.target, self.ref, self.sems, self.copies = target, held, sems, []

    def put(self, start=0, count=None, source=None):
        rows = pl.ds(start, self.ref.shape[0] if count is None else count)
        sem = self.sems.at[len(self.copies)]
        if len(self.target.shape) == 1:
            copy = pltpu.make_async_copy(self.ref.at[0], self.target, sem)
        else:
            source = self.ref.at[rows] if source is None else source
            copy = pltpu.make_async_copy(source, self.target.at[rows], sem)
        copy.start()
        self.copies.append(copy)


    def put_columns(self, start, count):
        cols = pl.ds(start, count)
        sem = self.sems.at[len(self.copies)]
        copy = pltpu.make_async_copy(self.ref.at[:, cols], self.target.at[:, cols], sem)
        copy.start()
        self.copies.append(copy)


most_puts = 16
most_cuts = 4
in_hbm = pl.BlockSpec(memory_space=pl.ANY)


def staged(run, ins, outs, name, scratch=(), aliases=None):
    spec = {"s": in_smem}
    plain = ("s", "a")
    shared = lambda kind: isinstance(kind, str) and kind[0] == "="
    top = lambda kind: isinstance(kind, tuple)

    def tail(x, kind):
        if kind == "t" or top(kind):
            return shaped((32 if kind == "t" else x.shape[0] - 32, x.shape[1]), x.dtype)
        return x

    held = [tail(x, kind) for x, kind in (*ins, *outs) if kind not in plain and not shared(kind)]
    held = [shaped(x.shape if len(x.shape) > 1 else (1, *x.shape), x.dtype) for x in held]
    n_in = sum(kind not in plain for _, kind in ins)
    n_out = sum(kind not in plain for _, kind in outs)

    def whole(*refs):
        refs = list(refs)
        given, made = refs[: len(ins)], refs[len(ins) : len(ins) + len(outs)]
        rest = refs[len(ins) + len(outs) :]
        own, bufs = rest[: len(scratch)], rest[len(scratch) :]
        in_sems, out_sems = bufs[-2:]
        bufs = list(bufs[:-2])
        views, at = [], 0
        for ref, (_, kind) in zip(given, ins):
            if kind not in plain:
                cuts = kind[1] if top(kind) else kind if isinstance(kind, int) else 1
                views.append(Coming(ref, bufs.pop(0), in_sems.at[at], cuts))
                at += 1
                if kind != "l" and cuts == 1:
                    views[-1].start()
            else:
                views.append(ref)
        going, at = [], 0
        for ref, (_, kind) in zip(made, outs):
            if kind not in plain:
                held_at = views[int(kind[1:])].held if shared(kind) else bufs.pop(0)
                going.append(Going(ref, held_at, out_sems.at[at]))
                at += 1
            else:
                going.append(ref)
        for view, (_, kind) in zip(views, ins):
            if kind in ("v", "t"):
                view.get()
        views = [view.held if kind in ("v", "t") else view for view, (_, kind) in zip(views, ins)]
        small = [item for item, (_, kind) in zip(going, outs) if kind == "v"]
        run(*views, *[item.ref if item in small else item for item in going], *own)
        for item in small:
            item.put()
        for view in views:
            if isinstance(view, Coming):
                view.get()
        for item in going:
            if isinstance(item, Going):
                for copy in item.copies:
                    copy.wait()

    return pl.pallas_call(
        whole,
        in_specs=[spec.get(kind, in_hbm) for _, kind in ins],
        out_specs=[spec.get(kind, in_hbm) for _, kind in outs],
        out_shape=[item for item, _ in outs],
        scratch_shapes=list(scratch)
        + [pltpu.VMEM(x.shape, x.dtype) for x in held]
        + [
            pltpu.SemaphoreType.DMA((max(n_in, 1), most_cuts)),
            pltpu.SemaphoreType.DMA((max(n_out, 1), most_puts)),
        ],
        input_output_aliases=aliases or {},
        compiler_params=pltpu.CompilerParams(vmem_limit_bytes=most_vmem),
        cost_estimate=small_cost,
        name=name,
    )(*[x for x, _ in ins])


def split_products(place_ref, bit, source, chosen, pairs, give, keep):
    groups, rows, _ = source.shape
    mine = (place_ref[0] >> bit) & 1
    for k, (out, side) in enumerate(((give, 1 - mine), (keep, mine))):
        for j in range(groups // 2):
            chosen[k, pl.ds(j * rows, rows), :] = source[insert_bit(j, bit, side)]
    for k, out in enumerate((give, keep)):
        for right, start, count, to in pairs:
            out[:, pl.ds(to, count)] = matmul(chosen[k], right[:, pl.ds(start, count)])


def mixer_forward(length, tokens, gain, bias, weights, taps, coef_t, rate_t, skip, out_weight, table, table_t):
    span, width = tokens.shape
    chans = out_weight.shape[0]
    states = coef_t.shape[0]
    block = table.shape[1]
    count = span // block
    step = 32
    far_steps = span // step
    group = 8
    lanes = 128

    def run(
        len_ref, tok, gain_ref, bias_ref, wq, wk, wv, taps_ref, coef_ref, rate_ref, skip_ref, wo, tab, tab_t,
        normed_o, query_o, keypad_o, value_o, mixed_o, gated_o, sig_o, ker_o, part_o,
        fine, coarse, signal, sig_bins, ker_bins, prod, query, value,
    ):
        size = len_ref[0]
        normed, keypad = normed_o.ref, keypad_o.ref
        sig16, ker16 = sig_o.ref, ker_o.ref

        within = iota((1, step, 1), 1).astype(f32)
        across = iota((1, group, 1), 1).astype(f32) * float(step)
        rate = rate_ref[...][:, None, :]
        fine[...] = jnp.exp(-rate * within)
        for k in range(far_steps // group):
            coarse[:, k] = coef_ref[...][:, None, :] * jnp.exp(-rate * (across + float(step * group * k)))
        keypad[pl.ds(0, pad), :] = jnp.zeros((pad, chans), f32)
        tok_ref, wq_ref, wk_ref, wv_ref = tok.get(), wq.get(), wk.get(), wv.get()
        for item in (wo, tab, tab_t):
            item.start()

        for i in range(count):
            rows = pl.ds(i * block, block)
            scaled, _ = norm_rows(tok_ref[rows, :].astype(f32))
            norm = (scaled * gain_ref[...] + bias_ref[...]).astype(bf16)
            normed[rows, :] = norm
            query[rows, :] = matmul(norm, wq_ref[...])
            query_o.ref[rows, :] = query[rows, :].astype(bf16)
            keypad[pl.ds(i * block + pad, block), :] = matmul(norm, wk_ref[...])
            value[rows, :] = matmul(norm, wv_ref[...])
            value_o.ref[rows, :] = value[rows, :].astype(bf16)
        for i in range(count):
            rows = pl.ds(i * block, block)
            shifted = shift_conv(taps_ref, keypad, i * block, block)
            sig = row_mask(i * block, block, size) * shifted * value[rows, :]
            signal[rows, :] = sig
            sig16[rows, :] = sig.astype(bf16)
            sig_bins[pl.ds(i * 2 * block, 2 * block), :] = matmul(tab.get()[...], sig16[rows, :])
        for item in (normed_o, query_o, keypad_o, value_o, sig_o):
            item.put()

        def some_taps(u, _):
            i = u // (chans // lanes)
            cols = pl.ds(pl.multiple_of((u - i * (chans // lanes)) * lanes, lanes), lanes)
            sums = [None] * group
            for n in range(states):
                near = fine[n, :, cols]
                for j in range(group):
                    term = coarse[n, i, pl.ds(j, 1), cols] * near
                    sums[j] = term if n == 0 else sums[j] + term
            for j in range(group):
                place = pl.ds(pl.multiple_of(i * block + j * step, step), step)
                ker16[place, cols] = sums[j].astype(bf16)
            return 0

        lax.fori_loop(0, far_steps // group * (chans // lanes), some_taps, 0)
        ker_o.put()
        sign = 1.0 - 2.0 * (iota((2 * block, 1), 0) % 2).astype(f32)
        before = None
        for i in range(count):
            ker = matmul(tab.get()[...], ker16[pl.ds(i * block, block), :])
            ker_bins[pl.ds(i * 2 * block, 2 * block), :] = ker if before is None else ker + sign * before
            before = ker

        def product(i, _):
            start = pl.multiple_of(i * 16, 16)
            first = (iota((16, 1), 0) + start) == 0
            scale = jnp.where(first, 0.5 / block, 1.0 / block)
            for lane in range(0, chans, lanes):
                cols = pl.ds(lane, lanes)

                def pair(ref, j):
                    return (
                        ref[pl.ds(j * 2 * block + start, 16), cols],
                        ref[pl.ds(j * 2 * block + block + start, 16), cols],
                    )

                sigs = [pair(sig_bins, j) for j in range(count)]
                kers = []
                for j in range(count):
                    c, d = pair(ker_bins, j)
                    other, d = edge(first, c, d)
                    kers.append((c, other, d))
                for j in range(count):
                    real = imag = None
                    for m in range(j + 1):
                        a, b = sigs[m]
                        c, other, d = kers[j - m]
                        r = a * c - b * d
                        s = a * d + b * other
                        real = r if real is None else real + r
                        imag = s if imag is None else imag + s
                    prod[pl.ds(j * 2 * block + start, 16), cols] = (real * scale).astype(bf16)
                    prod[pl.ds(j * 2 * block + block + start, 16), cols] = (imag * scale).astype(bf16)
            return 0

        lax.fori_loop(0, block // 16, product, 0)
        for i in range(count):
            rows = pl.ds(i * block, block)
            conv = matmul(tab_t.get()[...], prod[pl.ds(i * 2 * block, 2 * block), :])
            mixed = conv + skip_ref[...] * signal[rows, :]
            mixed_o.ref[rows, :] = mixed.astype(bf16)
            gated = (row_mask(i * block, block, size) * query[rows, :] * mixed).astype(bf16)
            gated_o.ref[rows, :] = gated
            part_o.ref[rows, :] = matmul(gated, wo.get()[...]) + 0.5 * tok_ref[rows, :].astype(f32)
            for item in (part_o, mixed_o, gated_o):
                item.put(i * block, block)

    outs = [
        (shaped((span, width), bf16), "h"),
        (shaped((span, chans), bf16), "h"),
        (shaped((span + pad, chans), f32), "h"),
        (shaped((span, chans), bf16), "h"),
        (shaped((span, chans), bf16), "h"),
        (shaped((span, chans), bf16), "h"),
        (shaped((span, chans), bf16), "h"),
        (shaped((span, chans), bf16), "h"),
        (shaped((span, width), f32), "h"),
    ]
    scratch = [
        pltpu.VMEM((states, step, chans), f32),
        pltpu.VMEM((states, far_steps // group, group, chans), f32),
        pltpu.VMEM((span, chans), f32),
        pltpu.VMEM((2 * span, chans), f32),
        pltpu.VMEM((2 * span, chans), f32),
        pltpu.VMEM((2 * span, chans), bf16),
        pltpu.VMEM((span, chans), f32),
        pltpu.VMEM((span, chans), f32),
    ]
    ins = [(length, "s"), (tokens, "h"), (gain, "v"), (bias, "v")]
    ins += [(weight, "h") for weight in weights]
    ins += [(taps, "v"), (coef_t, "v"), (rate_t, "v"), (skip, "v")]
    ins += [(out_weight, "l"), (table, "l"), (table_t, "l")]
    return staged(run, ins, outs, "mixer_forward", scratch)


def norm_sums(grad, value, start, gain_sum, bias_sum):
    rows = pl.ds(start, 128)
    scaled, _ = norm_rows(value[rows, :].astype(f32))
    part = grad[rows, :]
    return gain_sum + column_sum(part * scaled), bias_sum + column_sum(part)


def feed_prepare(length, cotangent, normed):
    span, width = cotangent.shape

    def run(len_ref, cot, normed_ref, down_o, down_t, normed_t, sums):
        size = len_ref[0]
        total = jnp.zeros((8, width), f32)
        for start in range(0, span, 256):
            rows = pl.ds(start, 256)
            grad = row_mask(start, 256, size) * cot.get()[rows, :].astype(f32)
            total = total + column_sum(grad)
            down_o.ref[rows, :] = grad.astype(bf16)
            down_o.put(start, 256)
            down_t.ref[:, rows] = grad.astype(bf16).T
        down_t.put()
        for start in range(0, span, 256):
            rows = pl.ds(start, 256)
            normed_t.ref[:, rows] = normed_ref.get()[rows, :].T
        normed_t.put()
        sums[...] = total

    outs = [
        (shaped((span, width), bf16), "h"),
        (shaped((width, span), bf16), "h"),
        (shaped((width, span), bf16), "h"),
        (shaped((8, width), f32), "v"),
    ]
    return staged(run, [(length, "s"), (cotangent, "h"), (normed, "h")], outs, "feed_prepare")


def feed_forward_back(place, mine, other, gain, bias, down, down_t, up_weight, up_bias, down_weight, cuts):
    span, width = mine.shape
    hidden = up_weight.shape[1]
    groups, rows_each, _ = down_t.shape
    half = width // 2
    bits, widths, thirds = cuts
    size = hidden // 3
    parts = len(bits)
    step = 256

    def run(*refs):
        place_ref, mine_ref, other_ref, gain_ref, bias_ref, dn, dn_t, up, upb, dw = refs[:10]
        resid_o, acts_o, part_o, sums, upb_sums = refs[10:15]
        gives, keeps = refs[15 : 15 + parts], refs[15 + parts : 15 + 2 * parts]
        second, second_t, grad_hid, hid_a, hid_b, pre_a, pre_b, hat, chosen_a, chosen_b = refs[15 + 2 * parts :]
        resid, acts = resid_o.ref, acts_o.ref
        cuts = span // step
        for k in range(cuts):
            for item in (mine_ref, other_ref):
                item.start(k + 1)
        for item in (up, dw, dn, dn_t):
            item.start()
        for k in range(cuts):
            rows = pl.ds(k * step, step)
            value = mine_ref.get(k)[rows, :] + other_ref.get(k)[rows, :]
            resid[rows, :] = value
            scaled, _ = norm_rows(value)
            hat[rows, :] = scaled
            norm = (scaled * gain_ref[...] + bias_ref[...]).astype(bf16)
            second[rows, :] = norm
            turned = norm.T
            for j in range(groups):
                second_t[j, :, rows] = turned[j * rows_each : (j + 1) * rows_each, :]
        up_ref, dw_ref, dn_ref = up.get(), dw.get(), dn.get()
        resid_o.put()
        slots = [(hid_a, pre_a), (hid_b, pre_b)]

        def rise(i, k):
            rows, cols = pl.ds(k * step, step), pl.ds(i * size, size)
            hid, pre = slots[k % 2]
            hid[...] = matmul(second[rows, :], up_ref[:, cols])
            pre[...] = times_transposed(dn_ref[rows, :], dw_ref[cols, :])

        def gelu(i, k):
            rows, cols = pl.ds(k * step, step), pl.ds(i * size, size)
            hid, pre = slots[k % 2]
            h = hid[...] + upb[:, cols]
            cdf = 0.5 + 0.5 * lax.erf(h * (1.0 / math.sqrt(2.0)))
            slope = cdf + h * jnp.exp(-0.5 * h * h) * (1.0 / math.sqrt(2.0 * math.pi))
            acts[rows, cols] = (h * cdf).astype(bf16)
            grad = (pre[...] * slope).astype(bf16)
            grad_hid[rows, cols] = grad
            return column_sum(grad.astype(f32))

        for i in range(3):
            total = jnp.zeros((8, size), f32)
            rise(i, 0)
            for k in range(cuts):
                if k + 1 < cuts:
                    rise(i, k + 1)
                total = total + gelu(i, k)
            upb_sums[:, pl.ds(i * size, size)] = total
            (down_part, down_at), (up_part, up_at) = thirds[i]
            for source, chosen, right, (which, at) in (
                (dn_t.get(), chosen_a, acts, (down_part, down_at)),
                (second_t, chosen_b, grad_hid, (up_part, up_at)),
            ):
                split_products(
                    place_ref, bits[which], source, chosen, [(right, i * size, size, at)], gives[which].ref, keeps[which].ref
                )
            for which in sorted({down_part, up_part}):
                gives[which].put()
                keeps[which].put()
            acts_o.put_columns(i * size, size)
        gain_sum = jnp.zeros((8, width), f32)
        bias_sum = jnp.zeros((8, width), f32)
        for k in range(cuts + 1):
            if k < cuts:
                rows = pl.ds(k * step, step)
                part_o.ref[rows, :] = times_transposed(grad_hid[rows, :], up_ref[...])
                part_o.put(k * step, step)
            if k:
                rows = pl.ds((k - 1) * step, step)
                part = part_o.ref[rows, :]
                gain_sum = gain_sum + column_sum(part * hat[rows, :])
                bias_sum = bias_sum + column_sum(part)
        sums[pl.ds(0, 8), :] = gain_sum
        sums[pl.ds(8, 8), :] = bias_sum

    outs = [
        (shaped((span, width), f32), "h"),
        (shaped((span, hidden), bf16), "h"),
        (shaped((span, width), f32), "h"),
        (shaped((16, width), f32), "v"),
        (shaped((8, hidden), f32), "v"),
    ]
    outs += [(shaped((half, w), f32), "h") for w in widths] * 2
    scratch = [
        pltpu.VMEM((span, width), bf16),
        pltpu.VMEM((groups, rows_each, span), bf16),
        pltpu.VMEM((span, hidden), bf16),
        pltpu.VMEM((step, size), f32),
        pltpu.VMEM((step, size), f32),
        pltpu.VMEM((step, size), f32),
        pltpu.VMEM((step, size), f32),
        pltpu.VMEM((span, width), f32),
        pltpu.VMEM((2, half, span), bf16),
        pltpu.VMEM((2, half, span), bf16),
    ]
    cut = span // step
    ins = [(place, "s"), (mine, cut), (other, cut), (gain, "v"), (bias, "v")]
    ins += [(down, "l"), (down_t, "l"), (up_weight, "l"), (up_bias, "v"), (down_weight, "l")]
    res = staged(run, ins, outs, "feed_forward_back", scratch)
    return res[:5], res[5 : 5 + parts], res[5 + parts :]


def mixer_back(
    length, place, down, mine, other, resid, feedgain, out_weight, mixed, query, sig16, ker16, table, table_t, skip,
    keypad, value, taps, normed_t, gated, weights, tokens, feed_sums, cuts,
):
    span, width = resid.shape
    chans = query.shape[1]
    groups, rows_each, _ = normed_t.shape
    half = width // 2
    block = table.shape[1]
    count = span // block
    lags = taps.shape[0]
    lanes = 128
    bits, pieces = cuts
    widths = [sum(n for _, _, n in part) for part in pieces]
    parts = len(bits)

    def run(*refs):
        len_ref, place_ref, dn, mine_ref, other_ref, resid_ref, gain_ref, wo, mixed_ref, query_ref = refs[:10]
        sig_ref, ker_ref, tab, tab_t, skip_ref, key, value_ref, taps_ref, norm_t, gated_ref = refs[10:20]
        wq, wk, wv, tok, feed_ref = refs[20:25]
        grad_resid_o, lag_o, part_o, skip_sums, taps_sums = refs[25:30]
        gives, keeps = refs[30 : 30 + parts], refs[30 + parts : 30 + 2 * parts]
        grad_mix, mix_t, mix_grad, bins, sigs, kers, back_prod, lag_prod, shifted_grad, shifted, grads, chosen, mix_sums, all_weights = refs[30 + 2 * parts :]
        size = len_ref[0]
        grad_resid = grad_resid_o.ref
        grad_query, grad_key, grad_value = [pl.ds(k * chans, chans) for k in range(3)]

        for item in (tab, sig_ref, ker_ref):
            item.start()
        for i in range(count):
            for item in (dn, mine_ref, other_ref, resid_ref):
                item.start(i + 1)
        before = None
        turn = 1.0 - 2.0 * (iota((2 * block, 1), 0) % 2).astype(f32)
        for i in range(count):
            rows, bin_rows = pl.ds(i * block, block), pl.ds(i * 2 * block, 2 * block)
            sigs[bin_rows, :] = matmul(tab.get()[...], sig_ref.get()[rows, :])
            ker = matmul(tab.get()[...], ker_ref.get()[rows, :])
            kers[bin_rows, :] = ker if before is None else ker + turn * before
            before = ker
        for i in range(count):
            rows = pl.ds(i * block, block)
            scaled, inverse = norm_rows(resid_ref.get(i)[rows, :])
            grad = norm_back(mine_ref.get(i)[rows, :] + other_ref.get(i)[rows, :], scaled, inverse, gain_ref[...])
            grad = dn.get(i)[rows, :].astype(f32) + grad
            if i == 0:
                for item in (wo, query_ref, mixed_ref, key, value_ref):
                    item.start()
            grad_resid[rows, :] = grad
            grad = grad.astype(bf16)
            grad_mix[rows, :] = grad
            turned = grad.T
            for j in range(groups):
                mix_t[j, :, rows] = turned[j * rows_each : (j + 1) * rows_each, :]
        keypad, val = key.get(), value_ref.get()
        for item in (tab_t, norm_t, gated_ref):
            item.start()
        total = jnp.zeros((8, chans), f32)
        for i in range(count):
            rows, bin_rows = pl.ds(i * block, block), pl.ds(i * 2 * block, 2 * block)
            mask = row_mask(i * block, block, size)
            grad_gated = mask * times_transposed(grad_mix[rows, :], wo.get()[...])
            grads[rows, grad_query] = (grad_gated * mixed_ref.get()[rows, :]).astype(bf16)
            grad = grad_gated * query_ref.get()[rows, :]
            mix_grad[rows, :] = grad
            moved = shift_conv(taps_ref, keypad, i * block, block)
            shifted[rows, :] = moved
            total = total + column_sum(grad * (mask * moved * val[rows, :]))
            bins[bin_rows, :] = matmul(tab.get()[...], grad.astype(bf16))
        skip_sums[...] = total
        grad_resid_o.put()
        for item in (wq, wk, wv, tok):
            item.start()

        def product(i, _):
            start = pl.multiple_of(i * 16, 16)
            row = iota((16, 1), 0) + start
            first = row == 0
            scale = jnp.where(first, 0.5 / block, 1.0 / block)
            sign = 1.0 - 2.0 * (row % 2).astype(f32)
            for lane in range(0, chans, lanes):
                cols = pl.ds(lane, lanes)

                def pair(ref, j):
                    return (
                        ref[pl.ds(j * 2 * block + start, 16), cols],
                        ref[pl.ds(j * 2 * block + block + start, 16), cols],
                    )

                def put(ref, j, real, imag):
                    ref[pl.ds(j * 2 * block + start, 16), cols] = (real * scale).astype(bf16)
                    ref[pl.ds(j * 2 * block + block + start, 16), cols] = (imag * scale).astype(bf16)

                grad_pairs = [pair(bins, j) for j in range(count)]

                def correlate(ref, pairs):
                    real = imag = None
                    for g, j in pairs:
                        a, b = grad_pairs[g]
                        c, d = pair(ref, j)
                        other, d = edge(first, c, d)
                        r = a * c + b * d
                        s = b * other - a * d
                        real = r if real is None else real + r
                        imag = s if imag is None else imag + s
                    return real, imag

                for j in range(count):
                    real, imag = correlate(kers, [(m, m - j) for m in range(j, count)])
                    put(back_prod, j, real, imag)
                later = None
                for j in reversed(range(count)):
                    real, imag = correlate(sigs, [(m + j, m) for m in range(count - j)])
                    if later is None:
                        put(lag_prod, j, real, imag)
                    else:
                        put(lag_prod, j, real + sign * later[0], imag + sign * later[1])
                    later = (real, imag)
            return 0

        lax.fori_loop(0, block // 16, product, 0)
        shifted_grad[pl.ds(span, pad), :] = jnp.zeros((pad, chans), f32)
        totals = [jnp.zeros((8, chans), f32)] * lags
        for i in range(count):
            rows = pl.ds(i * block, block)
            bin_rows = pl.ds(i * 2 * block, 2 * block)
            mask = row_mask(i * block, block, size)
            signal_grad = matmul(tab_t.get()[...], back_prod[bin_rows, :])
            lag_o.ref[rows, :] = matmul(tab_t.get()[...], lag_prod[bin_rows, :])
            signal_grad = mask * (signal_grad + skip_ref[...] * mix_grad[rows, :])
            grads[rows, grad_value] = (signal_grad * shifted[rows, :]).astype(bf16)
            shifted_grad[rows, :] = signal_grad * val[rows, :]
        lag_o.put()
        for i in range(count):
            rows = pl.ds(i * block, block)
            here = keypad[pl.ds(i * block + pad, block), :]
            grad = None
            for lag in range(lags):
                moved = shifted_grad[pl.ds(i * block + lag, block), :]
                totals[lag] = totals[lag] + column_sum(moved * here)
                term = taps_ref[lag : lag + 1, :] * moved
                grad = term if grad is None else grad + term
            grads[rows, grad_key] = grad.astype(bf16)
        for lag in range(lags):
            taps_sums[pl.ds(lag * 8, 8), :] = totals[lag]

        for i in range(parts):
            at, pairs = 0, ([], [])
            for which, start, n in pieces[i]:
                if which == 0:
                    pairs[0].append((gated_ref.get(), start, n, at))
                else:
                    pairs[1].append((grads, (which - 1) * chans + start, n, at))
                at += n
            for source, some in ((mix_t, pairs[0]), (norm_t.get(), pairs[1])):
                if some:
                    split_products(place_ref, bits[i], source, chosen, some, gives[i].ref, keeps[i].ref)
            gives[i].put()
            keeps[i].put()

        gain_sum = jnp.zeros((8, width), f32)
        bias_sum = jnp.zeros((8, width), f32)
        for k, w in enumerate((wq, wk, wv)):
            all_weights[:, pl.ds(k * chans, chans)] = w.get()[...]
        for i in range(count + 1):
            if i < count:
                rows = pl.ds(i * block, block)
                part_o.ref[rows, :] = times_transposed(grads[rows, :], all_weights[...])
                part_o.put(i * block, block)
            if i:
                rows = pl.ds((i - 1) * block, block)
                scaled, _ = norm_rows(tok.get()[rows, :].astype(f32))
                part = part_o.ref[rows, :]
                gain_sum = gain_sum + column_sum(part * scaled)
                bias_sum = bias_sum + column_sum(part)
        mix_sums[pl.ds(0, 8), :] = gain_sum
        mix_sums[pl.ds(8, 8), :] = bias_sum
        mix_sums[pl.ds(16, 16), :] = feed_ref[...]
        part_o.put(span, 32, mix_sums)

    outs = [
        (shaped((span, width), f32), "=5"),
        (shaped((span, chans), f32), "h"),
        (shaped((span + 32, width), f32), "=3"),
        (shaped((8, chans), f32), "v"),
        (shaped((8 * lags, chans), f32), "v"),
    ]
    outs += [(shaped((half, w), f32), "h") for w in widths] * 2
    scratch = [
        pltpu.VMEM((span, width), bf16),
        pltpu.VMEM((groups, rows_each, span), bf16),
        pltpu.VMEM((span, chans), f32),
        pltpu.VMEM((2 * span, chans), f32),
        pltpu.VMEM((2 * span, chans), f32),
        pltpu.VMEM((2 * span, chans), f32),
        pltpu.VMEM((2 * span, chans), bf16),
        pltpu.VMEM((2 * span, chans), bf16),
        pltpu.VMEM((span + pad, chans), f32),
        pltpu.VMEM((span, chans), f32),
        pltpu.VMEM((span, 3 * chans), bf16),
        pltpu.VMEM((2, half, span), bf16),
        pltpu.VMEM((32, width), f32),
        pltpu.VMEM((width, 3 * chans), bf16),
    ]
    ins = [(length, "s"), (place, "s"), (down, count), (mine, count), (other, count), (resid, count), (feedgain, "v")]
    ins += [(x, "l") for x in (out_weight, mixed, query, sig16, ker16, table, table_t)] + [(skip, "v")]
    ins += [(keypad, "l"), (value, "l"), (taps, "v"), (normed_t, "l"), (gated, "l")]
    ins += [(weight, "l") for weight in weights] + [(tokens, "l"), (feed_sums, "v")]
    res = staged(run, ins, outs, "mixer_back", scratch)
    return res[:5], res[5 : 5 + parts], res[5 + parts :]


def feed_down(acts, down_weight):
    span = acts.shape[0]
    width = down_weight.shape[1]

    def run(act, down, out):
        for start in range(0, span, 128):
            out.ref[pl.ds(start, 128), :] = matmul(act.get()[pl.ds(start, 128), :], down.get()[...])
            out.put(start, 128)

    outs = [(shaped((span, width), f32), "h")]
    return staged(run, [(acts, "h"), (down_weight, "h")], outs, "feed_down")[0]


def finish_tokens(tokens, grad_resid, mine, other, gain):
    span, width = tokens.shape
    cuts = 4
    step = span // cuts

    def run(tok, grad_ref, mine_ref, other_ref, gain_ref, out):
        items = (tok, mine_ref, other_ref, grad_ref)
        for k in range(cuts):
            for item in items:
                item.start(k + 1)
        for k in range(cuts):
            rows = pl.ds(k * step, step)
            scaled, inverse = norm_rows(tok.get(k)[rows, :].astype(f32))
            grad = mine_ref.get(k)[rows, :] + other_ref.get(k)[rows, :]
            out.ref[rows, :] = grad_ref.get(k)[rows, :] + norm_back(grad, scaled, inverse, gain_ref[...])
            out.put(k * step, step)

    ins = [(tokens, cuts), (grad_resid, cuts), (mine, ("top", cuts)), (other, ("top", cuts)), (gain, "v")]
    return staged(run, ins, [(shaped((span, width), f32), "h")], "finish_tokens")[0]


def finish_layer(length, resid, mine, other, bias):
    span, width = resid.shape
    cuts = 4
    step = span // cuts

    def run(len_ref, resid_ref, a, b, bias_ref, out):
        for k in range(cuts):
            for item in (resid_ref, a, b):
                item.start(k + 1)
        for k in range(cuts):
            rows = pl.ds(k * step, step)
            value = resid_ref.get(k)[rows, :] + ((a.get(k)[rows, :] + b.get(k)[rows, :]) + bias_ref[...])
            out.ref[rows, :] = (row_mask(k * step, step, len_ref[0]) * value).astype(bf16)
            out.put(k * step, step)

    ins = [(length, "s"), (resid, cuts), (mine, cuts), (other, cuts), (bias, "v")]
    return staged(run, ins, [(shaped((span, width), bf16), "h")], "finish_layer")[0]


def halve(place, keeps, gots, cuts, rows, widths, theirs, before=None):
    n, n_cuts, n_out = len(keeps), len(cuts), len(widths)
    half = keeps[0].shape[0] // 2
    runs = [1 << cut[3] for cut in cuts]
    copies_each = [half // rows // size for size in runs]

    def run(place_ref, *refs):
        keep_refs, got_refs = refs[:n], refs[n : 2 * n]
        refs = refs[2 * n + (0 if before is None else n_out) :]
        outs, refs = refs[:n_out], refs[n_out:]
        sums, adds, sems = refs[:n_cuts], refs[n_cuts : 2 * n_cuts], refs[2 * n_cuts]
        waits, at = [], 0
        for i, (which, start, count, pos, bit, _, _) in enumerate(cuts):
            mine = (place_ref[0] >> bit) & 1
            side = 1 - mine if theirs else mine
            cols = pl.ds(start, count)
            waits.append([])
            for j in range(copies_each[i]):
                first = insert_bit(j * runs[i], pos, side) * rows
                source = pl.ds(pl.multiple_of(first, rows), runs[i] * rows)
                target = pl.ds(j * runs[i] * rows, runs[i] * rows)
                for array, held in ((keep_refs[which], sums[i]), (got_refs[which], adds[i])):
                    copy = pltpu.make_async_copy(array.at[source, cols], held.at[target], sems.at[at])
                    copy.start()
                    waits[i].append(copy)
                    at += 1
        copies = []
        for i, (_, _, count, _, _, out, start) in enumerate(cuts):
            for copy in waits[i]:
                copy.wait()
            sums[i][...] = sums[i][...] + adds[i][...]
            copies.append(pltpu.make_async_copy(sums[i], outs[out].at[:, pl.ds(start, count)], sems.at[at]))
            copies[-1].start()
            at += 1
        for copy in copies:
            copy.wait()

    ins = [(place, "s")] + [(x, "a") for x in (*keeps, *gots)]
    aliases = None
    if before is not None:
        aliases = {len(ins) + k: k for k in range(n_out)}
        ins += [(item, "a") for item in before]
    outs = [(shaped((half, w), f32), "a") for w in widths]
    scratch = [pltpu.VMEM((half, cut[2]), f32) for cut in cuts] * 2
    scratch.append(pltpu.SemaphoreType.DMA((2 * sum(copies_each) + n_cuts,)))
    return staged(run, ins, outs, "halve", scratch, aliases)


def pack_small(coef, rate, taps, skip, upbias, downbias, norms, norms_other):
    states, chans = coef.shape
    lags = taps.shape[0] // 8
    wide = [(upbias, None), (downbias, None)]
    counts = [states, states, lags, 1, upbias.shape[1] // chans, downbias.shape[1] // chans]
    counts.append(4 * (norms.shape[1] // chans))
    total = -(-sum(counts) // 16) * 16

    def run(coef_ref, rate_ref, taps_ref, skip_ref, up_ref, down_ref, norm_a, norm_b, out):
        out[...] = jnp.zeros_like(out)
        out[pl.ds(0, states), :] = coef_ref[...]
        out[pl.ds(states, states), :] = rate_ref[...]
        at = 2 * states

        def lay(value, at):
            row = jnp.sum(value, 0, keepdims=True)
            for start in range(0, row.shape[1], chans):
                out[pl.ds(at, 1), :] = row[:, start : start + chans]
                at += 1
            return at

        for lag in range(lags):
            at = lay(taps_ref[pl.ds(8 * lag, 8), :], at)
        at = lay(skip_ref[...], at)
        at = lay(up_ref[...], at)
        at = lay(down_ref[...], at)
        for start in range(0, 32, 8):
            rows = pl.ds(start, 8)
            at = lay(norm_a[rows, :] + norm_b[rows, :], at)

    ins = [coef, rate, taps, skip, upbias, downbias, norms, norms_other]
    ins = [(x, "v") for x in ins[:6]] + [(x, "t") for x in ins[6:]]
    out = staged(run, ins, [(shaped((total, chans), f32), "v")], "pack_small")[0]
    return out, counts


def unpack_small(place, bit, mine, other, counts, lags, hidden, width):
    half, chans = mine.shape

    def run(place_ref, a, b, coef, rate, taps, skip, up, down, *rest):
        norms, whole = rest[:-1], rest[-1]
        side = (place_ref[0] >> bit) & 1
        whole[pl.ds(pl.multiple_of(side * half, 8), half), :] = a[...]
        whole[pl.ds(pl.multiple_of((1 - side) * half, 8), half), :] = b[...]
        at = 0
        for out in (coef, rate, taps):
            out[...] = whole[pl.ds(at, out.shape[0]), :]
            at += out.shape[0]
        for out in (skip, up, down, *norms):
            for start in range(0, out.shape[1], chans):
                out[:, pl.ds(start, chans)] = whole[pl.ds(at, 1), :]
                at += 1

    states = counts[0]
    outs = [(shaped((n, chans), f32), "v") for n in (states, states, lags)]
    outs += [(shaped((n,), f32), "v") for n in (chans, hidden, width, width, width, width, width)]
    ins = [(place, "s"), (mine, "v"), (other, "v")]
    return staged(run, ins, outs, "unpack_small", [pltpu.VMEM((2 * half, chans), f32)])


def collect(keeps, gots, layout, sizes):
    n = len(keeps)
    rows = keeps[0].shape[0]
    names = list(sizes)

    def run(*refs):
        outs = dict(zip(names, refs[2 * n :]))
        for i in range(n):
            total = refs[i][...] + refs[n + i][...]
            at = 0
            for name, start, count in layout[i]:
                piece = total[:, at : at + count]
                if sizes[name][1]:
                    outs[name][pl.ds(start, count), :] = piece.T
                else:
                    outs[name][:, pl.ds(start, count)] = piece
                at += count

    outs = []
    for columns, turned in sizes.values():
        outs.append((shaped((columns, rows) if turned else (rows, columns), f32), "v"))
    res = staged(run, [(x, "v") for x in (*keeps, *gots)], outs, "collect")
    return dict(zip(names, res))


def state_grads(coef_t, rate_t, lag_grad):
    states, chans = coef_t.shape
    span = lag_grad.shape[0]
    step = 32
    blocks = span // step
    lanes = 128
    group = 8
    tiles = step // 8

    def run(coef_ref, rate_ref, lag_ref, coef_out, rate_out, fine, coarse, plain, place, ramp):
        rate = rate_ref[...][:, None, :]
        within = lax.broadcasted_iota(jnp.int32, (1, step, 1), 1).astype(f32)
        across = lax.broadcasted_iota(jnp.int32, (1, blocks, 1), 1).astype(f32)
        fine[...] = jnp.exp(-rate * within)
        coarse[...] = jnp.exp(-rate * (step * across))
        plain[...] = jnp.zeros_like(plain)
        place[...] = jnp.zeros_like(place)
        ramp[...] = jnp.zeros_like(ramp)
        for base in range(0, blocks, group):
            lag = [
                [
                    lag_ref[pl.ds((base + j) * step + 8 * a, 8), :]
                    for a in range(tiles)
                ]
                for j in range(group)
            ]

            def add(n, _):
                near = [fine[n, pl.ds(8 * a, 8), :] for a in range(tiles)]
                suffix = None
                later = None
                tilted = None
                for j in reversed(range(group)):
                    far = coarse[n, pl.ds(base + j, 1), :]
                    total = None
                    slope = None
                    for a in reversed(range(tiles)):
                        term = lag[j][a] * near[a]
                        if total is None:
                            total = term
                        else:
                            slope = total if slope is None else slope + total
                            total = total + term
                    weighted = far * total
                    bent = far * slope
                    tilted = bent if tilted is None else tilted + bent
                    if suffix is None:
                        suffix = weighted
                    else:
                        later = suffix if later is None else later + suffix
                        suffix = suffix + weighted
                plain[n] = plain[n] + suffix
                place[n] = place[n] + (later + float(base) * suffix)
                ramp[n] = ramp[n] + tilted
                return 0

            lax.fori_loop(0, states, add, 0, unroll=4)
        rows = lax.broadcasted_iota(jnp.int32, (1, 8, 1), 1).astype(f32)
        whole = plain[...]
        coef_out[...] = jnp.sum(whole, 1)
        times = float(step) * place[...] + 8.0 * ramp[...] + rows * whole
        rate_out[...] = -coef_ref[...] * jnp.sum(times, 1)

    shape = jax.ShapeDtypeStruct((states, chans), f32)
    block = pl.BlockSpec((states, lanes), lambda i: (0, i))
    return pl.pallas_call(
        run,
        grid=(chans // lanes,),
        in_specs=[block, block, pl.BlockSpec((span, lanes), lambda i: (0, i))],
        out_specs=[block, block],
        out_shape=[shape, shape],
        scratch_shapes=[
            pltpu.VMEM((states, step, lanes), f32),
            pltpu.VMEM((states, blocks, lanes), f32),
        ]
        + [pltpu.VMEM((states, 8, lanes), f32)] * 3,
        compiler_params=pltpu.CompilerParams(vmem_limit_bytes=most_vmem),
        cost_estimate=small_cost,
        name="state_grads",
    )(coef_t, rate_t, lag_grad)


def follow(values, *before):
    held = lax.optimization_barrier((list(values), before))[0]
    return held


def take_columns(cols, start, count):
    taken = []
    for name, first, columns in cols:
        low, high = max(start, 0), min(start + count, columns)
        if low < high:
            taken.append((name, first + low, high - low))
        start -= columns
    return taken


def body(
    tokens,
    lengths,
    mixgain,
    mixbias,
    query_weight,
    key_weight,
    value_weight,
    shift_taps,
    state_coef,
    state_rate,
    state_skip,
    out_weight,
    feedgain,
    feedbias,
    up_weight,
    up_bias,
    down_weight,
    down_bias,
    cotangent,
):
    assert lengths.shape[0] == 1
    span, width = tokens.shape
    chans = query_weight.shape[1]
    hidden = up_weight.shape[1]
    lags = shift_taps.shape[0]
    places = lax.axis_size("freq")
    halving = places == 16 and width % (16 * places) == 0
    groups = places if halving else 2
    rows = width // groups
    place = lax.axis_index("freq").astype(jnp.int32).reshape(1)
    third, part = hidden // 3, chans // 3
    feed_cols = [[("down", i * third, third), ("up", i * third, third)] for i in range(3)]
    mixer_cols = [
        [("out", 0, 3 * part), ("query", 0, part)],
        [("query", part, 2 * part), ("key", 0, 2 * part)],
        [("key", 2 * part, part), ("value", 0, 3 * part)],
    ]
    order_of = {"out": 0, "query": 1, "key": 2, "value": 3}
    pieces = [[(order_of[n], s, c) for n, s, c in cols] for cols in mixer_cols]
    thirds = [((i, 0), (i, third)) for i in range(3)]
    if halving:
        orders = [[(0, 1, 2, 3), (0, 1, 3, 2)], [(1, 2, 0, 3), (1, 3, 0, 2)], [(2, 0, 1, 3)]]
        bits = [order[0][0] for order in orders]
    else:
        place = jnp.zeros_like(place)
        bits = [0] * 3

    block = 256
    table_np = dft_table(block)
    table, table_t = jnp.asarray(table_np), jnp.asarray(np.ascontiguousarray(table_np.T))
    coef_t, rate_t = state_coef.T, state_rate.T

    normed, query, keypad, value, mixed, gated, sig16, ker16, out_part = mixer_forward(
        lengths,
        tokens,
        mixgain,
        mixbias,
        (query_weight, key_weight, value_weight),
        shift_taps,
        coef_t,
        rate_t,
        state_skip,
        out_weight,
        table,
        table_t,
    )
    out_other = swap(out_part, "tp", 0)
    down, down_t, normed_t, downbias_part = feed_prepare(lengths, cotangent, normed)
    down_t = down_t.reshape(groups, rows, span)
    normed_t = normed_t.reshape(groups, rows, span)
    (resid, acts, second_part, feed_sums, upbias_part), gives, keeps = feed_forward_back(
        place, out_part, out_other, feedgain, feedbias, down, down_t, up_weight, up_bias, down_weight, (bits, [2 * third] * 3, thirds)
    )
    second_other = swap(second_part, "tp", 0)
    if halving:
        gots = [swap(give, "freq", bit) for give, bit in zip(gives, bits)]
    (grad_resid, lag_grad, normed_part, skip_part, taps_part), more_gives, more_keeps = mixer_back(
        lengths, place, down, second_part, second_other, resid, feedgain, out_weight, mixed, query, sig16, ker16, table, table_t, state_skip,
        keypad, value, shift_taps, normed_t, gated, (query_weight, key_weight, value_weight), tokens, feed_sums, (bits, pieces)
    )
    (acts,) = follow([acts], normed_part)
    down_part = feed_down(acts, down_weight)
    if halving:

        items = []
        for source, all_cols in enumerate((feed_cols, mixer_cols)):
            for cols, some in zip(all_cols, orders):
                size = sum(count for _, _, count in cols) // len(some)
                for k, order in enumerate(some):
                    items.append((order, take_columns(cols, k * size, size), source))

        def arrange(step, source=None):
            arrays, starts = {}, {}
            for item in items:
                if source is None or item[2] == source:
                    arrays.setdefault(item[0][step], []).append(item)
            for some in arrays.values():
                at = 0
                for item in some:
                    starts[id(item)] = at
                    at += width_of(item)
            links = sorted(arrays)
            return links, [sum(map(width_of, arrays[link])) for link in links], arrays, starts

        def width_of(item):
            return sum(count for _, _, count in item[1])

        def cuts_to(step, source=None):
            links, _, _, starts = arrange(step - 1, source)
            next_links, widths, _, next_starts = arrange(step)
            cuts = []
            for item in items:
                if source is None or item[2] == source:
                    order = item[0]
                    pos = sorted(order[step:]).index(order[step])
                    cuts.append(
                        (
                            links.index(order[step - 1]),
                            starts[id(item)],
                            width_of(item),
                            pos,
                            order[step],
                            next_links.index(order[step]),
                            next_starts[id(item)],
                        )
                    )
            return cuts, rows, widths

        def exchange(gives, step):
            return [swap(give, "freq", link) for give, link in zip(gives, arrange(step)[0])]

        def add_swapped(value, bit):
            return value + swap(value, "freq", bit)

        gots = follow(gots, down_part)
        more_gives, lag_grad, normed_part, down_part = follow(
            [more_gives, lag_grad, normed_part, down_part], *gots
        )
        more_gots = exchange(more_gives, 0)
        held_gives = halve(place, keeps, gots, *cuts_to(1, 0), True)
        held_keeps = halve(place, keeps, gots, *cuts_to(1, 0), False)
    normed_other = swap(normed_part, "tp", 0)
    down_other = swap(down_part, "tp", 0)
    if halving:
        more_gots = follow(more_gots, normed_other, down_other, held_gives[0], held_keeps[0])
        gives = halve(place, more_keeps, more_gots, *cuts_to(1, 1), True, held_gives)
        gots = exchange(gives, 1)
        (lag_grad,) = follow([lag_grad], *gives)
    coef_part, rate_part = state_grads(coef_t, rate_t, lag_grad)
    small, counts = pack_small(
        coef_part, rate_part, taps_part, skip_part, upbias_part, downbias_part, normed_part, normed_other
    )
    if halving:
        half = small.shape[0] // 2
        side = place[0] & 1
        give = lax.dynamic_slice_in_dim(small, (1 - side) * half, half, 0)
        small = lax.dynamic_slice_in_dim(small, side * half, half, 0)
        other = swap(give, "freq", 0)
        (more_gots[0],) = follow([more_gots[0]], give)
        keeps = halve(place, more_keeps, more_gots, *cuts_to(1, 1), False, held_keeps)
        (other,) = follow([other], *keeps)
        old = follow(gots, other, small)
        gives = halve(place, keeps, old, *cuts_to(2), True)
        (small,) = follow([small], *gives)
        gots = exchange(gives, 2)
        small = small + other
        other = swap(small, "freq", 2)
        (down_part,) = follow([down_part], small)
        layer_out = finish_layer(lengths, resid, down_part, down_other, down_bias)
        (other,) = follow([other], layer_out)
        small = small + other
        other = swap(small, "freq", 3)
        (old[0],) = follow([old[0]], small)
        keeps = halve(place, keeps, old, *cuts_to(2), False)
        (other,) = follow([other], *keeps)
        small = small + other
        old = follow(gots, small, *keeps)
        gives = halve(place, keeps, old, *cuts_to(3), True)
        (small,) = follow([small], *gives)
        gots = exchange(gives, 3)
        other = swap(small, "freq", 1)
        (old[0],) = follow([old[0]], *gives)
        keeps = halve(place, keeps, old, *cuts_to(3), False)
        (other,) = follow([other], *keeps)
        small = small + other
        other = swap(small, "freq", 0)
        (normed_part,) = follow([normed_part], small)
        tokens_grad = finish_tokens(tokens, grad_resid, normed_part, normed_other, mixgain)
        (other,) = follow([other], tokens_grad)
        coef_sum, rate_sum, taps_sum, skip_sum, upbias_sum, downbias_sum, *norms = unpack_small(
            place, 0, small, other, counts, lags, hidden, width
        )
        gots = follow(gots, coef_sum)
        sizes = {"down": (hidden, False), "up": (hidden, False), "out": (chans, False)}
        sizes |= {name: (chans, False) for name in ("query", "key", "value")}
        links, _, arrays, _ = arrange(3)
        grads = collect(keeps, gots, [sum((item[1] for item in arrays[link]), []) for link in links], sizes)
    else:
        tokens_grad = finish_tokens(tokens, grad_resid, normed_part, normed_other, mixgain)
        layer_out = finish_layer(lengths, resid, down_part, down_other, down_bias)
        small = lax.psum(small, "freq")
        grads = {name: [] for name in ("down", "up", "out", "query", "key", "value")}
        for i in range(3):
            whole = jnp.concatenate(
                [
                    jnp.concatenate([keeps[i], more_keeps[i]], 1),
                    jnp.concatenate([gives[i], more_gives[i]], 1),
                ],
                0,
            )
            total = lax.psum_scatter(whole, "freq", scatter_dimension=0, tiled=True)
            at = 0
            for name, _, columns in feed_cols[i] + mixer_cols[i]:
                grads[name].append(total[:, at : at + columns])
                at += columns
        grads = {name: jnp.concatenate(some, 1) for name, some in grads.items()}
        cuts = np.cumsum(counts)
        coef_sum, rate_sum, taps_sum, skip_sum, upbias_sum, downbias_sum, norms, _ = jnp.split(small, cuts)
        norms = norms.reshape(4, width)
        skip_sum, upbias_sum, downbias_sum = [x.reshape(-1) for x in (skip_sum, upbias_sum, downbias_sum)]
    return (
        layer_out,
        tokens_grad,
        norms[0],
        norms[1],
        grads["query"],
        grads["key"],
        grads["value"],
        taps_sum,
        coef_sum.T,
        rate_sum.T,
        skip_sum,
        grads["out"].T,
        norms[2],
        norms[3],
        grads["up"],
        upbias_sum,
        grads["down"].T,
        downbias_sum,
    )


def solution(mesh):
    in_specs = (
        P("freq", None),
        P("freq"),
        P(),
        P(),
        P(None, "tp"),
        P(None, "tp"),
        P(None, "tp"),
        P(None, "tp"),
        P("tp", None),
        P("tp", None),
        P("tp"),
        P("tp", None),
        P(),
        P(),
        P(None, "tp"),
        P("tp"),
        P("tp", None),
        P(),
        P("freq", None),
    )
    out_specs = (
        P("freq", None),
        P("freq", None),
        P(),
        P(),
        P("freq", "tp"),
        P("freq", "tp"),
        P("freq", "tp"),
        P(None, "tp"),
        P("tp", None),
        P("tp", None),
        P("tp"),
        P("tp", "freq"),
        P(),
        P(),
        P("freq", "tp"),
        P("tp"),
        P("tp", "freq"),
        P(),
    )
    return jax.shard_map(body, mesh=mesh, in_specs=in_specs, out_specs=out_specs, check_vma=False)
```
